32 devices in a mesh: win: 16 (over z, y, x), rcv: 2 (over core).
Axes of the slice: x: 2, y: 2, z: 4, core: 2. Of those that a mesh axis runs over, the one named last changes fastest.
Arguments:
- spectra: bfloat16 [32, 2, 32, 4096], P('win', None, 'rcv'), may hold values from -6 to 6
- source_channel: int32 [8], replicated, may hold values from 0 to 31
Outputs:
- stack: float32 [512, 8, 32], P('win', None, 'rcv')
The draws below stay inside these ranges and needn't reach their ends.
All inputs are finite; a program needn't handle non-finite values.
Results may differ from the reference program's by a relative error of at most 0.0011.
Values may be sent and summed in bfloat16 or wider, within the bound.
No kernel may reach another device: no remote copies, remote signals or barrier semaphores. Data moves between devices by JAX's collectives and lax.ppermute only.
A program may use at most 64 MiB of HBM per device.

```python
import jax
import jax.numpy as jnp
from jax import lax

F = 4096
L = 512
S = 8
ITERS = 5
R = 32
W = 32


def touch_ends(array, key, low, top_value):
    longest = array.shape.index(max(array.shape))
    spots = []
    for shift in (0, 1):
        where = [jax.random.randint(jax.random.fold_in(key, axis), (), 0, length) for axis, length in enumerate(array.shape)]
        where[longest] = (where[longest] + shift) % array.shape[longest]
        spots.append(tuple(where))
    return array.at[spots[0]].set(low).at[spots[1]].set(top_value)


def shard_levels(stream_key, dims, shards, smallest, top_value):
    def one(dim, parts):
        steps = jax.random.uniform(jax.random.fold_in(jax.random.fold_in(stream_key, 6), dim), (parts,), jnp.float32, smallest / len(shards), top_value / len(shards))
        return jnp.repeat(jnp.exp(steps), dims[dim] // parts).reshape((-1,) + (1,) * (len(dims) - dim - 1))

    level = one(*shards[0])
    for cut in shards[1:]:
        level = level * one(*cut)
    return level


def centred(own_key, extent, width, reach, shards=(), kind=jnp.bfloat16):
    entries = jax.random.normal(own_key, extent, jnp.float32) * width
    if len(shards) > 0:
        entries = shard_levels(own_key, extent, shards, -0.22, 0.18) * entries
    return jnp.clip(entries, min=-reach, max=reach).astype(kind)


def setup_inputs(seed: int = 0) -> dict:
    key_list = jax.random.split(jax.random.key(seed), 3)
    return {
        "spectra": centred(key_list[0], (W, 2, R, F), 1.0, 6.0, ((0, 16), (2, 2))),
        "source_channel": touch_ends(jax.random.randint(key_list[1], (S,), 0, R), jax.random.fold_in(key_list[1], 1), 0, R - 1).astype(jnp.int32),
    }


TUKEY = 4.685
EPSILON = 1e-06

def make_basis(bin_count, lag_count):
    freq = jnp.arange(bin_count, dtype=jnp.int32)
    shifts = jnp.arange(lag_count, dtype=jnp.int32) - lag_count // 2
    phase = shifts[:, None] * freq[None, :] % (2 * bin_count)
    angle = phase.astype(jnp.float32) * (2.0 * jnp.pi / (2 * bin_count))
    factor = jnp.where(freq == 0, 1.0, 2.0).astype(jnp.float32) / jnp.sqrt(jnp.float32(8 * bin_count))
    table = jnp.concatenate([jnp.cos(angle) * factor[None, :], -jnp.sin(angle) * factor[None, :]], axis=1)
    return table.astype(jnp.bfloat16)

def bisquare_stack(samples):
    center = lax.optimization_barrier(jnp.mean(samples, axis=0))
    for iteration in range(ITERS):
        deviation = samples - center
        squared = deviation * deviation
        scale_two = lax.optimization_barrier(jnp.mean(squared, axis=0)) + EPSILON
        ratio = squared / (TUKEY * TUKEY * scale_two)
        weight = jnp.where(ratio < 1.0, (1.0 - ratio) * (1.0 - ratio), 0.0)
        center = lax.optimization_barrier(jnp.sum(weight * samples, axis=0)) / lax.optimization_barrier(jnp.sum(weight, axis=0))
    return center

def reference(spectra, source_channel):
    basis = make_basis(F, L)

    def one_window(window):
        picked = window[:, source_channel, :].astype(jnp.float32)
        receivers = window.astype(jnp.float32)
        real_a = picked[0][:, None, :]
        imag_b = picked[1][:, None, :]
        real_p = receivers[0][None, :, :]
        imag_q = receivers[1][None, :, :]
        real_part = (real_a * real_p + imag_b * imag_q).reshape(S * R, F)
        imag_part = (imag_b * real_p - real_a * imag_q).reshape(S * R, F)
        cross = jnp.concatenate([real_part, imag_part], axis=1).astype(jnp.bfloat16)
        return jnp.dot(basis, cross.T, preferred_element_type=jnp.float32)
    corr = lax.map(one_window, spectra)
    return bisquare_stack(corr).reshape(L, S, R)
```

```python
import jax
import jax.numpy as jnp
import numpy as np
from jax import lax
from jax.sharding import PartitionSpec as P

L = 512
ITERS = 5


TUKEY = 4.685
EPSILON = 1e-06


def make_basis(bin_count, lag_count):
    freq = np.arange(bin_count, dtype=np.int64)
    shifts = np.arange(lag_count, dtype=np.int64) - lag_count // 2
    phase = shifts[:, None] * freq[None, :] % (2 * bin_count)
    angle = phase * (2.0 * np.pi / (2 * bin_count))
    factor = np.where(freq == 0, 1.0, 2.0) / np.sqrt(8.0 * bin_count)
    table = np.concatenate([np.cos(angle) * factor[None, :], -np.sin(angle) * factor[None, :]], axis=1)
    return jnp.asarray(table.astype(np.float32).astype(jnp.bfloat16))


def bisquare_stack(samples):
    center = jnp.mean(samples, axis=0)
    for iteration in range(ITERS):
        deviation = samples - center
        squared = deviation * deviation
        scale_two = jnp.mean(squared, axis=0) + EPSILON
        ratio = squared / (TUKEY * TUKEY * scale_two)
        weight = jnp.where(ratio < 1.0, (1.0 - ratio) * (1.0 - ratio), 0.0)
        center = jnp.sum(weight * samples, axis=0) / jnp.sum(weight, axis=0)
    return center


def per_device(spectra, source_channel):
    win_count = spectra.shape[0]
    chan_count = spectra.shape[2]
    bin_count = spectra.shape[3]
    source_count = source_channel.shape[0]
    receivers_parts = lax.axis_size("rcv")
    channels = lax.iota(jnp.int32, chan_count) + lax.axis_index("rcv") * chan_count
    onehot = (source_channel[:, None] == channels[None, :]).astype(jnp.bfloat16)
    own = jnp.einsum("sr,wcrf->wcsf", onehot, spectra, preferred_element_type=jnp.float32).astype(
        jnp.bfloat16
    )
    picked = own
    moving = own
    for step in range(receivers_parts - 1):
        moving = lax.ppermute(
            moving, "rcv", [(i, (i + 1) % receivers_parts) for i in range(receivers_parts)]
        )
        picked = picked + moving
    source_float = picked.astype(jnp.float32)
    receiver_float = spectra.astype(jnp.float32)
    real_a = source_float[:, 0][:, :, None, :]
    imag_b = source_float[:, 1][:, :, None, :]
    real_p = receiver_float[:, 0][:, None, :, :]
    imag_q = receiver_float[:, 1][:, None, :, :]
    pair_count = source_count * chan_count
    real_part = (real_a * real_p + imag_b * imag_q).reshape(win_count, pair_count, bin_count)
    imag_part = (imag_b * real_p - real_a * imag_q).reshape(win_count, pair_count, bin_count)
    cross = jnp.concatenate([real_part, imag_part], axis=2).astype(jnp.bfloat16)
    basis = make_basis(bin_count, L)
    corr = jnp.einsum("lk,wpk->lwp", basis, cross, preferred_element_type=jnp.float32)
    parts = lax.axis_size("win")
    block = L // parts
    corr = corr.astype(jnp.bfloat16).reshape(parts, block, win_count * pair_count)
    regrouped = lax.all_to_all(corr, "win", split_axis=0, concat_axis=0, tiled=True)
    regrouped = regrouped.reshape(parts, block, win_count, pair_count).astype(jnp.float32)
    regrouped = regrouped.transpose(0, 2, 1, 3).reshape(parts * win_count, block, pair_count)
    result = bisquare_stack(regrouped)
    return result.reshape(block, source_count, chan_count)


def solution(mesh):
    return jax.shard_map(
        per_device,
        mesh=mesh,
        in_specs=(P("win", None, "rcv", None), P()),
        out_specs=P("win", None, "rcv"),
        check_vma=False,
    )
```

```python
import functools

import jax
import jax.numpy as jnp
import numpy as np
from jax import lax
from jax.experimental import pallas as pl
from jax.experimental.pallas import tpu as pltpu
from jax.sharding import PartitionSpec as P

L = 512
ITERS = 5


TUKEY = 4.685
EPSILON = 1e-06


def make_basis(bin_count, lag_count):
    freq = np.arange(bin_count, dtype=np.int64)
    shifts = np.arange(lag_count, dtype=np.int64) - lag_count // 2
    phase = shifts[:, None] * freq[None, :] % (2 * bin_count)
    angle = phase * (2.0 * np.pi / (2 * bin_count))
    factor = np.where(freq == 0, 1.0, 2.0) / np.sqrt(8.0 * bin_count)
    table = np.concatenate([np.cos(angle) * factor[None, :], -np.sin(angle) * factor[None, :]], axis=1)
    return jnp.asarray(table.astype(np.float32).astype(jnp.bfloat16))


def stack_kernel(x_ref, out_ref, y_ref, *, win_count):
    parts, block, width = x_ref.shape
    pairs = width // win_count
    count = parts * win_count
    for part in range(parts):
        both = x_ref[part].astype(jnp.float32)
        for w in range(win_count):
            y_ref[part * win_count + w] = both[:, w * pairs : (w + 1) * pairs]
    rows = 8
    centers = []
    for start in range(0, block, rows):
        raw = [y_ref[n, start : start + rows, :] for n in range(count)]
        mean = tree_sum(raw) * (1.0 / count)
        samples = [x - mean for x in raw]
        variance = tree_sum([x * x for x in samples]) * (1.0 / count)
        center = jnp.zeros_like(mean)
        for iteration in range(ITERS):
            scale_two = variance + center * center + EPSILON
            inverse = 1.0 / (TUKEY * TUKEY * scale_two)
            weights, products = [], []
            for x in samples:
                deviation = x - center
                kept = jnp.maximum(1.0 - deviation * deviation * inverse, 0.0)
                weight = kept * kept
                weights.append(weight)
                products.append(weight * x)
            center = tree_sum(products) / tree_sum(weights)
        centers.append(center + mean)
    out_ref[...] = jnp.concatenate(centers, axis=0).T


def tree_sum(terms):
    sums = list(terms[:4])
    for index, term in enumerate(terms[4:]):
        sums[index % 4] = sums[index % 4] + term
    return (sums[0] + sums[1]) + (sums[2] + sums[3])


def stack_blocks(regrouped, win_count, source_count):
    parts, block, width = regrouped.shape
    pairs = width // win_count
    result = pl.pallas_call(
        functools.partial(stack_kernel, win_count=win_count),
        out_shape=jax.ShapeDtypeStruct((pairs, block), jnp.float32),
        in_specs=[pl.BlockSpec(memory_space=pltpu.VMEM)],
        out_specs=pl.BlockSpec(memory_space=pltpu.VMEM),
        scratch_shapes=[pltpu.VMEM((parts * win_count, block, pairs), jnp.float32)],
        compiler_params=pltpu.CompilerParams(vmem_limit_bytes=16 * 2**20),
        name="bisquare_stack",
    )(regrouped)
    return result.reshape(source_count, pairs // source_count, block).transpose(2, 0, 1)


def per_device(spectra, source_channel):
    win_count = spectra.shape[0]
    chan_count = spectra.shape[2]
    bin_count = spectra.shape[3]
    source_count = source_channel.shape[0]
    receivers_parts = lax.axis_size("rcv")
    channels = lax.iota(jnp.int32, chan_count) + lax.axis_index("rcv") * chan_count
    onehot = (source_channel[:, None] == channels[None, :]).astype(jnp.bfloat16)
    own = jnp.einsum("sr,wcrf->wcsf", onehot, spectra, preferred_element_type=jnp.float32).astype(
        jnp.bfloat16
    )
    picked = own
    moving = own
    for step in range(receivers_parts - 1):
        moving = lax.ppermute(
            moving, "rcv", [(i, (i + 1) % receivers_parts) for i in range(receivers_parts)]
        )
        picked = picked + moving
    source_float = picked.astype(jnp.float32)
    receiver_float = spectra.astype(jnp.float32)
    real_a = source_float[:, 0][:, :, None, :]
    imag_b = source_float[:, 1][:, :, None, :]
    real_p = receiver_float[:, 0][:, None, :, :]
    imag_q = receiver_float[:, 1][:, None, :, :]
    pair_count = source_count * chan_count
    real_part = (real_a * real_p + imag_b * imag_q).reshape(win_count, pair_count, bin_count)
    imag_part = (imag_b * real_p - real_a * imag_q).reshape(win_count, pair_count, bin_count)
    cross = jnp.concatenate([real_part, imag_part], axis=2).astype(jnp.bfloat16)
    basis = make_basis(bin_count, L)
    corr = jnp.einsum("lk,wpk->lwp", basis, cross, preferred_element_type=jnp.float32)
    parts = lax.axis_size("win")
    block = L // parts
    corr = corr.astype(jnp.bfloat16).reshape(parts, block, win_count * pair_count)
    regrouped = lax.all_to_all(corr, "win", split_axis=0, concat_axis=0, tiled=True)
    return stack_blocks(regrouped, win_count, source_count)


def solution(mesh):
    return jax.shard_map(
        per_device,
        mesh=mesh,
        in_specs=(P("win", None, "rcv", None), P()),
        out_specs=P("win", None, "rcv"),
        check_vma=False,
    )
```

```python
import functools

import jax
import jax.numpy as jnp
import numpy as np
from jax import lax
from jax.experimental import pallas as pl
from jax.experimental.pallas import tpu as pltpu
from jax.sharding import PartitionSpec as P

L = 512
ITERS = 5


TUKEY = 4.685
EPSILON = 1e-06


def make_tables(bin_count, lag_count, rows):
    freq = np.arange(bin_count, dtype=np.int64)
    shifts = np.arange(lag_count // 2 + 1, dtype=np.int64)
    phase = shifts[:, None] * freq[None, :] % (2 * bin_count)
    angle = phase * (2.0 * np.pi / (2 * bin_count))
    factor = np.where(freq == 0, 1.0, 2.0) / np.sqrt(8.0 * bin_count)
    table = np.zeros((2, rows, bin_count), np.float32)
    table[0, : len(shifts)] = np.cos(angle) * factor
    table[1, : len(shifts)] = -np.sin(angle) * factor
    return jnp.asarray(table.astype(jnp.bfloat16))


def correlate_kernel(*refs, peers, chunk):
    rows_ref, table_ref = refs[:2]
    block_refs = refs[2 : 2 + peers]
    out_ref, even_ref, odd_ref, float_ref = refs[2 + peers :]
    win_count, _, chan_count, bin_count = block_refs[0].shape
    source_count = rows_ref.shape[0]
    half = out_ref.shape[0] // 2
    for start in range(0, bin_count, chunk):
        bins = slice(start, start + chunk)
        for k in range(peers):
            for w in range(win_count):
                for part in range(2):
                    float_ref[w, part, k * chan_count : (k + 1) * chan_count, bins] = block_refs[k][
                        w, part, :, bins
                    ].astype(jnp.float32)
        reals, imags = [], []
        for w in range(win_count):
            real_p = float_ref[w, 0, :chan_count, bins]
            imag_q = float_ref[w, 1, :chan_count, bins]
            for s in range(source_count):
                real_a = float_ref[w, 0, pl.ds(rows_ref[s], 1), bins]
                imag_b = float_ref[w, 1, pl.ds(rows_ref[s], 1), bins]
                reals.append((real_a * real_p + imag_b * imag_q).astype(jnp.bfloat16))
                imags.append((imag_b * real_p - real_a * imag_q).astype(jnp.bfloat16))
        for index, parts, sum_ref in ((0, reals, even_ref), (1, imags, odd_ref)):
            term = lax.dot_general(
                table_ref[index, :, bins],
                jnp.concatenate(parts, axis=0),
                (((1,), (1,)), ((), ())),
                preferred_element_type=jnp.float32,
            )
            if start == 0:
                sum_ref[...] = term
            else:
                sum_ref[...] += term
    out_ref[half:, :] = (even_ref[:half, :] + odd_ref[:half, :]).astype(jnp.bfloat16)
    back = (even_ref[...] - odd_ref[...]).astype(jnp.bfloat16)
    lag = lax.broadcasted_iota(jnp.int32, (half, half), 0)
    shift = lax.broadcasted_iota(jnp.int32, (half, half), 1)
    flip = (lag + shift == half).astype(jnp.bfloat16)
    turned = jnp.dot(flip, back[:half], preferred_element_type=jnp.float32)
    first = jnp.where(
        lax.broadcasted_iota(jnp.int32, turned.shape, 0) == 0,
        back[half : half + 16].astype(jnp.float32)[:1],
        turned,
    )
    out_ref[:half, :] = first.astype(jnp.bfloat16)


def correlate(blocks, source_rows):
    win_count, _, chan_count, bin_count = blocks[0].shape
    source_count = source_rows.shape[0]
    rows = L // 2 + 16
    chunk = min(512, bin_count)
    table = make_tables(bin_count, L, rows)
    width = win_count * source_count * chan_count
    vmem = pl.BlockSpec(memory_space=pltpu.VMEM)
    return pl.pallas_call(
        functools.partial(correlate_kernel, peers=len(blocks), chunk=chunk),
        out_shape=jax.ShapeDtypeStruct((L, width), jnp.bfloat16),
        in_specs=[pl.BlockSpec(memory_space=pltpu.SMEM), vmem] + [vmem] * len(blocks),
        out_specs=vmem,
        scratch_shapes=[
            pltpu.VMEM((rows, width), jnp.float32),
            pltpu.VMEM((rows, width), jnp.float32),
            pltpu.VMEM((win_count, 2, len(blocks) * chan_count, bin_count), jnp.float32),
        ],
        compiler_params=pltpu.CompilerParams(vmem_limit_bytes=40 * 2**20),
        name="correlate",
    )(source_rows, table, *blocks)


def stack_kernel(x_ref, out_ref, y_ref, *, win_count):
    parts, block, width = x_ref.shape
    pairs = width // win_count
    count = parts * win_count
    for part in range(parts):
        both = x_ref[part].astype(jnp.float32)
        for w in range(win_count):
            y_ref[part * win_count + w] = both[:, w * pairs : (w + 1) * pairs]
    rows = 8
    centers = []
    for start in range(0, block, rows):
        raw = [y_ref[n, start : start + rows, :] for n in range(count)]
        mean = tree_sum(raw) * (1.0 / count)
        samples = [x - mean for x in raw]
        variance = tree_sum([x * x for x in samples]) * (1.0 / count)
        center = jnp.zeros_like(mean)
        for iteration in range(ITERS):
            scale_two = variance + center * center + EPSILON
            inverse = 1.0 / (TUKEY * TUKEY * scale_two)
            weights, products = [], []
            for x in samples:
                deviation = x - center
                kept = jnp.maximum(1.0 - deviation * deviation * inverse, 0.0)
                weight = kept * kept
                weights.append(weight)
                products.append(weight * x)
            center = tree_sum(products) / tree_sum(weights)
        centers.append(center + mean)
    out_ref[...] = jnp.concatenate(centers, axis=0).T


def tree_sum(terms):
    sums = list(terms[:4])
    for index, term in enumerate(terms[4:]):
        sums[index % 4] = sums[index % 4] + term
    return (sums[0] + sums[1]) + (sums[2] + sums[3])


def stack_blocks(regrouped, win_count, source_count):
    parts, block, width = regrouped.shape
    pairs = width // win_count
    result = pl.pallas_call(
        functools.partial(stack_kernel, win_count=win_count),
        out_shape=jax.ShapeDtypeStruct((pairs, block), jnp.float32),
        in_specs=[pl.BlockSpec(memory_space=pltpu.VMEM)],
        out_specs=pl.BlockSpec(memory_space=pltpu.VMEM),
        scratch_shapes=[pltpu.VMEM((parts * win_count, block, pairs), jnp.float32)],
        compiler_params=pltpu.CompilerParams(vmem_limit_bytes=16 * 2**20),
        name="bisquare_stack",
    )(regrouped)
    return result.reshape(source_count, pairs // source_count, block).transpose(2, 0, 1)


def per_device(spectra, source_channel):
    win_count = spectra.shape[0]
    chan_count = spectra.shape[2]
    source_count = source_channel.shape[0]
    peers = lax.axis_size("rcv")
    me = lax.axis_index("rcv")
    blocks = [spectra]
    for step in range(1, peers):
        blocks.append(lax.ppermute(spectra, "rcv", [(i, (i + step) % peers) for i in range(peers)]))
    back = (me - source_channel // chan_count + peers) % peers
    source_rows = back * chan_count + source_channel % chan_count
    corr = correlate(blocks, source_rows)
    parts = lax.axis_size("win")
    corr = corr.reshape(parts, L // parts, corr.shape[1])
    regrouped = lax.all_to_all(corr, "win", split_axis=0, concat_axis=0, tiled=True)
    return stack_blocks(regrouped, win_count, source_count)


def solution(mesh):
    return jax.shard_map(
        per_device,
        mesh=mesh,
        in_specs=(P("win", None, "rcv", None), P()),
        out_specs=P("win", None, "rcv"),
        check_vma=False,
    )
```

```python
import functools

import jax
import jax.numpy as jnp
import numpy as np
from jax import lax
from jax.experimental import pallas as pl
from jax.experimental.pallas import tpu as pltpu
from jax.sharding import PartitionSpec as P

L = 512
ITERS = 5


TUKEY = 4.685
EPSILON = 1e-06


def make_tables(bin_count, lag_count, rows):
    freq = np.arange(bin_count, dtype=np.int64)
    shifts = np.arange(lag_count // 2 + 1, dtype=np.int64)
    phase = shifts[:, None] * freq[None, :] % (2 * bin_count)
    angle = phase * (2.0 * np.pi / (2 * bin_count))
    factor = np.where(freq == 0, 1.0, 2.0) / np.sqrt(8.0 * bin_count)
    table = np.zeros((2, rows, bin_count), np.float32)
    table[0, : len(shifts)] = np.cos(angle) * factor
    table[1, : len(shifts)] = -np.sin(angle) * factor
    return jnp.asarray(table.astype(jnp.bfloat16))


def correlate_kernel(*refs, peers, chunk):
    rows_ref, table_ref = refs[:2]
    block_refs = refs[2 : 2 + peers]
    out_ref, even_ref, odd_ref, float_ref = refs[2 + peers :]
    win_count, _, chan_count, bin_count = block_refs[0].shape
    source_count = rows_ref.shape[0]
    half = out_ref.shape[0] // 2
    own_ref = block_refs[0]
    for start in range(0, bin_count, chunk):
        bins = slice(start, start + chunk)
        for k in range(peers):
            for w in range(win_count):
                for part in range(2):
                    float_ref[w, part, k * chan_count : (k + 1) * chan_count, bins] = block_refs[k][
                        w, part, :, bins
                    ].astype(jnp.float32)
        reals, imags = [], []
        for w in range(win_count):
            real_p = own_ref[w, 0, :, bins]
            imag_q = own_ref[w, 1, :, bins]
            for s in range(source_count):
                real_a = float_ref[w, 0, pl.ds(rows_ref[s], 1), bins]
                imag_b = float_ref[w, 1, pl.ds(rows_ref[s], 1), bins]
                reals.append((real_a * real_p + imag_b * imag_q).astype(jnp.bfloat16))
                imags.append((imag_b * real_p - real_a * imag_q).astype(jnp.bfloat16))
        for index, parts, sum_ref in ((0, reals, even_ref), (1, imags, odd_ref)):
            term = lax.dot_general(
                table_ref[index, :, bins],
                jnp.concatenate(parts, axis=0),
                (((1,), (1,)), ((), ())),
                preferred_element_type=jnp.float32,
            )
            if start == 0:
                sum_ref[...] = term
            else:
                sum_ref[...] += term
    out_ref[half:, :] = (even_ref[:half, :] + odd_ref[:half, :]).astype(jnp.bfloat16)
    back = (even_ref[...] - odd_ref[...]).astype(jnp.bfloat16)
    lag = lax.broadcasted_iota(jnp.int32, (half, half), 0)
    shift = lax.broadcasted_iota(jnp.int32, (half, half), 1)
    flip = (lag + shift == half).astype(jnp.bfloat16)
    turned = jnp.dot(flip, back[:half], preferred_element_type=jnp.float32)
    first = jnp.where(
        lax.broadcasted_iota(jnp.int32, turned.shape, 0) == 0,
        back[half : half + 16].astype(jnp.float32)[:1],
        turned,
    )
    out_ref[:half, :] = first.astype(jnp.bfloat16)


def correlate(table, blocks, source_rows):
    win_count, _, chan_count, bin_count = blocks[0].shape
    source_count = source_rows.shape[0]
    rows = table.shape[1]
    chunk = min(512, bin_count)
    width = win_count * source_count * chan_count
    vmem = pl.BlockSpec(memory_space=pltpu.VMEM)
    return pl.pallas_call(
        functools.partial(correlate_kernel, peers=len(blocks), chunk=chunk),
        out_shape=jax.ShapeDtypeStruct((L, width), jnp.bfloat16),
        in_specs=[pl.BlockSpec(memory_space=pltpu.SMEM), vmem] + [vmem] * len(blocks),
        out_specs=vmem,
        scratch_shapes=[
            pltpu.VMEM((rows, width), jnp.float32),
            pltpu.VMEM((rows, width), jnp.float32),
            pltpu.VMEM((win_count, 2, len(blocks) * chan_count, bin_count), jnp.float32),
        ],
        compiler_params=pltpu.CompilerParams(vmem_limit_bytes=40 * 2**20),
        name="correlate",
    )(source_rows, table, *blocks)


def widen_kernel(table_ref, own_ref, out_ref):
    for w in range(own_ref.shape[0]):
        for part in range(2):
            out_ref[w, part] = own_ref[w, part].astype(jnp.float32)


def widen(table, own):
    vmem = pl.BlockSpec(memory_space=pltpu.VMEM)
    return pl.pallas_call(
        widen_kernel,
        out_shape=jax.ShapeDtypeStruct(own.shape, jnp.float32),
        in_specs=[vmem, vmem],
        out_specs=vmem,
        compiler_params=pltpu.CompilerParams(vmem_limit_bytes=16 * 2**20),
        cost_estimate=pl.CostEstimate(
            flops=0, bytes_accessed=2 * table.size + 6 * own.size, transcendentals=0
        ),
        name="widen",
    )(table, own)


def stack_kernel(x_ref, out_ref, y_ref, *, win_count):
    parts, block, width = x_ref.shape
    pairs = width // win_count
    count = parts * win_count
    for part in range(parts):
        both = x_ref[part].astype(jnp.float32)
        for w in range(win_count):
            y_ref[part * win_count + w] = both[:, w * pairs : (w + 1) * pairs]
    rows = 8
    centers = []
    for start in range(0, block, rows):
        raw = [y_ref[n, start : start + rows, :] for n in range(count)]
        mean = tree_sum(raw) * (1.0 / count)
        samples = [x - mean for x in raw]
        variance = tree_sum([x * x for x in samples]) * (1.0 / count)
        center = jnp.zeros_like(mean)
        for iteration in range(ITERS):
            scale_two = variance + center * center + EPSILON
            inverse = 1.0 / (TUKEY * TUKEY * scale_two)
            weights, products = [], []
            for x in samples:
                deviation = x - center
                kept = jnp.maximum(1.0 - deviation * deviation * inverse, 0.0)
                weight = kept * kept
                weights.append(weight)
                products.append(weight * x)
            center = tree_sum(products) / tree_sum(weights)
        centers.append(center + mean)
    out_ref[...] = jnp.concatenate(centers, axis=0).T


def tree_sum(terms):
    sums = list(terms[:4])
    for index, term in enumerate(terms[4:]):
        sums[index % 4] = sums[index % 4] + term
    return (sums[0] + sums[1]) + (sums[2] + sums[3])


def stack_blocks(regrouped, win_count, source_count):
    parts, block, width = regrouped.shape
    pairs = width // win_count
    result = pl.pallas_call(
        functools.partial(stack_kernel, win_count=win_count),
        out_shape=jax.ShapeDtypeStruct((pairs, block), jnp.float32),
        in_specs=[pl.BlockSpec(memory_space=pltpu.VMEM)],
        out_specs=pl.BlockSpec(memory_space=pltpu.VMEM),
        scratch_shapes=[pltpu.VMEM((parts * win_count, block, pairs), jnp.float32)],
        compiler_params=pltpu.CompilerParams(vmem_limit_bytes=16 * 2**20),
        name="bisquare_stack",
    )(regrouped)
    return result.reshape(source_count, pairs // source_count, block).transpose(2, 0, 1)


def per_device(spectra, source_channel):
    win_count = spectra.shape[0]
    chan_count = spectra.shape[2]
    source_count = source_channel.shape[0]
    peers = lax.axis_size("rcv")
    me = lax.axis_index("rcv")
    table = make_tables(spectra.shape[3], L, L // 2 + 16)
    own = widen(table, spectra)
    blocks = [own]
    for step in range(1, peers):
        blocks.append(lax.ppermute(spectra, "rcv", [(i, (i + step) % peers) for i in range(peers)]))
    back = (me - source_channel // chan_count + peers) % peers
    source_rows = back * chan_count + source_channel % chan_count
    corr = correlate(table, blocks, source_rows)
    parts = lax.axis_size("win")
    corr = corr.reshape(parts, L // parts, corr.shape[1])
    regrouped = lax.all_to_all(corr, "win", split_axis=0, concat_axis=0, tiled=True)
    return stack_blocks(regrouped, win_count, source_count)


def solution(mesh):
    return jax.shard_map(
        per_device,
        mesh=mesh,
        in_specs=(P("win", None, "rcv", None), P()),
        out_specs=P("win", None, "rcv"),
        check_vma=False,
    )
```

```python
import functools

import jax
import jax.numpy as jnp
import numpy as np
from jax import lax
from jax.experimental import pallas as pl
from jax.experimental.pallas import tpu as pltpu
from jax.sharding import PartitionSpec as P

L = 512
ITERS = 5
VMEM_LIMIT = 24 * 2**20


TUKEY = 4.685
EPSILON = 1e-06


def make_tables(bin_count, lag_count, rows):
    freq = np.arange(bin_count, dtype=np.int64)
    shifts = np.arange(lag_count // 2 + 1, dtype=np.int64)
    phase = shifts[:, None] * freq[None, :] % (2 * bin_count)
    angle = phase * (2.0 * np.pi / (2 * bin_count))
    factor = np.where(freq == 0, 1.0, 2.0) / np.sqrt(8.0 * bin_count)
    table = np.zeros((2, rows, bin_count), np.float32)
    table[0, : len(shifts)] = np.cos(angle) * factor
    table[1, : len(shifts)] = -np.sin(angle) * factor
    return jnp.asarray(table.astype(jnp.bfloat16))


def correlate_kernel(*refs, peers, chunk):
    rows_ref, table_ref = refs[:2]
    block_refs = refs[2 : 2 + peers]
    out_ref, even_ref, odd_ref, float_ref = refs[2 + peers :]
    win_count, _, chan_count, bin_count = block_refs[0].shape
    source_count = rows_ref.shape[0]
    half = out_ref.shape[0] // 2
    own_ref = block_refs[0]
    for start in range(0, bin_count, chunk):
        bins = slice(start, start + chunk)
        for k in range(peers):
            for w in range(win_count):
                for part in range(2):
                    float_ref[w, part, k * chan_count : (k + 1) * chan_count, bins] = block_refs[k][
                        w, part, :, bins
                    ].astype(jnp.float32)
        reals, imags = [], []
        for w in range(win_count):
            real_p = own_ref[w, 0, :, bins]
            imag_q = own_ref[w, 1, :, bins]
            for s in range(source_count):
                real_a = float_ref[w, 0, pl.ds(rows_ref[s], 1), bins]
                imag_b = float_ref[w, 1, pl.ds(rows_ref[s], 1), bins]
                reals.append((real_a * real_p + imag_b * imag_q).astype(jnp.bfloat16))
                imags.append((imag_b * real_p - real_a * imag_q).astype(jnp.bfloat16))
        for index, parts, sum_ref in ((0, reals, even_ref), (1, imags, odd_ref)):
            term = lax.dot_general(
                table_ref[index, :, bins],
                jnp.concatenate(parts, axis=0),
                (((1,), (1,)), ((), ())),
                preferred_element_type=jnp.float32,
            )
            if start == 0:
                sum_ref[...] = term
            else:
                sum_ref[...] += term
    out_ref[half:, :] = (even_ref[:half, :] + odd_ref[:half, :]).astype(jnp.bfloat16)
    back = (even_ref[...] - odd_ref[...]).astype(jnp.bfloat16)
    lag = lax.broadcasted_iota(jnp.int32, (half, half), 0)
    shift = lax.broadcasted_iota(jnp.int32, (half, half), 1)
    flip = (lag + shift == half).astype(jnp.bfloat16)
    turned = jnp.dot(flip, back[:half], preferred_element_type=jnp.float32)
    first = jnp.where(
        lax.broadcasted_iota(jnp.int32, turned.shape, 0) == 0,
        back[half : half + 16].astype(jnp.float32)[:1],
        turned,
    )
    out_ref[:half, :] = first.astype(jnp.bfloat16)


def correlate(table, blocks, source_rows):
    win_count, _, chan_count, bin_count = blocks[0].shape
    source_count = source_rows.shape[0]
    rows = table.shape[1]
    chunk = min(512, bin_count)
    width = win_count * source_count * chan_count
    vmem = pl.BlockSpec(memory_space=pltpu.VMEM)
    return pl.pallas_call(
        functools.partial(correlate_kernel, peers=len(blocks), chunk=chunk),
        out_shape=jax.ShapeDtypeStruct((L, width), jnp.bfloat16),
        in_specs=[pl.BlockSpec(memory_space=pltpu.SMEM), vmem] + [vmem] * len(blocks),
        out_specs=vmem,
        scratch_shapes=[
            pltpu.VMEM((rows, width), jnp.float32),
            pltpu.VMEM((rows, width), jnp.float32),
            pltpu.VMEM((win_count, 2, len(blocks) * chan_count, bin_count), jnp.float32),
        ],
        compiler_params=pltpu.CompilerParams(vmem_limit_bytes=VMEM_LIMIT),
        name="correlate",
    )(source_rows, table, *blocks)


def widen_kernel(table_ref, own_ref, out_ref):
    for w in range(own_ref.shape[0]):
        for part in range(2):
            out_ref[w, part] = own_ref[w, part].astype(jnp.float32)


def widen(table, own):
    vmem = pl.BlockSpec(memory_space=pltpu.VMEM)
    return pl.pallas_call(
        widen_kernel,
        out_shape=jax.ShapeDtypeStruct(own.shape, jnp.float32),
        in_specs=[vmem, vmem],
        out_specs=vmem,
        compiler_params=pltpu.CompilerParams(vmem_limit_bytes=VMEM_LIMIT),
        cost_estimate=pl.CostEstimate(
            flops=0, bytes_accessed=2 * table.size + 6 * own.size, transcendentals=0
        ),
        name="widen",
    )(table, own)


def stack_kernel(x_ref, out_ref, y_ref, *, win_count):
    parts, block, width = x_ref.shape
    pairs = width // win_count
    count = parts * win_count
    for part in range(parts):
        both = x_ref[part].astype(jnp.float32)
        for w in range(win_count):
            y_ref[part * win_count + w] = both[:, w * pairs : (w + 1) * pairs]
    rows = 8
    centers = []
    for start in range(0, block, rows):
        raw = [y_ref[n, start : start + rows, :] for n in range(count)]
        mean = tree_sum(raw) * (1.0 / count)
        samples = [x - mean for x in raw]
        variance = tree_sum([x * x for x in samples]) * (1.0 / count)
        center = jnp.zeros_like(mean)
        for iteration in range(ITERS):
            scale_two = variance + center * center + EPSILON
            inverse = 1.0 / (TUKEY * TUKEY * scale_two)
            weights, products = [], []
            for x in samples:
                deviation = x - center
                kept = jnp.maximum(1.0 - deviation * deviation * inverse, 0.0)
                weight = kept * kept
                weights.append(weight)
                products.append(weight * x)
            center = tree_sum(products) / tree_sum(weights)
        centers.append(center + mean)
    out_ref[...] = jnp.concatenate(centers, axis=0).T


def tree_sum(terms):
    sums = list(terms[:4])
    for index, term in enumerate(terms[4:]):
        sums[index % 4] = sums[index % 4] + term
    return (sums[0] + sums[1]) + (sums[2] + sums[3])


def stack_blocks(regrouped, win_count, source_count):
    parts, block, width = regrouped.shape
    pairs = width // win_count
    result = pl.pallas_call(
        functools.partial(stack_kernel, win_count=win_count),
        out_shape=jax.ShapeDtypeStruct((pairs, block), jnp.float32),
        in_specs=[pl.BlockSpec(memory_space=pltpu.VMEM)],
        out_specs=pl.BlockSpec(memory_space=pltpu.VMEM),
        scratch_shapes=[pltpu.VMEM((parts * win_count, block, pairs), jnp.float32)],
        compiler_params=pltpu.CompilerParams(vmem_limit_bytes=VMEM_LIMIT),
        name="bisquare_stack",
    )(regrouped)
    return result.reshape(source_count, pairs // source_count, block).transpose(2, 0, 1)


def per_device(spectra, source_channel):
    win_count = spectra.shape[0]
    chan_count = spectra.shape[2]
    source_count = source_channel.shape[0]
    peers = lax.axis_size("rcv")
    me = lax.axis_index("rcv")
    table = make_tables(spectra.shape[3], L, L // 2 + 16)
    own = widen(table, spectra)
    blocks = [own]
    for step in range(1, peers):
        blocks.append(lax.ppermute(spectra, "rcv", [(i, (i + step) % peers) for i in range(peers)]))
    back = (me - source_channel // chan_count + peers) % peers
    source_rows = back * chan_count + source_channel % chan_count
    corr = correlate(table, blocks, source_rows)
    parts = lax.axis_size("win")
    corr = corr.reshape(parts, L // parts, corr.shape[1])
    regrouped = lax.all_to_all(corr, "win", split_axis=0, concat_axis=0, tiled=True)
    return stack_blocks(regrouped, win_count, source_count)


def solution(mesh):
    return jax.shard_map(
        per_device,
        mesh=mesh,
        in_specs=(P("win", None, "rcv", None), P()),
        out_specs=P("win", None, "rcv"),
        check_vma=False,
    )
```

```python
import functools

import jax
import jax.numpy as jnp
import numpy as np
from jax import lax
from jax.experimental import pallas as pl
from jax.experimental.pallas import tpu as pltpu
from jax.sharding import PartitionSpec as P

L = 512
ITERS = 5
VMEM_LIMIT = 24 * 2**20


TUKEY = 4.685
EPSILON = 1e-06


def make_tables(bin_count, lag_count, rows):
    freq = np.arange(bin_count, dtype=np.int64)
    shifts = np.arange(lag_count // 2 + 1, dtype=np.int64)
    phase = shifts[:, None] * freq[None, :] % (2 * bin_count)
    angle = phase * (2.0 * np.pi / (2 * bin_count))
    factor = np.where(freq == 0, 1.0, 2.0) / np.sqrt(8.0 * bin_count)
    table = np.zeros((2, rows, bin_count), np.float32)
    table[0, : len(shifts)] = np.cos(angle) * factor
    table[1, : len(shifts)] = -np.sin(angle) * factor
    return jnp.asarray(table.astype(jnp.bfloat16))


def correlate_kernel(*refs, peers, chunk):
    rows_ref, table_ref = refs[:2]
    block_refs = refs[2 : 2 + peers]
    out_refs = refs[2 + peers : -4]
    lags_ref, even_ref, odd_ref, float_ref = refs[-4:]
    win_count, _, chan_count, bin_count = block_refs[0].shape
    source_count = rows_ref.shape[0] - 1
    parts = len(out_refs)
    block = lags_ref.shape[1]
    half = L // 2
    own_ref = block_refs[0]
    for start in range(0, bin_count, chunk):
        bins = slice(start, start + chunk)
        for k in range(peers):
            for w in range(win_count):
                for part in range(2):
                    float_ref[w, part, k * chan_count : (k + 1) * chan_count, bins] = block_refs[k][
                        w, part, :, bins
                    ].astype(jnp.float32)
        reals, imags = [], []
        for w in range(win_count):
            real_p = own_ref[w, 0, :, bins]
            imag_q = own_ref[w, 1, :, bins]
            for s in range(source_count):
                real_a = float_ref[w, 0, pl.ds(rows_ref[s], 1), bins]
                imag_b = float_ref[w, 1, pl.ds(rows_ref[s], 1), bins]
                reals.append((real_a * real_p + imag_b * imag_q).astype(jnp.bfloat16))
                imags.append((imag_b * real_p - real_a * imag_q).astype(jnp.bfloat16))
        for index, terms, sum_ref in ((0, reals, even_ref), (1, imags, odd_ref)):
            term = lax.dot_general(
                table_ref[index, :, bins],
                jnp.concatenate(terms, axis=0),
                (((1,), (1,)), ((), ())),
                preferred_element_type=jnp.float32,
            )
            if start == 0:
                sum_ref[...] = term
            else:
                sum_ref[...] += term
    ahead = even_ref[:half, :] + odd_ref[:half, :]
    lags_ref[parts // 2 :] = ahead.reshape(parts // 2, block, ahead.shape[1])
    back = (even_ref[...] - odd_ref[...]).astype(jnp.bfloat16)
    lag = lax.broadcasted_iota(jnp.int32, (half, half), 0)
    shift = lax.broadcasted_iota(jnp.int32, (half, half), 1)
    flip = (lag + shift == half).astype(jnp.bfloat16)
    turned = jnp.dot(flip, back[:half], preferred_element_type=jnp.float32)
    first = jnp.where(
        lax.broadcasted_iota(jnp.int32, turned.shape, 0) == 0,
        back[half : half + 16].astype(jnp.float32)[:1],
        turned,
    )
    lags_ref[: parts // 2] = first.reshape(parts // 2, block, first.shape[1])
    for step in range(parts):
        out_refs[step][...] = lags_ref[partner(rows_ref[source_count], step, parts)].astype(jnp.bfloat16)


def partner(index, step, parts):
    if parts & (parts - 1) == 0:
        return index ^ step
    return (index + step) % parts


def correlate(table, blocks, source_rows, me, parts):
    win_count, _, chan_count, bin_count = blocks[0].shape
    source_count = source_rows.shape[0]
    places = jnp.concatenate([source_rows, me[None]])
    rows = table.shape[1]
    chunk = min(512, bin_count)
    width = win_count * source_count * chan_count
    vmem = pl.BlockSpec(memory_space=pltpu.VMEM)
    return pl.pallas_call(
        functools.partial(correlate_kernel, peers=len(blocks), chunk=chunk),
        out_shape=[jax.ShapeDtypeStruct((L // parts, width), jnp.bfloat16)] * parts,
        in_specs=[pl.BlockSpec(memory_space=pltpu.SMEM), vmem] + [vmem] * len(blocks),
        out_specs=[vmem] * parts,
        scratch_shapes=[
            pltpu.VMEM((parts, L // parts, width), jnp.float32),
            pltpu.VMEM((rows, width), jnp.float32),
            pltpu.VMEM((rows, width), jnp.float32),
            pltpu.VMEM((win_count, 2, len(blocks) * chan_count, bin_count), jnp.float32),
        ],
        compiler_params=pltpu.CompilerParams(vmem_limit_bytes=VMEM_LIMIT),
        name="correlate",
    )(places, table, *blocks)


def widen_kernel(table_ref, own_ref, out_ref):
    for w in range(own_ref.shape[0]):
        for part in range(2):
            out_ref[w, part] = own_ref[w, part].astype(jnp.float32)


def widen(table, own):
    vmem = pl.BlockSpec(memory_space=pltpu.VMEM)
    return pl.pallas_call(
        widen_kernel,
        out_shape=jax.ShapeDtypeStruct(own.shape, jnp.float32),
        in_specs=[vmem, vmem],
        out_specs=vmem,
        compiler_params=pltpu.CompilerParams(vmem_limit_bytes=VMEM_LIMIT),
        cost_estimate=pl.CostEstimate(
            flops=0, bytes_accessed=2 * table.size + 6 * own.size, transcendentals=0
        ),
        name="widen",
    )(table, own)


def stack_kernel(*refs, win_count):
    part_refs, out_ref, y_ref = refs[:-2], refs[-2], refs[-1]
    parts = len(part_refs)
    block, width = part_refs[0].shape
    pairs = width // win_count
    count = parts * win_count
    for part in range(parts):
        both = part_refs[part][...].astype(jnp.float32)
        for w in range(win_count):
            y_ref[part * win_count + w] = both[:, w * pairs : (w + 1) * pairs]
    rows = 8
    centers = []
    for start in range(0, block, rows):
        raw = [y_ref[n, start : start + rows, :] for n in range(count)]
        mean = tree_sum(raw) * (1.0 / count)
        samples = [x - mean for x in raw]
        variance = tree_sum([x * x for x in samples]) * (1.0 / count)
        center = jnp.zeros_like(mean)
        for iteration in range(ITERS):
            scale_two = variance + center * center + EPSILON
            inverse = 1.0 / (TUKEY * TUKEY * scale_two)
            weights, products = [], []
            for x in samples:
                deviation = x - center
                kept = jnp.maximum(1.0 - deviation * deviation * inverse, 0.0)
                weight = kept * kept
                weights.append(weight)
                products.append(weight * x)
            center = tree_sum(products) / tree_sum(weights)
        centers.append(center + mean)
    out_ref[...] = jnp.concatenate(centers, axis=0).T


def tree_sum(terms):
    sums = list(terms[:4])
    for index, term in enumerate(terms[4:]):
        sums[index % 4] = sums[index % 4] + term
    return (sums[0] + sums[1]) + (sums[2] + sums[3])


def stack_blocks(received, win_count, source_count):
    parts = len(received)
    block, width = received[0].shape
    pairs = width // win_count
    result = pl.pallas_call(
        functools.partial(stack_kernel, win_count=win_count),
        out_shape=jax.ShapeDtypeStruct((pairs, block), jnp.float32),
        in_specs=[pl.BlockSpec(memory_space=pltpu.VMEM)] * parts,
        out_specs=pl.BlockSpec(memory_space=pltpu.VMEM),
        scratch_shapes=[pltpu.VMEM((parts * win_count, block, pairs), jnp.float32)],
        compiler_params=pltpu.CompilerParams(vmem_limit_bytes=VMEM_LIMIT),
        name="bisquare_stack",
    )(*received)
    return result.reshape(source_count, pairs // source_count, block).transpose(2, 0, 1)


def per_device(spectra, source_channel):
    win_count = spectra.shape[0]
    chan_count = spectra.shape[2]
    source_count = source_channel.shape[0]
    peers = lax.axis_size("rcv")
    me = lax.axis_index("rcv")
    table = make_tables(spectra.shape[3], L, L // 2 + 16)
    own = widen(table, spectra)
    blocks = [own]
    for step in range(1, peers):
        blocks.append(lax.ppermute(spectra, "rcv", [(i, (i + step) % peers) for i in range(peers)]))
    back = (me - source_channel // chan_count + peers) % peers
    source_rows = back * chan_count + source_channel % chan_count
    parts = lax.axis_size("win")
    sent = correlate(table, blocks, source_rows, lax.axis_index("win"), parts)
    received = [sent[0]]
    for step in range(parts - 1, 0, -1):
        pairs = [(i, partner(i, step, parts)) for i in range(parts)]
        received.append(lax.ppermute(sent[step], "win", pairs))
    return stack_blocks(received, win_count, source_count)


def solution(mesh):
    return jax.shard_map(
        per_device,
        mesh=mesh,
        in_specs=(P("win", None, "rcv", None), P()),
        out_specs=P("win", None, "rcv"),
        check_vma=False,
    )
```

```python
import functools

import jax
import jax.numpy as jnp
import numpy as np
from jax import lax
from jax.experimental import pallas as pl
from jax.experimental.pallas import tpu as pltpu
from jax.sharding import PartitionSpec as P

L = 512
ITERS = 5
VMEM_LIMIT = 24 * 2**20


TUKEY = 4.685
EPSILON = 1e-06


def make_tables(bin_count, lag_count, rows):
    freq = np.arange(bin_count, dtype=np.int64)
    shifts = np.arange(lag_count // 2 + 1, dtype=np.int64)
    phase = shifts[:, None] * freq[None, :] % (2 * bin_count)
    angle = phase * (2.0 * np.pi / (2 * bin_count))
    factor = np.where(freq == 0, 1.0, 2.0) / np.sqrt(8.0 * bin_count)
    table = np.zeros((2, rows, bin_count), np.float32)
    table[0, : len(shifts)] = np.cos(angle) * factor
    table[1, : len(shifts)] = -np.sin(angle) * factor
    return jnp.asarray(table.astype(jnp.bfloat16))


def correlate_kernel(*refs, peers, chunk):
    rows_ref, table_ref = refs[:2]
    block_refs = refs[2 : 2 + peers]
    out_ref, even_ref, odd_ref, float_ref = refs[2 + peers :]
    win_count, _, chan_count, bin_count = block_refs[0].shape
    source_count = rows_ref.shape[0]
    half = out_ref.shape[0] // 2
    for start in range(0, bin_count, chunk):
        bins = slice(start, start + chunk)
        for k in range(peers):
            for w in range(win_count):
                for part in range(2):
                    float_ref[w, part, k * chan_count : (k + 1) * chan_count, bins] = block_refs[k][
                        w, part, :, bins
                    ].astype(jnp.float32)
        reals, imags = [], []
        for w in range(win_count):
            real_p = float_ref[w, 0, :chan_count, bins]
            imag_q = float_ref[w, 1, :chan_count, bins]
            for s in range(source_count):
                real_a = float_ref[w, 0, pl.ds(rows_ref[s], 1), bins]
                imag_b = float_ref[w, 1, pl.ds(rows_ref[s], 1), bins]
                reals.append((real_a * real_p + imag_b * imag_q).astype(jnp.bfloat16))
                imags.append((imag_b * real_p - real_a * imag_q).astype(jnp.bfloat16))
        for index, parts, sum_ref in ((0, reals, even_ref), (1, imags, odd_ref)):
            term = lax.dot_general(
                table_ref[index, :, bins],
                jnp.concatenate(parts, axis=0),
                (((1,), (1,)), ((), ())),
                preferred_element_type=jnp.float32,
            )
            if start == 0:
                sum_ref[...] = term
            else:
                sum_ref[...] += term
    out_ref[half:, :] = (even_ref[:half, :] + odd_ref[:half, :]).astype(jnp.bfloat16)
    back = (even_ref[...] - odd_ref[...]).astype(jnp.bfloat16)
    lag = lax.broadcasted_iota(jnp.int32, (half, half), 0)
    shift = lax.broadcasted_iota(jnp.int32, (half, half), 1)
    flip = (lag + shift == half).astype(jnp.bfloat16)
    turned = jnp.dot(flip, back[:half], preferred_element_type=jnp.float32)
    first = jnp.where(
        lax.broadcasted_iota(jnp.int32, turned.shape, 0) == 0,
        back[half : half + 16].astype(jnp.float32)[:1],
        turned,
    )
    out_ref[:half, :] = first.astype(jnp.bfloat16)


def correlate(table, blocks, source_rows):
    win_count, _, chan_count, bin_count = blocks[0].shape
    source_count = source_rows.shape[0]
    rows = table.shape[1]
    chunk = min(512, bin_count)
    width = win_count * source_count * chan_count
    vmem = pl.BlockSpec(memory_space=pltpu.VMEM)
    return pl.pallas_call(
        functools.partial(correlate_kernel, peers=len(blocks), chunk=chunk),
        out_shape=jax.ShapeDtypeStruct((L, width), jnp.bfloat16),
        in_specs=[pl.BlockSpec(memory_space=pltpu.SMEM), vmem] + [vmem] * len(blocks),
        out_specs=vmem,
        scratch_shapes=[
            pltpu.VMEM((rows, width), jnp.float32),
            pltpu.VMEM((rows, width), jnp.float32),
            pltpu.VMEM((win_count, 2, len(blocks) * chan_count, bin_count), jnp.float32),
        ],
        compiler_params=pltpu.CompilerParams(vmem_limit_bytes=VMEM_LIMIT),
        name="correlate",
    )(source_rows, table, *blocks)


def places_kernel(me_ref, channel_ref, out_ref, *, peers, chan_count):
    for s in range(channel_ref.shape[0]):
        channel = channel_ref[s]
        owner = lax.div(channel, chan_count)
        step = lax.rem(me_ref[0] - owner + peers, peers)
        out_ref[s] = step * chan_count + channel - owner * chan_count


def find_places(source_channel, peers, chan_count, meanwhile):
    me = lax.axis_index("rcv").astype(jnp.int32)
    smem = pl.BlockSpec(memory_space=pltpu.SMEM)
    return pl.pallas_call(
        functools.partial(places_kernel, peers=peers, chan_count=chan_count),
        out_shape=jax.ShapeDtypeStruct(source_channel.shape, jnp.int32),
        in_specs=[smem, smem],
        out_specs=smem,
        compiler_params=pltpu.CompilerParams(vmem_limit_bytes=VMEM_LIMIT),
        cost_estimate=pl.CostEstimate(flops=0, bytes_accessed=meanwhile, transcendentals=0),
        name="places",
    )(me[None], source_channel)


def stack_kernel(x_ref, out_ref, y_ref, *, win_count):
    parts, block, width = x_ref.shape
    pairs = width // win_count
    count = parts * win_count
    for part in range(parts):
        both = x_ref[part].astype(jnp.float32)
        for w in range(win_count):
            y_ref[part * win_count + w] = both[:, w * pairs : (w + 1) * pairs]
    rows = 8
    centers = []
    for start in range(0, block, rows):
        raw = [y_ref[n, start : start + rows, :] for n in range(count)]
        mean = tree_sum(raw) * (1.0 / count)
        samples = [x - mean for x in raw]
        variance = tree_sum([x * x for x in samples]) * (1.0 / count)
        center = jnp.zeros_like(mean)
        for iteration in range(ITERS):
            scale_two = variance + center * center + EPSILON
            inverse = 1.0 / (TUKEY * TUKEY * scale_two)
            weights, products = [], []
            for x in samples:
                deviation = x - center
                kept = jnp.maximum(1.0 - deviation * deviation * inverse, 0.0)
                weight = kept * kept
                weights.append(weight)
                products.append(weight * x)
            center = tree_sum(products) / tree_sum(weights)
        centers.append(center + mean)
    out_ref[...] = jnp.concatenate(centers, axis=0).T


def tree_sum(terms):
    sums = list(terms[:4])
    for index, term in enumerate(terms[4:]):
        sums[index % 4] = sums[index % 4] + term
    return (sums[0] + sums[1]) + (sums[2] + sums[3])


def stack_blocks(regrouped, win_count, source_count):
    parts, block, width = regrouped.shape
    pairs = width // win_count
    result = pl.pallas_call(
        functools.partial(stack_kernel, win_count=win_count),
        out_shape=jax.ShapeDtypeStruct((pairs, block), jnp.float32),
        in_specs=[pl.BlockSpec(memory_space=pltpu.VMEM)],
        out_specs=pl.BlockSpec(memory_space=pltpu.VMEM),
        scratch_shapes=[pltpu.VMEM((parts * win_count, block, pairs), jnp.float32)],
        compiler_params=pltpu.CompilerParams(vmem_limit_bytes=VMEM_LIMIT),
        name="bisquare_stack",
    )(regrouped)
    return result.reshape(source_count, pairs // source_count, block).transpose(2, 0, 1)


def per_device(spectra, source_channel):
    win_count = spectra.shape[0]
    chan_count = spectra.shape[2]
    source_count = source_channel.shape[0]
    peers = lax.axis_size("rcv")
    table = make_tables(spectra.shape[3], L, L // 2 + 16)
    source_rows = find_places(source_channel, peers, chan_count, 4 * (table.size + spectra.size))
    blocks = [spectra]
    for step in range(1, peers):
        blocks.append(lax.ppermute(spectra, "rcv", [(i, (i + step) % peers) for i in range(peers)]))
    corr = correlate(table, blocks, source_rows)
    parts = lax.axis_size("win")
    corr = corr.reshape(parts, L // parts, corr.shape[1])
    regrouped = lax.all_to_all(corr, "win", split_axis=0, concat_axis=0, tiled=True)
    return stack_blocks(regrouped, win_count, source_count)


def solution(mesh):
    return jax.shard_map(
        per_device,
        mesh=mesh,
        in_specs=(P("win", None, "rcv", None), P()),
        out_specs=P("win", None, "rcv"),
        check_vma=False,
    )
```

```python
import functools

import jax
import jax.numpy as jnp
import numpy as np
from jax import lax
from jax.experimental import pallas as pl
from jax.experimental.pallas import tpu as pltpu
from jax.sharding import PartitionSpec as P

L = 512
ITERS = 5
VMEM_LIMIT = 24 * 2**20


TUKEY = 4.685
EPSILON = 1e-06


def make_tables(bin_count, lag_count, rows):
    freq = np.arange(bin_count, dtype=np.int64)
    shifts = np.arange(lag_count // 2 + 1, dtype=np.int64)
    phase = shifts[:, None] * freq[None, :] % (2 * bin_count)
    angle = phase * (2.0 * np.pi / (2 * bin_count))
    factor = np.where(freq == 0, 1.0, 2.0) / np.sqrt(8.0 * bin_count)
    table = np.zeros((2, rows, bin_count), np.float32)
    table[0, : len(shifts)] = np.cos(angle) * factor
    table[1, : len(shifts)] = -np.sin(angle) * factor
    return jnp.asarray(table.astype(jnp.bfloat16))


def correlate_kernel(*refs, peers, chunk):
    rows_ref, table_ref = refs[:2]
    block_refs = refs[2 : 2 + peers]
    out_ref, even_ref, odd_ref, float_ref = refs[2 + peers :]
    win_count, _, chan_count, bin_count = block_refs[0].shape
    source_count = rows_ref.shape[0]
    half = out_ref.shape[0] // 2
    for start in range(0, bin_count, chunk):
        bins = slice(start, start + chunk)
        for k in range(peers):
            for w in range(win_count):
                for part in range(2):
                    float_ref[w, part, k * chan_count : (k + 1) * chan_count, bins] = block_refs[k][
                        w, part, :, bins
                    ].astype(jnp.float32)
        reals, imags = [], []
        for w in range(win_count):
            real_p = float_ref[w, 0, :chan_count, bins]
            imag_q = float_ref[w, 1, :chan_count, bins]
            for s in range(source_count):
                real_a = float_ref[w, 0, pl.ds(rows_ref[s], 1), bins]
                imag_b = float_ref[w, 1, pl.ds(rows_ref[s], 1), bins]
                reals.append((real_a * real_p + imag_b * imag_q).astype(jnp.bfloat16))
                imags.append((imag_b * real_p - real_a * imag_q).astype(jnp.bfloat16))
        for index, parts, sum_ref in ((0, reals, even_ref), (1, imags, odd_ref)):
            term = lax.dot_general(
                table_ref[index, :, bins],
                jnp.concatenate(parts, axis=0),
                (((1,), (1,)), ((), ())),
                preferred_element_type=jnp.float32,
            )
            if start == 0:
                sum_ref[...] = term
            else:
                sum_ref[...] += term
    out_ref[half:, :] = (even_ref[:half, :] + odd_ref[:half, :]).astype(jnp.bfloat16)
    back = (even_ref[...] - odd_ref[...]).astype(jnp.bfloat16)
    lag = lax.broadcasted_iota(jnp.int32, (half, half), 0)
    shift = lax.broadcasted_iota(jnp.int32, (half, half), 1)
    flip = (lag + shift == half).astype(jnp.bfloat16)
    turned = jnp.dot(flip, back[:half], preferred_element_type=jnp.float32)
    first = jnp.where(
        lax.broadcasted_iota(jnp.int32, turned.shape, 0) == 0,
        back[half : half + 16].astype(jnp.float32)[:1],
        turned,
    )
    out_ref[:half, :] = first.astype(jnp.bfloat16)


def correlate(table, blocks, source_rows):
    win_count, _, chan_count, bin_count = blocks[0].shape
    source_count = source_rows.shape[0]
    rows = table.shape[1]
    chunk = min(512, bin_count)
    width = win_count * source_count * chan_count
    vmem = pl.BlockSpec(memory_space=pltpu.VMEM)
    return pl.pallas_call(
        functools.partial(correlate_kernel, peers=len(blocks), chunk=chunk),
        out_shape=jax.ShapeDtypeStruct((L, width), jnp.bfloat16),
        in_specs=[pl.BlockSpec(memory_space=pltpu.SMEM), vmem] + [vmem] * len(blocks),
        out_specs=vmem,
        scratch_shapes=[
            pltpu.VMEM((rows, width), jnp.float32),
            pltpu.VMEM((rows, width), jnp.float32),
            pltpu.VMEM((win_count, 2, len(blocks) * chan_count, bin_count), jnp.float32),
        ],
        compiler_params=pltpu.CompilerParams(vmem_limit_bytes=VMEM_LIMIT),
        name="correlate",
    )(source_rows, table, *blocks)


def places_kernel(me_ref, channel_ref, out_ref, *, peers, chan_count):
    for s in range(channel_ref.shape[0]):
        channel = channel_ref[s]
        owner = lax.div(channel, chan_count)
        step = lax.rem(me_ref[0] - owner + peers, peers)
        out_ref[s] = step * chan_count + channel - owner * chan_count


def find_places(source_channel, peers, chan_count, meanwhile):
    me = lax.axis_index("rcv").astype(jnp.int32)
    smem = pl.BlockSpec(memory_space=pltpu.SMEM)
    return pl.pallas_call(
        functools.partial(places_kernel, peers=peers, chan_count=chan_count),
        out_shape=jax.ShapeDtypeStruct(source_channel.shape, jnp.int32),
        in_specs=[smem, smem],
        out_specs=smem,
        compiler_params=pltpu.CompilerParams(vmem_limit_bytes=VMEM_LIMIT),
        cost_estimate=pl.CostEstimate(flops=0, bytes_accessed=meanwhile, transcendentals=0),
        name="places",
    )(me[None], source_channel)


def stack_kernel(x_ref, out_ref, y_ref, *, win_count):
    parts, block, width = x_ref.shape
    pairs = width // win_count
    count = parts * win_count
    for part in range(parts):
        both = x_ref[part].astype(jnp.float32)
        for w in range(win_count):
            y_ref[part * win_count + w] = both[:, w * pairs : (w + 1) * pairs]
    rows = 8
    centers = []
    for start in range(0, block, rows):
        raw = [y_ref[n, start : start + rows, :] for n in range(count)]
        mean = tree_sum(raw) * (1.0 / count)
        samples = [x - mean for x in raw]
        variance = tree_sum([x * x for x in samples]) * (1.0 / count)
        center = jnp.zeros_like(mean)
        for iteration in range(ITERS):
            scale_two = variance + center * center + EPSILON
            inverse = 1.0 / (TUKEY * TUKEY * scale_two)
            weights, products = [], []
            for x in samples:
                deviation = x - center
                kept = jnp.maximum(1.0 - deviation * deviation * inverse, 0.0)
                weight = kept * kept
                weights.append(weight)
                products.append(weight * x)
            center = tree_sum(products) / tree_sum(weights)
        centers.append(center + mean)
    out_ref[...] = jnp.concatenate(centers, axis=0).T


def tree_sum(terms):
    sums = list(terms[:4])
    for index, term in enumerate(terms[4:]):
        sums[index % 4] = sums[index % 4] + term
    return (sums[0] + sums[1]) + (sums[2] + sums[3])


def stack_blocks(regrouped, win_count, source_count):
    parts, block, width = regrouped.shape
    pairs = width // win_count
    result = pl.pallas_call(
        functools.partial(stack_kernel, win_count=win_count),
        out_shape=jax.ShapeDtypeStruct((pairs, block), jnp.float32),
        in_specs=[pl.BlockSpec(memory_space=pltpu.VMEM)],
        out_specs=pl.BlockSpec(memory_space=pltpu.VMEM),
        scratch_shapes=[pltpu.VMEM((parts * win_count, block, pairs), jnp.float32)],
        compiler_params=pltpu.CompilerParams(vmem_limit_bytes=VMEM_LIMIT),
        name="bisquare_stack",
    )(regrouped)
    return result.reshape(source_count, pairs // source_count, block).transpose(2, 0, 1)


def per_device(spectra, source_channel):
    win_count = spectra.shape[0]
    chan_count = spectra.shape[2]
    source_count = source_channel.shape[0]
    peers = lax.axis_size("rcv")
    table = make_tables(spectra.shape[3], L, L // 2 + 16)
    source_rows = find_places(source_channel, peers, chan_count, 4 * (table.size + spectra.size))
    stay = [(i, i) for i in range(peers)]
    blocks = [lax.ppermute(spectra, "rcv", [(i, (i + step) % peers) for i in range(peers)]) for step in range(peers)]
    table = lax.ppermute(table, "rcv", stay)
    corr = correlate(table, blocks, source_rows)
    parts = lax.axis_size("win")
    corr = corr.reshape(parts, L // parts, corr.shape[1])
    regrouped = lax.all_to_all(corr, "win", split_axis=0, concat_axis=0, tiled=True)
    return stack_blocks(regrouped, win_count, source_count)


def solution(mesh):
    return jax.shard_map(
        per_device,
        mesh=mesh,
        in_specs=(P("win", None, "rcv", None), P()),
        out_specs=P("win", None, "rcv"),
        check_vma=False,
    )
```

```python
import functools

import jax
import jax.numpy as jnp
import numpy as np
from jax import lax
from jax.experimental import pallas as pl
from jax.experimental.pallas import tpu as pltpu
from jax.sharding import PartitionSpec as P

L = 512
ITERS = 5
VMEM_LIMIT = 24 * 2**20


TUKEY = 4.685
EPSILON = 1e-06


def make_tables(bin_count, lag_count, rows):
    freq = np.arange(bin_count, dtype=np.int64)
    shifts = np.arange(lag_count // 2 + 1, dtype=np.int64)
    phase = shifts[:, None] * freq[None, :] % (2 * bin_count)
    angle = phase * (2.0 * np.pi / (2 * bin_count))
    factor = np.where(freq == 0, 1.0, 2.0) / np.sqrt(8.0 * bin_count)
    table = np.zeros((2, rows, bin_count), np.float32)
    table[0, : len(shifts)] = np.cos(angle) * factor
    table[1, : len(shifts)] = -np.sin(angle) * factor
    return jnp.asarray(table.astype(jnp.bfloat16))


def correlate_kernel(*refs, peers, chunk):
    rows_ref, table_ref = refs[:2]
    block_refs = refs[2 : 2 + peers]
    out_ref, even_ref, odd_ref, float_ref = refs[2 + peers :]
    win_count, _, chan_count, bin_count = block_refs[0].shape
    source_count = rows_ref.shape[0]
    half = out_ref.shape[0] // 2
    for start in range(0, bin_count, chunk):
        bins = slice(start, start + chunk)
        for k in range(peers):
            for w in range(win_count):
                for part in range(2):
                    float_ref[w, part, k * chan_count : (k + 1) * chan_count, bins] = block_refs[k][
                        w, part, :, bins
                    ].astype(jnp.float32)
        reals, imags = [], []
        for w in range(win_count):
            real_p = float_ref[w, 0, :chan_count, bins]
            imag_q = float_ref[w, 1, :chan_count, bins]
            for s in range(source_count):
                real_a = float_ref[w, 0, pl.ds(rows_ref[s], 1), bins]
                imag_b = float_ref[w, 1, pl.ds(rows_ref[s], 1), bins]
                reals.append((real_a * real_p + imag_b * imag_q).astype(jnp.bfloat16))
                imags.append((imag_b * real_p - real_a * imag_q).astype(jnp.bfloat16))
        for index, parts, sum_ref in ((0, reals, even_ref), (1, imags, odd_ref)):
            term = lax.dot_general(
                table_ref[index, :, bins],
                jnp.concatenate(parts, axis=0),
                (((1,), (1,)), ((), ())),
                preferred_element_type=jnp.float32,
            )
            if start == 0:
                sum_ref[...] = term
            else:
                sum_ref[...] += term
    out_ref[half:, :] = (even_ref[:half, :] + odd_ref[:half, :]).astype(jnp.bfloat16)
    back = (even_ref[...] - odd_ref[...]).astype(jnp.bfloat16)
    lag = lax.broadcasted_iota(jnp.int32, (half, half), 0)
    shift = lax.broadcasted_iota(jnp.int32, (half, half), 1)
    flip = (lag + shift == half).astype(jnp.bfloat16)
    turned = jnp.dot(flip, back[:half], preferred_element_type=jnp.float32)
    first = jnp.where(
        lax.broadcasted_iota(jnp.int32, turned.shape, 0) == 0,
        back[half : half + 16].astype(jnp.float32)[:1],
        turned,
    )
    out_ref[:half, :] = first.astype(jnp.bfloat16)


def correlate(table, blocks, source_rows):
    win_count, _, chan_count, bin_count = blocks[0].shape
    source_count = source_rows.shape[0]
    rows = table.shape[1]
    chunk = min(512, bin_count)
    width = win_count * source_count * chan_count
    vmem = pl.BlockSpec(memory_space=pltpu.VMEM)
    return pl.pallas_call(
        functools.partial(correlate_kernel, peers=len(blocks), chunk=chunk),
        out_shape=jax.ShapeDtypeStruct((L, width), jnp.bfloat16),
        in_specs=[pl.BlockSpec(memory_space=pltpu.SMEM), vmem] + [vmem] * len(blocks),
        out_specs=vmem,
        scratch_shapes=[
            pltpu.VMEM((rows, width), jnp.float32),
            pltpu.VMEM((rows, width), jnp.float32),
            pltpu.VMEM((win_count, 2, len(blocks) * chan_count, bin_count), jnp.float32),
        ],
        compiler_params=pltpu.CompilerParams(vmem_limit_bytes=VMEM_LIMIT),
        name="correlate",
    )(source_rows, table, *blocks)


def places_kernel(me_ref, channel_ref, out_ref, *, peers, chan_count):
    for s in range(channel_ref.shape[0]):
        channel = channel_ref[s]
        owner = lax.div(channel, chan_count)
        step = lax.rem(me_ref[0] - owner + peers, peers)
        out_ref[s] = step * chan_count + channel - owner * chan_count


def find_places(source_channel, peers, chan_count, meanwhile):
    me = lax.axis_index("rcv").astype(jnp.int32)
    smem = pl.BlockSpec(memory_space=pltpu.SMEM)
    return pl.pallas_call(
        functools.partial(places_kernel, peers=peers, chan_count=chan_count),
        out_shape=jax.ShapeDtypeStruct(source_channel.shape, jnp.int32),
        in_specs=[smem, smem],
        out_specs=smem,
        compiler_params=pltpu.CompilerParams(vmem_limit_bytes=VMEM_LIMIT),
        cost_estimate=pl.CostEstimate(flops=meanwhile, bytes_accessed=0, transcendentals=0),
        name="places",
    )(me[None], source_channel)


def stack_kernel(x_ref, out_ref, y_ref, *, win_count):
    parts, block, width = x_ref.shape
    pairs = width // win_count
    count = parts * win_count
    for part in range(parts):
        both = x_ref[part].astype(jnp.float32)
        for w in range(win_count):
            y_ref[part * win_count + w] = both[:, w * pairs : (w + 1) * pairs]
    rows = 8
    centers = []
    for start in range(0, block, rows):
        raw = [y_ref[n, start : start + rows, :] for n in range(count)]
        mean = tree_sum(raw) * (1.0 / count)
        samples = [x - mean for x in raw]
        variance = tree_sum([x * x for x in samples]) * (1.0 / count)
        center = jnp.zeros_like(mean)
        for iteration in range(ITERS):
            scale_two = variance + center * center + EPSILON
            inverse = 1.0 / (TUKEY * TUKEY * scale_two)
            weights, products = [], []
            for x in samples:
                deviation = x - center
                kept = jnp.maximum(1.0 - deviation * deviation * inverse, 0.0)
                weight = kept * kept
                weights.append(weight)
                products.append(weight * x)
            center = tree_sum(products) / tree_sum(weights)
        centers.append(center + mean)
    out_ref[...] = jnp.concatenate(centers, axis=0).T


def tree_sum(terms):
    sums = list(terms[:4])
    for index, term in enumerate(terms[4:]):
        sums[index % 4] = sums[index % 4] + term
    return (sums[0] + sums[1]) + (sums[2] + sums[3])


def stack_blocks(regrouped, win_count, source_count):
    parts, block, width = regrouped.shape
    pairs = width // win_count
    result = pl.pallas_call(
        functools.partial(stack_kernel, win_count=win_count),
        out_shape=jax.ShapeDtypeStruct((pairs, block), jnp.float32),
        in_specs=[pl.BlockSpec(memory_space=pltpu.VMEM)],
        out_specs=pl.BlockSpec(memory_space=pltpu.VMEM),
        scratch_shapes=[pltpu.VMEM((parts * win_count, block, pairs), jnp.float32)],
        compiler_params=pltpu.CompilerParams(vmem_limit_bytes=VMEM_LIMIT),
        name="bisquare_stack",
    )(regrouped)
    return result.reshape(source_count, pairs // source_count, block).transpose(2, 0, 1)


def per_device(spectra, source_channel):
    win_count = spectra.shape[0]
    chan_count = spectra.shape[2]
    source_count = source_channel.shape[0]
    peers = lax.axis_size("rcv")
    table = make_tables(spectra.shape[3], L, L // 2 + 16)
    source_rows = find_places(source_channel, peers, chan_count, 2000 * table.size)
    blocks = [spectra]
    for step in range(1, peers):
        blocks.append(lax.ppermute(spectra, "rcv", [(i, (i + step) % peers) for i in range(peers)]))
    corr = correlate(table, blocks, source_rows)
    parts = lax.axis_size("win")
    corr = corr.reshape(parts, L // parts, corr.shape[1])
    regrouped = lax.all_to_all(corr, "win", split_axis=0, concat_axis=0, tiled=True)
    return stack_blocks(regrouped, win_count, source_count)


def solution(mesh):
    return jax.shard_map(
        per_device,
        mesh=mesh,
        in_specs=(P("win", None, "rcv", None), P()),
        out_specs=P("win", None, "rcv"),
        check_vma=False,
    )
```

```python
import functools

import jax
import jax.numpy as jnp
import numpy as np
from jax import lax
from jax.experimental import pallas as pl
from jax.experimental.pallas import tpu as pltpu
from jax.sharding import PartitionSpec as P

L = 512
ITERS = 5
VMEM_LIMIT = 24 * 2**20


TUKEY = 4.685
EPSILON = 1e-06


def make_tables(bin_count, lag_count, rows):
    freq = np.arange(bin_count, dtype=np.int64)
    shifts = np.arange(lag_count // 2 + 1, dtype=np.int64)
    phase = shifts[:, None] * freq[None, :] % (2 * bin_count)
    angle = phase * (2.0 * np.pi / (2 * bin_count))
    factor = np.where(freq == 0, 1.0, 2.0) / np.sqrt(8.0 * bin_count)
    table = np.zeros((2, rows, bin_count), np.float32)
    table[0, : len(shifts)] = np.cos(angle) * factor
    table[1, : len(shifts)] = -np.sin(angle) * factor
    return jnp.asarray(table.astype(jnp.bfloat16))


def correlate_kernel(*refs, peers, chunk):
    channel_ref, table_ref, flip_ref = refs[:3]
    block_refs = refs[3 : 3 + peers]
    out_ref, even_ref, odd_ref, float_ref = refs[3 + peers :]
    win_count, _, chan_count, bin_count = block_refs[0].shape
    source_count = channel_ref.shape[0]
    half = out_ref.shape[0] // 2
    me = lax.axis_index("rcv")
    rows = []
    for s in range(source_count):
        owner = lax.div(channel_ref[s], chan_count)
        place = lax.rem(me - owner + peers, peers) * chan_count
        rows.append(place + lax.rem(channel_ref[s], chan_count))
    for start in range(0, bin_count, chunk):
        bins = slice(start, start + chunk)
        for k in range(peers):
            for w in range(win_count):
                for part in range(2):
                    float_ref[w, part, k * chan_count : (k + 1) * chan_count, bins] = block_refs[k][
                        w, part, :, bins
                    ].astype(jnp.float32)
        reals, imags = [], []
        for w in range(win_count):
            real_p = float_ref[w, 0, :chan_count, bins]
            imag_q = float_ref[w, 1, :chan_count, bins]
            for s in range(source_count):
                real_a = float_ref[w, 0, pl.ds(rows[s], 1), bins]
                imag_b = float_ref[w, 1, pl.ds(rows[s], 1), bins]
                reals.append((real_a * real_p + imag_b * imag_q).astype(jnp.bfloat16))
                imags.append((imag_b * real_p - real_a * imag_q).astype(jnp.bfloat16))
        for index, parts, sum_ref in ((0, reals, even_ref), (1, imags, odd_ref)):
            term = lax.dot_general(
                table_ref[index, :, bins],
                jnp.concatenate(parts, axis=0),
                (((1,), (1,)), ((), ())),
                preferred_element_type=jnp.float32,
            )
            if start == 0:
                sum_ref[...] = term
            else:
                sum_ref[...] += term
    out_ref[half:, :] = (even_ref[:half, :] + odd_ref[:half, :]).astype(jnp.bfloat16)
    back = (even_ref[...] - odd_ref[...]).astype(jnp.bfloat16)
    turned = jnp.dot(flip_ref[...], back[:half], preferred_element_type=jnp.float32)
    first = jnp.where(
        lax.broadcasted_iota(jnp.int32, turned.shape, 0) == 0,
        back[half : half + 16].astype(jnp.float32)[:1],
        turned,
    )
    out_ref[:half, :] = first.astype(jnp.bfloat16)


def correlate(source_channel, table, flip, blocks):
    win_count, _, chan_count, bin_count = blocks[0].shape
    source_count = source_channel.shape[0]
    rows = table.shape[1]
    chunk = min(512, bin_count)
    width = win_count * source_count * chan_count
    vmem = pl.BlockSpec(memory_space=pltpu.VMEM)
    return pl.pallas_call(
        functools.partial(correlate_kernel, peers=len(blocks), chunk=chunk),
        out_shape=jax.ShapeDtypeStruct((L, width), jnp.bfloat16),
        in_specs=[pl.BlockSpec(memory_space=pltpu.SMEM), vmem, vmem] + [vmem] * len(blocks),
        out_specs=vmem,
        scratch_shapes=[
            pltpu.VMEM((rows, width), jnp.float32),
            pltpu.VMEM((rows, width), jnp.float32),
            pltpu.VMEM((win_count, 2, len(blocks) * chan_count, bin_count), jnp.float32),
        ],
        compiler_params=pltpu.CompilerParams(vmem_limit_bytes=VMEM_LIMIT),
        name="correlate",
    )(source_channel, table, flip, *blocks)


def flip_kernel(out_ref):
    lag = lax.broadcasted_iota(jnp.int32, out_ref.shape, 0)
    shift = lax.broadcasted_iota(jnp.int32, out_ref.shape, 1)
    out_ref[...] = (lag + shift == out_ref.shape[0]).astype(jnp.float32).astype(jnp.bfloat16)


def make_flip(half, meanwhile):
    return pl.pallas_call(
        flip_kernel,
        out_shape=jax.ShapeDtypeStruct((half, half), jnp.bfloat16),
        out_specs=pl.BlockSpec(memory_space=pltpu.VMEM),
        compiler_params=pltpu.CompilerParams(vmem_limit_bytes=VMEM_LIMIT),
        cost_estimate=pl.CostEstimate(flops=meanwhile, bytes_accessed=0, transcendentals=0),
        name="make_flip",
    )()


def stack_kernel(x_ref, out_ref, y_ref, *, win_count):
    parts, block, width = x_ref.shape
    pairs = width // win_count
    count = parts * win_count
    for part in range(parts):
        both = x_ref[part].astype(jnp.float32)
        for w in range(win_count):
            y_ref[part * win_count + w] = both[:, w * pairs : (w + 1) * pairs]
    rows = 8
    centers = []
    for start in range(0, block, rows):
        raw = [y_ref[n, start : start + rows, :] for n in range(count)]
        mean = tree_sum(raw) * (1.0 / count)
        samples = [x - mean for x in raw]
        variance = tree_sum([x * x for x in samples]) * (1.0 / count)
        center = jnp.zeros_like(mean)
        for iteration in range(ITERS):
            scale_two = variance + center * center + EPSILON
            inverse = 1.0 / (TUKEY * TUKEY * scale_two)
            weights, products = [], []
            for x in samples:
                deviation = x - center
                kept = jnp.maximum(1.0 - deviation * deviation * inverse, 0.0)
                weight = kept * kept
                weights.append(weight)
                products.append(weight * x)
            center = tree_sum(products) / tree_sum(weights)
        centers.append(center + mean)
    out_ref[...] = jnp.concatenate(centers, axis=0).T


def tree_sum(terms):
    sums = list(terms[:4])
    for index, term in enumerate(terms[4:]):
        sums[index % 4] = sums[index % 4] + term
    return (sums[0] + sums[1]) + (sums[2] + sums[3])


def stack_blocks(regrouped, win_count, source_count):
    parts, block, width = regrouped.shape
    pairs = width // win_count
    result = pl.pallas_call(
        functools.partial(stack_kernel, win_count=win_count),
        out_shape=jax.ShapeDtypeStruct((pairs, block), jnp.float32),
        in_specs=[pl.BlockSpec(memory_space=pltpu.VMEM)],
        out_specs=pl.BlockSpec(memory_space=pltpu.VMEM),
        scratch_shapes=[pltpu.VMEM((parts * win_count, block, pairs), jnp.float32)],
        compiler_params=pltpu.CompilerParams(vmem_limit_bytes=VMEM_LIMIT),
        name="bisquare_stack",
    )(regrouped)
    return result.reshape(source_count, pairs // source_count, block).transpose(2, 0, 1)


def per_device(spectra, source_channel):
    win_count = spectra.shape[0]
    source_count = source_channel.shape[0]
    peers = lax.axis_size("rcv")
    table = make_tables(spectra.shape[3], L, L // 2 + 16)
    flip = make_flip(L // 2, 2000 * table.size)
    blocks = [spectra]
    for step in range(1, peers):
        blocks.append(lax.ppermute(spectra, "rcv", [(i, (i + step) % peers) for i in range(peers)]))
    corr = correlate(source_channel, table, flip, blocks)
    parts = lax.axis_size("win")
    corr = corr.reshape(parts, L // parts, corr.shape[1])
    regrouped = lax.all_to_all(corr, "win", split_axis=0, concat_axis=0, tiled=True)
    return stack_blocks(regrouped, win_count, source_count)


def solution(mesh):
    return jax.shard_map(
        per_device,
        mesh=mesh,
        in_specs=(P("win", None, "rcv", None), P()),
        out_specs=P("win", None, "rcv"),
        check_vma=False,
    )
```

```python
import functools

import jax
import jax.numpy as jnp
import numpy as np
from jax import lax
from jax.experimental import pallas as pl
from jax.experimental.pallas import tpu as pltpu
from jax.sharding import PartitionSpec as P

L = 512
ITERS = 5
VMEM_LIMIT = 24 * 2**20


TUKEY = 4.685
EPSILON = 1e-06


def make_tables(bin_count, lag_count, rows):
    freq = np.arange(bin_count, dtype=np.int64)
    shifts = np.arange(lag_count // 2 + 1, dtype=np.int64)
    phase = shifts[:, None] * freq[None, :] % (2 * bin_count)
    angle = phase * (2.0 * np.pi / (2 * bin_count))
    factor = np.where(freq == 0, 1.0, 2.0) / np.sqrt(8.0 * bin_count)
    table = np.zeros((2, rows, bin_count), np.float32)
    table[0, : len(shifts)] = np.cos(angle) * factor
    table[1, : len(shifts)] = -np.sin(angle) * factor
    return jnp.asarray(table.astype(jnp.bfloat16))


def correlate_kernel(*refs, peers, chunk, window):
    channel_ref, table_ref, flip_ref = refs[:3]
    block_refs = refs[3 : 3 + peers]
    out_ref, even_ref, odd_ref, float_ref = refs[3 + peers :]
    _, _, chan_count, bin_count = block_refs[0].shape
    source_count = channel_ref.shape[0]
    half = out_ref.shape[0] // 2
    me = lax.axis_index("rcv")
    rows = []
    for s in range(source_count):
        owner = lax.div(channel_ref[s], chan_count)
        place = lax.rem(me - owner + peers, peers) * chan_count
        rows.append(place + lax.rem(channel_ref[s], chan_count))
    for start in range(0, bin_count, chunk):
        bins = slice(start, start + chunk)
        for k in range(peers):
            for part in range(2):
                float_ref[part, k * chan_count : (k + 1) * chan_count, bins] = block_refs[k][
                    window, part, :, bins
                ].astype(jnp.float32)
        reals, imags = [], []
        real_p = float_ref[0, :chan_count, bins]
        imag_q = float_ref[1, :chan_count, bins]
        for s in range(source_count):
            real_a = float_ref[0, pl.ds(rows[s], 1), bins]
            imag_b = float_ref[1, pl.ds(rows[s], 1), bins]
            reals.append((real_a * real_p + imag_b * imag_q).astype(jnp.bfloat16))
            imags.append((imag_b * real_p - real_a * imag_q).astype(jnp.bfloat16))
        for index, parts, sum_ref in ((0, reals, even_ref), (1, imags, odd_ref)):
            term = lax.dot_general(
                table_ref[index, :, bins],
                jnp.concatenate(parts, axis=0),
                (((1,), (1,)), ((), ())),
                preferred_element_type=jnp.float32,
            )
            if start == 0:
                sum_ref[...] = term
            else:
                sum_ref[...] += term
    out_ref[half:, :] = (even_ref[:half, :] + odd_ref[:half, :]).astype(jnp.bfloat16)
    back = (even_ref[...] - odd_ref[...]).astype(jnp.bfloat16)
    turned = jnp.dot(flip_ref[...], back[:half], preferred_element_type=jnp.float32)
    first = jnp.where(
        lax.broadcasted_iota(jnp.int32, turned.shape, 0) == 0,
        back[half : half + 16].astype(jnp.float32)[:1],
        turned,
    )
    out_ref[:half, :] = first.astype(jnp.bfloat16)


def correlate(source_channel, table, flip, blocks, window):
    _, _, chan_count, bin_count = blocks[0].shape
    source_count = source_channel.shape[0]
    rows = table.shape[1]
    chunk = min(512, bin_count)
    width = source_count * chan_count
    vmem = pl.BlockSpec(memory_space=pltpu.VMEM)
    return pl.pallas_call(
        functools.partial(correlate_kernel, peers=len(blocks), chunk=chunk, window=window),
        out_shape=jax.ShapeDtypeStruct((L, width), jnp.bfloat16),
        in_specs=[pl.BlockSpec(memory_space=pltpu.SMEM), vmem, vmem] + [vmem] * len(blocks),
        out_specs=vmem,
        scratch_shapes=[
            pltpu.VMEM((rows, width), jnp.float32),
            pltpu.VMEM((rows, width), jnp.float32),
            pltpu.VMEM((2, len(blocks) * chan_count, bin_count), jnp.float32),
        ],
        compiler_params=pltpu.CompilerParams(vmem_limit_bytes=VMEM_LIMIT),
        name="correlate",
    )(source_channel, table, flip, *blocks)


def flip_kernel(out_ref):
    lag = lax.broadcasted_iota(jnp.int32, out_ref.shape, 0)
    shift = lax.broadcasted_iota(jnp.int32, out_ref.shape, 1)
    out_ref[...] = (lag + shift == out_ref.shape[0]).astype(jnp.float32).astype(jnp.bfloat16)


def make_flip(half, meanwhile):
    return pl.pallas_call(
        flip_kernel,
        out_shape=jax.ShapeDtypeStruct((half, half), jnp.bfloat16),
        out_specs=pl.BlockSpec(memory_space=pltpu.VMEM),
        compiler_params=pltpu.CompilerParams(vmem_limit_bytes=VMEM_LIMIT),
        cost_estimate=pl.CostEstimate(flops=meanwhile, bytes_accessed=0, transcendentals=0),
        name="make_flip",
    )()


def stack_kernel(*refs):
    window_refs, out_ref, y_ref = refs[:-2], refs[-2], refs[-1]
    parts, block, pairs = window_refs[0].shape
    count = parts * len(window_refs)
    for w, x_ref in enumerate(window_refs):
        for part in range(parts):
            y_ref[w * parts + part] = x_ref[part].astype(jnp.float32)
    rows = 8
    centers = []
    for start in range(0, block, rows):
        raw = [y_ref[n, start : start + rows, :] for n in range(count)]
        mean = tree_sum(raw) * (1.0 / count)
        samples = [x - mean for x in raw]
        variance = tree_sum([x * x for x in samples]) * (1.0 / count)
        center = jnp.zeros_like(mean)
        for iteration in range(ITERS):
            scale_two = variance + center * center + EPSILON
            inverse = 1.0 / (TUKEY * TUKEY * scale_two)
            weights, products = [], []
            for x in samples:
                deviation = x - center
                kept = jnp.maximum(1.0 - deviation * deviation * inverse, 0.0)
                weight = kept * kept
                weights.append(weight)
                products.append(weight * x)
            center = tree_sum(products) / tree_sum(weights)
        centers.append(center + mean)
    out_ref[...] = jnp.concatenate(centers, axis=0).T


def tree_sum(terms):
    sums = list(terms[:4])
    for index, term in enumerate(terms[4:]):
        sums[index % 4] = sums[index % 4] + term
    return (sums[0] + sums[1]) + (sums[2] + sums[3])


def stack_blocks(received, source_count):
    win_count = len(received)
    parts, block, pairs = received[0].shape
    result = pl.pallas_call(
        stack_kernel,
        out_shape=jax.ShapeDtypeStruct((pairs, block), jnp.float32),
        in_specs=[pl.BlockSpec(memory_space=pltpu.VMEM)] * win_count,
        out_specs=pl.BlockSpec(memory_space=pltpu.VMEM),
        scratch_shapes=[pltpu.VMEM((parts * win_count, block, pairs), jnp.float32)],
        compiler_params=pltpu.CompilerParams(vmem_limit_bytes=VMEM_LIMIT),
        name="bisquare_stack",
    )(*received)
    return result.reshape(source_count, pairs // source_count, block).transpose(2, 0, 1)


def per_device(spectra, source_channel):
    win_count = spectra.shape[0]
    source_count = source_channel.shape[0]
    peers = lax.axis_size("rcv")
    table = make_tables(spectra.shape[3], L, L // 2 + 16)
    flip = make_flip(L // 2, 2000 * table.size)
    blocks = [spectra]
    for step in range(1, peers):
        blocks.append(lax.ppermute(spectra, "rcv", [(i, (i + step) % peers) for i in range(peers)]))
    parts = lax.axis_size("win")
    received = []
    for window in range(win_count):
        corr = correlate(source_channel, table, flip, blocks, window)
        corr = corr.reshape(parts, L // parts, corr.shape[1])
        received.append(lax.all_to_all(corr, "win", split_axis=0, concat_axis=0, tiled=True))
    return stack_blocks(received, source_count)


def solution(mesh):
    return jax.shard_map(
        per_device,
        mesh=mesh,
        in_specs=(P("win", None, "rcv", None), P()),
        out_specs=P("win", None, "rcv"),
        check_vma=False,
    )
```

```python
import functools

import jax
import jax.numpy as jnp
import numpy as np
from jax import lax
from jax.experimental import pallas as pl
from jax.experimental.pallas import tpu as pltpu
from jax.sharding import PartitionSpec as P

L = 512
ITERS = 5
VMEM_LIMIT = 24 * 2**20


TUKEY = 4.685
EPSILON = 1e-06


def make_tables(bin_count, lag_count, rows):
    freq = np.arange(bin_count, dtype=np.int64)
    shifts = np.arange(lag_count // 2 + 1, dtype=np.int64)
    phase = shifts[:, None] * freq[None, :] % (2 * bin_count)
    angle = phase * (2.0 * np.pi / (2 * bin_count))
    factor = np.where(freq == 0, 1.0, 2.0) / np.sqrt(8.0 * bin_count)
    table = np.zeros((2, rows, bin_count), np.float32)
    table[0, : len(shifts)] = np.cos(angle) * factor
    table[1, : len(shifts)] = -np.sin(angle) * factor
    return jnp.asarray(table.astype(jnp.bfloat16))


def flip_kernel(out_ref):
    lag = lax.broadcasted_iota(jnp.int32, out_ref.shape, 0)
    shift = lax.broadcasted_iota(jnp.int32, out_ref.shape, 1)
    out_ref[...] = (lag + shift == out_ref.shape[0]).astype(jnp.float32).astype(jnp.bfloat16)


def make_flip(half, meanwhile):
    return pl.pallas_call(
        flip_kernel,
        out_shape=jax.ShapeDtypeStruct((half, half), jnp.bfloat16),
        out_specs=pl.BlockSpec(memory_space=pltpu.VMEM),
        compiler_params=pltpu.CompilerParams(vmem_limit_bytes=VMEM_LIMIT),
        cost_estimate=pl.CostEstimate(flops=meanwhile, bytes_accessed=0, transcendentals=0),
        name="make_flip",
    )()


def share(win_count, source_count, peers):
    items = win_count * source_count // peers
    assert items * peers == win_count * source_count
    assert items % source_count == 0 or source_count % items == 0
    return items


def correlate_kernel(*refs, peers, chunk):
    channel_ref, table_ref, flip_ref = refs[:3]
    block_refs = refs[3 : 3 + peers]
    out_ref, lags_ref, even_ref, odd_ref, float_ref = refs[3 + peers :]
    win_count, _, chan_count, bin_count = block_refs[0].shape
    source_count = channel_ref.shape[0]
    items = share(win_count, source_count, peers)
    windows = float_ref.shape[0]
    parts, _, block, width = out_ref.shape
    half = flip_ref.shape[0]
    me = lax.axis_index("rcv")
    first = lax.div(me * items, source_count)
    rows = []
    for t in range(items):
        channel = channel_ref[lax.rem(me * items + t, source_count)]
        owner = lax.div(channel, chan_count)
        place = lax.rem(me - owner + peers, peers) * chan_count
        rows.append(place + lax.rem(channel, chan_count))
    for start in range(0, bin_count, chunk):
        bins = slice(start, start + chunk)
        for k in range(peers):
            for w in range(windows):
                for part in range(2):
                    float_ref[w, part, k * chan_count : (k + 1) * chan_count, bins] = block_refs[k][
                        first + w, part, :, bins
                    ].astype(jnp.float32)
        reals, imags = [], []
        for k in range(peers):
            receivers = slice(k * chan_count, (k + 1) * chan_count)
            for t in range(items):
                w = t // source_count
                real_p = float_ref[w, 0, receivers, bins]
                imag_q = float_ref[w, 1, receivers, bins]
                real_a = float_ref[w, 0, pl.ds(rows[t], 1), bins]
                imag_b = float_ref[w, 1, pl.ds(rows[t], 1), bins]
                reals.append((real_a * real_p + imag_b * imag_q).astype(jnp.bfloat16))
                imags.append((imag_b * real_p - real_a * imag_q).astype(jnp.bfloat16))
        for index, terms, sum_ref in ((0, reals, even_ref), (1, imags, odd_ref)):
            term = lax.dot_general(
                table_ref[index, :, bins],
                jnp.concatenate(terms, axis=0),
                (((1,), (1,)), ((), ())),
                preferred_element_type=jnp.float32,
            )
            if start == 0:
                sum_ref[...] = term
            else:
                sum_ref[...] += term
    lags_ref[half:, :] = even_ref[:half, :] + odd_ref[:half, :]
    back = (even_ref[...] - odd_ref[...]).astype(jnp.bfloat16)
    turned = jnp.dot(flip_ref[...], back[:half], preferred_element_type=jnp.float32)
    lags_ref[:half, :] = jnp.where(
        lax.broadcasted_iota(jnp.int32, turned.shape, 0) == 0,
        back[half : half + 16].astype(jnp.float32)[:1],
        turned,
    )
    for k in range(peers):
        owner = lax.rem(me - k + peers, peers)
        for part in range(parts):
            out_ref[part, owner] = lags_ref[
                part * block : (part + 1) * block, k * width : (k + 1) * width
            ].astype(jnp.bfloat16)


def correlate(source_channel, table, flip, blocks, parts):
    win_count, _, chan_count, bin_count = blocks[0].shape
    source_count = source_channel.shape[0]
    peers = len(blocks)
    items = share(win_count, source_count, peers)
    rows = table.shape[1]
    chunk = min(512, bin_count)
    width = items * chan_count
    vmem = pl.BlockSpec(memory_space=pltpu.VMEM)
    return pl.pallas_call(
        functools.partial(correlate_kernel, peers=peers, chunk=chunk),
        out_shape=jax.ShapeDtypeStruct((parts, peers, L // parts, width), jnp.bfloat16),
        in_specs=[pl.BlockSpec(memory_space=pltpu.SMEM), vmem, vmem] + [vmem] * peers,
        out_specs=vmem,
        scratch_shapes=[
            pltpu.VMEM((L, peers * width), jnp.float32),
            pltpu.VMEM((rows, peers * width), jnp.float32),
            pltpu.VMEM((rows, peers * width), jnp.float32),
            pltpu.VMEM((max(1, items // source_count), 2, peers * chan_count, bin_count), jnp.float32),
        ],
        compiler_params=pltpu.CompilerParams(vmem_limit_bytes=VMEM_LIMIT),
        name="correlate",
    )(source_channel, table, flip, *blocks)


def stack_kernel(x_ref, out_ref, y_ref):
    count, block, pairs = x_ref.shape
    for n in range(count):
        y_ref[n] = x_ref[n].astype(jnp.float32)
    rows = 8
    centers = []
    for start in range(0, block, rows):
        raw = [y_ref[n, start : start + rows, :] for n in range(count)]
        mean = tree_sum(raw) * (1.0 / count)
        samples = [x - mean for x in raw]
        variance = tree_sum([x * x for x in samples]) * (1.0 / count)
        center = jnp.zeros_like(mean)
        for iteration in range(ITERS):
            scale_two = variance + center * center + EPSILON
            inverse = 1.0 / (TUKEY * TUKEY * scale_two)
            weights, products = [], []
            for x in samples:
                deviation = x - center
                kept = jnp.maximum(1.0 - deviation * deviation * inverse, 0.0)
                weight = kept * kept
                weights.append(weight)
                products.append(weight * x)
            center = tree_sum(products) / tree_sum(weights)
        centers.append(center + mean)
    out_ref[...] = jnp.concatenate(centers, axis=0).T


def tree_sum(terms):
    sums = list(terms[:4])
    for index, term in enumerate(terms[4:]):
        sums[index % 4] = sums[index % 4] + term
    return (sums[0] + sums[1]) + (sums[2] + sums[3])


def stack_blocks(samples, source_count):
    count, block, pairs = samples.shape
    result = pl.pallas_call(
        stack_kernel,
        out_shape=jax.ShapeDtypeStruct((pairs, block), jnp.float32),
        in_specs=[pl.BlockSpec(memory_space=pltpu.VMEM)],
        out_specs=pl.BlockSpec(memory_space=pltpu.VMEM),
        scratch_shapes=[pltpu.VMEM((count, block, pairs), jnp.float32)],
        compiler_params=pltpu.CompilerParams(vmem_limit_bytes=VMEM_LIMIT),
        name="bisquare_stack",
    )(samples)
    return result.reshape(source_count, pairs // source_count, block).transpose(2, 0, 1)


def per_device(spectra, source_channel):
    win_count, _, chan_count, bin_count = spectra.shape
    source_count = source_channel.shape[0]
    peers = lax.axis_size("rcv")
    parts = lax.axis_size("win")
    block = L // parts
    items = share(win_count, source_count, peers)
    table = make_tables(bin_count, L, L // 2 + 16)
    flip = make_flip(L // 2, 2000 * table.size)
    blocks = [spectra]
    for step in range(1, peers):
        blocks.append(lax.ppermute(spectra, "rcv", [(i, (i + step) % peers) for i in range(peers)]))
    corr = correlate(source_channel, table, flip, blocks, parts)
    corr = corr.reshape(parts * peers, block, items * chan_count)
    moved = lax.all_to_all(corr, ("win", "rcv"), split_axis=0, concat_axis=0, tiled=True)
    if items != source_count:
        moved = moved.reshape(parts * peers, block, items, chan_count).transpose(0, 2, 1, 3)
        moved = moved.reshape(parts * win_count, source_count, block, chan_count).transpose(0, 2, 1, 3)
        moved = moved.reshape(parts * win_count, block, source_count * chan_count)
    return stack_blocks(moved, source_count)


def solution(mesh):
    return jax.shard_map(
        per_device,
        mesh=mesh,
        in_specs=(P("win", None, "rcv", None), P()),
        out_specs=P("win", None, "rcv"),
        check_vma=False,
    )
```

```python
import functools

import jax
import jax.numpy as jnp
import numpy as np
from jax import lax
from jax.experimental import pallas as pl
from jax.experimental.pallas import tpu as pltpu
from jax.sharding import PartitionSpec as P

L = 512
ITERS = 5
VMEM_LIMIT = 24 * 2**20


TUKEY = 4.685
EPSILON = 1e-06


def make_tables(bin_count, lag_count, rows):
    freq = np.arange(bin_count, dtype=np.int64)
    shifts = np.arange(lag_count // 2 + 1, dtype=np.int64)
    phase = shifts[:, None] * freq[None, :] % (2 * bin_count)
    angle = phase * (2.0 * np.pi / (2 * bin_count))
    factor = np.where(freq == 0, 1.0, 2.0) / np.sqrt(8.0 * bin_count)
    table = np.zeros((2, rows, bin_count), np.float32)
    table[0, : len(shifts)] = np.cos(angle) * factor
    table[1, : len(shifts)] = -np.sin(angle) * factor
    return jnp.asarray(table.astype(jnp.bfloat16))


def flip_kernel(out_ref):
    lag = lax.broadcasted_iota(jnp.int32, out_ref.shape, 0)
    shift = lax.broadcasted_iota(jnp.int32, out_ref.shape, 1)
    out_ref[...] = (lag + shift == out_ref.shape[0]).astype(jnp.float32).astype(jnp.bfloat16)


def make_flip(half, meanwhile):
    return pl.pallas_call(
        flip_kernel,
        out_shape=jax.ShapeDtypeStruct((half, half), jnp.bfloat16),
        out_specs=pl.BlockSpec(memory_space=pltpu.VMEM),
        compiler_params=pltpu.CompilerParams(vmem_limit_bytes=VMEM_LIMIT),
        cost_estimate=pl.CostEstimate(flops=meanwhile, bytes_accessed=0, transcendentals=0),
        name="make_flip",
    )()


def share(win_count, source_count, peers):
    items = win_count * source_count // peers
    assert items * peers == win_count * source_count
    assert items % source_count == 0 or source_count % items == 0
    return items


def correlate_kernel(*refs, peers, chunk):
    channel_ref, table_ref, flip_ref = refs[:3]
    block_refs = refs[3 : 3 + peers]
    out_ref, lags_ref, even_ref, odd_ref, float_ref = refs[3 + peers :]
    win_count, _, chan_count, bin_count = block_refs[0].shape
    source_count = channel_ref.shape[0]
    items = share(win_count, source_count, peers)
    windows = float_ref.shape[0]
    parts, _, block, width = out_ref.shape
    half = flip_ref.shape[0]
    me = lax.axis_index("rcv")
    first = lax.div(me * items, source_count)
    rows = []
    for t in range(items):
        channel = channel_ref[lax.rem(me * items + t, source_count)]
        owner = lax.div(channel, chan_count)
        place = lax.rem(me - owner + peers, peers) * chan_count
        rows.append(place + lax.rem(channel, chan_count))
    for start in range(0, bin_count, chunk):
        bins = slice(start, start + chunk)
        for k in range(peers):
            for w in range(windows):
                for part in range(2):
                    float_ref[w, part, k * chan_count : (k + 1) * chan_count, bins] = block_refs[k][
                        first + w, part, :, bins
                    ].astype(jnp.float32)
        reals, imags = [], []
        for t in range(items):
            w = t // source_count
            real_p = float_ref[w, 0, :, bins]
            imag_q = float_ref[w, 1, :, bins]
            real_a = float_ref[w, 0, pl.ds(rows[t], 1), bins]
            imag_b = float_ref[w, 1, pl.ds(rows[t], 1), bins]
            reals.append((real_a * real_p + imag_b * imag_q).astype(jnp.bfloat16))
            imags.append((imag_b * real_p - real_a * imag_q).astype(jnp.bfloat16))
        receivers = [slice(k * chan_count, (k + 1) * chan_count) for k in range(peers)]
        reals = [term[part] for part in receivers for term in reals]
        imags = [term[part] for part in receivers for term in imags]
        for index, terms, sum_ref in ((0, reals, even_ref), (1, imags, odd_ref)):
            term = lax.dot_general(
                table_ref[index, :, bins],
                jnp.concatenate(terms, axis=0),
                (((1,), (1,)), ((), ())),
                preferred_element_type=jnp.float32,
            )
            if start == 0:
                sum_ref[...] = term
            else:
                sum_ref[...] += term
    lags_ref[half:, :] = even_ref[:half, :] + odd_ref[:half, :]
    back = (even_ref[...] - odd_ref[...]).astype(jnp.bfloat16)
    turned = jnp.dot(flip_ref[...], back[:half], preferred_element_type=jnp.float32)
    lags_ref[:half, :] = jnp.where(
        lax.broadcasted_iota(jnp.int32, turned.shape, 0) == 0,
        back[half : half + 16].astype(jnp.float32)[:1],
        turned,
    )
    for k in range(peers):
        owner = lax.rem(me - k + peers, peers)
        for part in range(parts):
            out_ref[part, owner] = lags_ref[
                part * block : (part + 1) * block, k * width : (k + 1) * width
            ].astype(jnp.bfloat16)


def correlate(source_channel, table, flip, blocks, parts):
    win_count, _, chan_count, bin_count = blocks[0].shape
    source_count = source_channel.shape[0]
    peers = len(blocks)
    items = share(win_count, source_count, peers)
    rows = table.shape[1]
    chunk = min(1024, bin_count)
    width = items * chan_count
    vmem = pl.BlockSpec(memory_space=pltpu.VMEM)
    return pl.pallas_call(
        functools.partial(correlate_kernel, peers=peers, chunk=chunk),
        out_shape=jax.ShapeDtypeStruct((parts, peers, L // parts, width), jnp.bfloat16),
        in_specs=[pl.BlockSpec(memory_space=pltpu.SMEM), vmem, vmem] + [vmem] * peers,
        out_specs=vmem,
        scratch_shapes=[
            pltpu.VMEM((L, peers * width), jnp.float32),
            pltpu.VMEM((rows, peers * width), jnp.float32),
            pltpu.VMEM((rows, peers * width), jnp.float32),
            pltpu.VMEM((max(1, items // source_count), 2, peers * chan_count, bin_count), jnp.float32),
        ],
        compiler_params=pltpu.CompilerParams(vmem_limit_bytes=VMEM_LIMIT),
        name="correlate",
    )(source_channel, table, flip, *blocks)


def stack_kernel(x_ref, out_ref, y_ref):
    count, block, pairs = x_ref.shape
    for n in range(count):
        y_ref[n] = x_ref[n].astype(jnp.float32)
    mean = tree_sum([y_ref[n] for n in range(count)]) * (1.0 / count)
    squares = []
    for n in range(count):
        sample = y_ref[n] - mean
        y_ref[n] = sample
        squares.append(sample * sample)
    variance = tree_sum(squares) * (1.0 / count)
    center = jnp.zeros_like(mean)
    for iteration in range(ITERS):
        scale_two = variance + center * center + EPSILON
        inverse = 1.0 / (TUKEY * TUKEY * scale_two)
        weights, products = [], []
        for n in range(count):
            sample = y_ref[n]
            deviation = sample - center
            kept = jnp.maximum(1.0 - deviation * deviation * inverse, 0.0)
            weight = kept * kept
            weights.append(weight)
            products.append(weight * sample)
        center = tree_sum(products) / tree_sum(weights)
    out_ref[...] = (center + mean).T


def tree_sum(terms):
    sums = list(terms[:2])
    for index, term in enumerate(terms[2:]):
        sums[index % 2] = sums[index % 2] + term
    return sums[0] + sums[1]


def stack_blocks(samples, source_count):
    count, block, pairs = samples.shape
    result = pl.pallas_call(
        stack_kernel,
        out_shape=jax.ShapeDtypeStruct((pairs, block), jnp.float32),
        in_specs=[pl.BlockSpec(memory_space=pltpu.VMEM)],
        out_specs=pl.BlockSpec(memory_space=pltpu.VMEM),
        scratch_shapes=[pltpu.VMEM((count, block, pairs), jnp.float32)],
        compiler_params=pltpu.CompilerParams(vmem_limit_bytes=VMEM_LIMIT),
        name="bisquare_stack",
    )(samples)
    return result.reshape(source_count, pairs // source_count, block).transpose(2, 0, 1)


def per_device(spectra, source_channel):
    win_count, _, chan_count, bin_count = spectra.shape
    source_count = source_channel.shape[0]
    peers = lax.axis_size("rcv")
    parts = lax.axis_size("win")
    block = L // parts
    items = share(win_count, source_count, peers)
    table = make_tables(bin_count, L, L // 2 + 16)
    flip = make_flip(L // 2, 2000 * table.size)
    blocks = [spectra]
    for step in range(1, peers):
        blocks.append(lax.ppermute(spectra, "rcv", [(i, (i + step) % peers) for i in range(peers)]))
    corr = correlate(source_channel, table, flip, blocks, parts)
    corr = corr.reshape(parts * peers, block, items * chan_count)
    moved = lax.all_to_all(corr, ("win", "rcv"), split_axis=0, concat_axis=0, tiled=True)
    if items != source_count:
        moved = moved.reshape(parts * peers, block, items, chan_count).transpose(0, 2, 1, 3)
        moved = moved.reshape(parts * win_count, source_count, block, chan_count).transpose(0, 2, 1, 3)
        moved = moved.reshape(parts * win_count, block, source_count * chan_count)
    return stack_blocks(moved, source_count)


def solution(mesh):
    return jax.shard_map(
        per_device,
        mesh=mesh,
        in_specs=(P("win", None, "rcv", None), P()),
        out_specs=P("win", None, "rcv"),
        check_vma=False,
    )
```

```python
import functools

import jax
import jax.numpy as jnp
import numpy as np
from jax import lax
from jax.experimental import pallas as pl
from jax.experimental.pallas import tpu as pltpu
from jax.sharding import PartitionSpec as P

L = 512
ITERS = 5
VMEM_LIMIT = 24 * 2**20


TUKEY = 4.685
EPSILON = 1e-06


def make_tables(bin_count, lag_count, rows):
    freq = np.arange(bin_count, dtype=np.int64)
    shifts = np.arange(lag_count // 2 + 1, dtype=np.int64)
    phase = shifts[:, None] * freq[None, :] % (2 * bin_count)
    angle = phase * (2.0 * np.pi / (2 * bin_count))
    factor = np.where(freq == 0, 1.0, 2.0) / np.sqrt(8.0 * bin_count)
    table = np.zeros((2, rows, bin_count), np.float32)
    table[0, : len(shifts)] = np.cos(angle) * factor
    table[1, : len(shifts)] = -np.sin(angle) * factor
    return jnp.asarray(table.astype(jnp.bfloat16))


def flip_kernel(out_ref):
    lag = lax.broadcasted_iota(jnp.int32, out_ref.shape, 0)
    shift = lax.broadcasted_iota(jnp.int32, out_ref.shape, 1)
    out_ref[...] = (lag + shift == out_ref.shape[0]).astype(jnp.float32).astype(jnp.bfloat16)


def make_flip(half, meanwhile):
    return pl.pallas_call(
        flip_kernel,
        out_shape=jax.ShapeDtypeStruct((half, half), jnp.bfloat16),
        out_specs=pl.BlockSpec(memory_space=pltpu.VMEM),
        compiler_params=pltpu.CompilerParams(vmem_limit_bytes=VMEM_LIMIT),
        cost_estimate=pl.CostEstimate(flops=meanwhile, bytes_accessed=0, transcendentals=0),
        name="make_flip",
    )()


def share(win_count, source_count, peers):
    items = win_count * source_count // peers
    assert items * peers == win_count * source_count
    assert items % source_count == 0 or source_count % items == 0
    return items


def correlate_kernel(*refs, peers, chunk):
    channel_ref, table_ref, flip_ref = refs[:3]
    block_refs = refs[3 : 3 + peers]
    out_ref, lags_ref, even_ref, odd_ref, cross_ref, float_ref = refs[3 + peers :]
    win_count, _, chan_count, bin_count = block_refs[0].shape
    source_count = channel_ref.shape[0]
    items = share(win_count, source_count, peers)
    windows = float_ref.shape[0]
    parts, _, block, width = out_ref.shape
    half = flip_ref.shape[0]
    me = lax.axis_index("rcv")
    first = lax.div(me * items, source_count)
    rows = []
    for t in range(items):
        channel = channel_ref[lax.rem(me * items + t, source_count)]
        owner = lax.div(channel, chan_count)
        place = lax.rem(me - owner + peers, peers) * chan_count
        rows.append(place + lax.rem(channel, chan_count))
    def form_cross(bins):
        for k in range(peers):
            for w in range(windows):
                for part in range(2):
                    float_ref[w, part, k * chan_count : (k + 1) * chan_count, bins] = block_refs[k][
                        first + w, part, :, bins
                    ].astype(jnp.float32)
        for t in range(items):
            w = t // source_count
            real_p = float_ref[w, 0, :, bins]
            imag_q = float_ref[w, 1, :, bins]
            real_a = float_ref[w, 0, pl.ds(rows[t], 1), bins]
            imag_b = float_ref[w, 1, pl.ds(rows[t], 1), bins]
            real = (real_a * real_p + imag_b * imag_q).astype(jnp.bfloat16)
            imag = (imag_b * real_p - real_a * imag_q).astype(jnp.bfloat16)
            for k in range(peers):
                receivers = slice(k * chan_count, (k + 1) * chan_count)
                pairs = slice(k * width + t * chan_count, k * width + (t + 1) * chan_count)
                cross_ref[0, pairs, bins] = real[receivers]
                cross_ref[1, pairs, bins] = imag[receivers]

    def add_products(bins):
        for index, sum_ref in ((0, even_ref), (1, odd_ref)):
            term = lax.dot_general(
                table_ref[index, :, bins],
                cross_ref[index, :, bins],
                (((1,), (1,)), ((), ())),
                preferred_element_type=jnp.float32,
            )
            if bins.start == 0:
                sum_ref[...] = term
            else:
                sum_ref[...] += term

    chunks = [slice(start, start + chunk) for start in range(0, bin_count, chunk)]
    form_cross(chunks[0])
    for index, bins in enumerate(chunks):
        if index + 1 < len(chunks):
            form_cross(chunks[index + 1])
        add_products(bins)
    lags_ref[half:, :] = even_ref[:half, :] + odd_ref[:half, :]
    back = (even_ref[...] - odd_ref[...]).astype(jnp.bfloat16)
    turned = jnp.dot(flip_ref[...], back[:half], preferred_element_type=jnp.float32)
    lags_ref[:half, :] = jnp.where(
        lax.broadcasted_iota(jnp.int32, turned.shape, 0) == 0,
        back[half : half + 16].astype(jnp.float32)[:1],
        turned,
    )
    for k in range(peers):
        owner = lax.rem(me - k + peers, peers)
        for part in range(parts):
            out_ref[part, owner] = lags_ref[
                part * block : (part + 1) * block, k * width : (k + 1) * width
            ].astype(jnp.bfloat16)


def correlate(source_channel, table, flip, blocks, parts):
    win_count, _, chan_count, bin_count = blocks[0].shape
    source_count = source_channel.shape[0]
    peers = len(blocks)
    items = share(win_count, source_count, peers)
    rows = table.shape[1]
    chunk = min(512, bin_count)
    width = items * chan_count
    vmem = pl.BlockSpec(memory_space=pltpu.VMEM)
    return pl.pallas_call(
        functools.partial(correlate_kernel, peers=peers, chunk=chunk),
        out_shape=jax.ShapeDtypeStruct((parts, peers, L // parts, width), jnp.bfloat16),
        in_specs=[pl.BlockSpec(memory_space=pltpu.SMEM), vmem, vmem] + [vmem] * peers,
        out_specs=vmem,
        scratch_shapes=[
            pltpu.VMEM((L, peers * width), jnp.float32),
            pltpu.VMEM((rows, peers * width), jnp.float32),
            pltpu.VMEM((rows, peers * width), jnp.float32),
            pltpu.VMEM((2, peers * width, bin_count), jnp.bfloat16),
            pltpu.VMEM((max(1, items // source_count), 2, peers * chan_count, bin_count), jnp.float32),
        ],
        compiler_params=pltpu.CompilerParams(vmem_limit_bytes=VMEM_LIMIT),
        name="correlate",
    )(source_channel, table, flip, *blocks)


def stack_kernel(x_ref, out_ref, y_ref):
    count, block, pairs = x_ref.shape
    for n in range(count):
        y_ref[n] = x_ref[n].astype(jnp.float32)
    mean = tree_sum([y_ref[n] for n in range(count)]) * (1.0 / count)
    squares = []
    for n in range(count):
        sample = y_ref[n] - mean
        y_ref[n] = sample
        squares.append(sample * sample)
    variance = tree_sum(squares) * (1.0 / count)
    center = jnp.zeros_like(mean)
    for iteration in range(ITERS):
        limit = TUKEY * TUKEY * (variance + center * center + EPSILON)
        weights, products = [], []
        for n in range(count):
            sample = y_ref[n]
            deviation = sample - center
            kept = jnp.maximum(limit - deviation * deviation, 0.0)
            weight = kept * kept
            weights.append(weight)
            products.append(weight * sample)
        center = tree_sum(products) / tree_sum(weights)
    out_ref[...] = (center + mean).T


def tree_sum(terms):
    sums = list(terms[:2])
    for index, term in enumerate(terms[2:]):
        sums[index % 2] = sums[index % 2] + term
    return sums[0] + sums[1]


def stack_blocks(samples, source_count):
    count, block, pairs = samples.shape
    result = pl.pallas_call(
        stack_kernel,
        out_shape=jax.ShapeDtypeStruct((pairs, block), jnp.float32),
        in_specs=[pl.BlockSpec(memory_space=pltpu.VMEM)],
        out_specs=pl.BlockSpec(memory_space=pltpu.VMEM),
        scratch_shapes=[pltpu.VMEM((count, block, pairs), jnp.float32)],
        compiler_params=pltpu.CompilerParams(vmem_limit_bytes=VMEM_LIMIT),
        name="bisquare_stack",
    )(samples)
    return result.reshape(source_count, pairs // source_count, block).transpose(2, 0, 1)


def per_device(spectra, source_channel):
    win_count, _, chan_count, bin_count = spectra.shape
    source_count = source_channel.shape[0]
    peers = lax.axis_size("rcv")
    parts = lax.axis_size("win")
    block = L // parts
    items = share(win_count, source_count, peers)
    table = make_tables(bin_count, L, L // 2 + 16)
    flip = make_flip(L // 2, 2000 * table.size)
    blocks = [spectra]
    for step in range(1, peers):
        blocks.append(lax.ppermute(spectra, "rcv", [(i, (i + step) % peers) for i in range(peers)]))
    corr = correlate(source_channel, table, flip, blocks, parts)
    corr = corr.reshape(parts * peers, block, items * chan_count)
    moved = lax.all_to_all(corr, ("win", "rcv"), split_axis=0, concat_axis=0, tiled=True)
    if items != source_count:
        moved = moved.reshape(parts * peers, block, items, chan_count).transpose(0, 2, 1, 3)
        moved = moved.reshape(parts * win_count, source_count, block, chan_count).transpose(0, 2, 1, 3)
        moved = moved.reshape(parts * win_count, block, source_count * chan_count)
    return stack_blocks(moved, source_count)


def solution(mesh):
    return jax.shard_map(
        per_device,
        mesh=mesh,
        in_specs=(P("win", None, "rcv", None), P()),
        out_specs=P("win", None, "rcv"),
        check_vma=False,
    )
```

```python
import functools

import jax
import jax.numpy as jnp
import numpy as np
from jax import lax
from jax.experimental import pallas as pl
from jax.experimental.pallas import tpu as pltpu
from jax.sharding import PartitionSpec as P

L = 512
ITERS = 5
VMEM_LIMIT = 24 * 2**20


TUKEY = 4.685
EPSILON = 1e-06


def make_tables(bin_count, lag_count):
    freq = np.arange(bin_count, dtype=np.int64)
    shifts = np.arange(lag_count // 2, dtype=np.int64) + 1
    phase = freq[:, None] * shifts[None, :] % (2 * bin_count)
    angle = phase * (2.0 * np.pi / (2 * bin_count))
    factor = np.where(freq == 0, 1.0, 2.0)[:, None] / np.sqrt(8.0 * bin_count)
    table = np.stack([np.cos(angle) * factor, -np.sin(angle) * factor])
    return jnp.asarray(table.astype(np.float32).astype(jnp.bfloat16))


def level_at_zero(bin_count):
    return float(np.float32(2.0 / np.sqrt(8.0 * bin_count)).astype(jnp.bfloat16))


def order_kernel(out_ref):
    half = out_ref.shape[1]
    lag = lax.broadcasted_iota(jnp.int32, (half, half), 0)
    column = lax.broadcasted_iota(jnp.int32, (half, half), 1)
    behind = lag + column == half - 1
    ahead = lag == jnp.where(column == half - 1, 0, column + 1)
    out_ref[0] = behind.astype(jnp.float32).astype(jnp.bfloat16)
    out_ref[1] = ahead.astype(jnp.float32).astype(jnp.bfloat16)


def make_order(half, meanwhile):
    return pl.pallas_call(
        order_kernel,
        out_shape=jax.ShapeDtypeStruct((2, half, half), jnp.bfloat16),
        out_specs=pl.BlockSpec(memory_space=pltpu.VMEM),
        compiler_params=pltpu.CompilerParams(vmem_limit_bytes=VMEM_LIMIT),
        cost_estimate=pl.CostEstimate(flops=meanwhile, bytes_accessed=0, transcendentals=0),
        name="make_order",
    )()


def share(win_count, source_count, peers):
    items = win_count * source_count // peers
    assert items * peers == win_count * source_count
    assert items % source_count == 0 or source_count % items == 0
    return items


def correlate_kernel(*refs, peers, chunk):
    channel_ref, table_ref, order_ref = refs[:3]
    block_refs = refs[3 : 3 + peers]
    out_ref, lags_ref, even_ref, odd_ref, zero_ref, cross_ref, float_ref = refs[3 + peers :]
    win_count, _, chan_count, bin_count = block_refs[0].shape
    source_count = channel_ref.shape[0]
    items = share(win_count, source_count, peers)
    windows = float_ref.shape[0]
    parts, _, block, width = out_ref.shape
    half = order_ref.shape[1]
    me = lax.axis_index("rcv")
    first = lax.div(me * items, source_count)
    rows = []
    for t in range(items):
        channel = channel_ref[lax.rem(me * items + t, source_count)]
        owner = lax.div(channel, chan_count)
        place = lax.rem(me - owner + peers, peers) * chan_count
        rows.append(place + lax.rem(channel, chan_count))
    def form_cross(bins):
        for k in range(peers):
            for w in range(windows):
                for part in range(2):
                    float_ref[w, part, k * chan_count : (k + 1) * chan_count, bins] = block_refs[k][
                        first + w, part, :, bins
                    ].astype(jnp.float32)
        for t in range(items):
            w = t // source_count
            real_p = float_ref[w, 0, :, bins]
            imag_q = float_ref[w, 1, :, bins]
            real_a = float_ref[w, 0, pl.ds(rows[t], 1), bins]
            imag_b = float_ref[w, 1, pl.ds(rows[t], 1), bins]
            real = (real_a * real_p + imag_b * imag_q).astype(jnp.bfloat16)
            imag = (imag_b * real_p - real_a * imag_q).astype(jnp.bfloat16)
            for k in range(peers):
                receivers = slice(k * chan_count, (k + 1) * chan_count)
                pairs = slice(k * width + t * chan_count, k * width + (t + 1) * chan_count)
                cross_ref[0, pairs, bins] = real[receivers]
                cross_ref[1, pairs, bins] = imag[receivers]
                level = sum_lanes(real[receivers].astype(jnp.float32))
                if bins.start == 0:
                    zero_ref[pairs, :] = level
                else:
                    zero_ref[pairs, :] += level

    def add_products(bins):
        for index, sum_ref in ((0, even_ref), (1, odd_ref)):
            term = jnp.dot(
                cross_ref[index, :, bins], table_ref[index, bins, :], preferred_element_type=jnp.float32
            )
            if bins.start == 0:
                sum_ref[...] = term
            else:
                sum_ref[...] += term

    chunks = [slice(start, start + chunk) for start in range(0, bin_count, chunk)]
    form_cross(chunks[0])
    for index, bins in enumerate(chunks):
        if index + 1 < len(chunks):
            form_cross(chunks[index + 1])
        add_products(bins)
    first_bin = cross_ref[0, :, :128].astype(jnp.float32)[:, :1]
    level = jnp.sum(zero_ref[...], axis=1, keepdims=True) - 0.5 * first_bin
    at_zero = level * level_at_zero(bin_count)
    column = lax.broadcasted_iota(jnp.int32, even_ref.shape, 1)
    ahead = jnp.where(column == half - 1, at_zero, even_ref[...] + odd_ref[...])
    for index, side in ((0, even_ref[...] - odd_ref[...]), (1, ahead)):
        lags_ref[index * half : (index + 1) * half, :] = lax.dot_general(
            order_ref[index],
            side.astype(jnp.bfloat16),
            (((1,), (1,)), ((), ())),
            preferred_element_type=jnp.float32,
        )
    for k in range(peers):
        owner = lax.rem(me - k + peers, peers)
        for part in range(parts):
            out_ref[part, owner] = lags_ref[
                part * block : (part + 1) * block, k * width : (k + 1) * width
            ].astype(jnp.bfloat16)


def sum_lanes(values):
    tiles = [values[:, start : start + 128] for start in range(0, values.shape[1], 128)]
    return tree_sum(tiles)


def correlate(source_channel, table, order, blocks, parts):
    win_count, _, chan_count, bin_count = blocks[0].shape
    source_count = source_channel.shape[0]
    peers = len(blocks)
    items = share(win_count, source_count, peers)
    half = table.shape[2]
    chunk = min(512, bin_count)
    width = items * chan_count
    vmem = pl.BlockSpec(memory_space=pltpu.VMEM)
    return pl.pallas_call(
        functools.partial(correlate_kernel, peers=peers, chunk=chunk),
        out_shape=jax.ShapeDtypeStruct((parts, peers, L // parts, width), jnp.bfloat16),
        in_specs=[pl.BlockSpec(memory_space=pltpu.SMEM), vmem, vmem] + [vmem] * peers,
        out_specs=vmem,
        scratch_shapes=[
            pltpu.VMEM((L, peers * width), jnp.float32),
            pltpu.VMEM((peers * width, half), jnp.float32),
            pltpu.VMEM((peers * width, half), jnp.float32),
            pltpu.VMEM((peers * width, 128), jnp.float32),
            pltpu.VMEM((2, peers * width, bin_count), jnp.bfloat16),
            pltpu.VMEM((max(1, items // source_count), 2, peers * chan_count, bin_count), jnp.float32),
        ],
        compiler_params=pltpu.CompilerParams(vmem_limit_bytes=VMEM_LIMIT),
        name="correlate",
    )(source_channel, table, order, *blocks)


def stack_kernel(x_ref, out_ref, y_ref):
    count, block, pairs = x_ref.shape
    for n in range(count):
        y_ref[n] = x_ref[n].astype(jnp.float32)
    mean = tree_sum([y_ref[n] for n in range(count)]) * (1.0 / count)
    squares = []
    for n in range(count):
        sample = y_ref[n] - mean
        y_ref[n] = sample
        squares.append(sample * sample)
    variance = tree_sum(squares) * (1.0 / count)
    center = jnp.zeros_like(mean)
    for iteration in range(ITERS):
        limit = TUKEY * TUKEY * (variance + center * center + EPSILON)
        weights, products = [], []
        for n in range(count):
            sample = y_ref[n]
            deviation = sample - center
            kept = jnp.maximum(limit - deviation * deviation, 0.0)
            weight = kept * kept
            weights.append(weight)
            products.append(weight * sample)
        center = tree_sum(products) / tree_sum(weights)
    out_ref[...] = (center + mean).T


def tree_sum(terms):
    sums = list(terms[:2])
    for index, term in enumerate(terms[2:]):
        sums[index % 2] = sums[index % 2] + term
    return sums[0] + sums[1]


def stack_blocks(samples, source_count):
    count, block, pairs = samples.shape
    result = pl.pallas_call(
        stack_kernel,
        out_shape=jax.ShapeDtypeStruct((pairs, block), jnp.float32),
        in_specs=[pl.BlockSpec(memory_space=pltpu.VMEM)],
        out_specs=pl.BlockSpec(memory_space=pltpu.VMEM),
        scratch_shapes=[pltpu.VMEM((count, block, pairs), jnp.float32)],
        compiler_params=pltpu.CompilerParams(vmem_limit_bytes=VMEM_LIMIT),
        name="bisquare_stack",
    )(samples)
    return result.reshape(source_count, pairs // source_count, block).transpose(2, 0, 1)


def per_device(spectra, source_channel):
    win_count, _, chan_count, bin_count = spectra.shape
    source_count = source_channel.shape[0]
    peers = lax.axis_size("rcv")
    parts = lax.axis_size("win")
    block = L // parts
    items = share(win_count, source_count, peers)
    table = make_tables(bin_count, L)
    order = make_order(L // 2, 2000 * table.size)
    blocks = [spectra]
    for step in range(1, peers):
        blocks.append(lax.ppermute(spectra, "rcv", [(i, (i + step) % peers) for i in range(peers)]))
    corr = correlate(source_channel, table, order, blocks, parts)
    corr = corr.reshape(parts * peers, block, items * chan_count)
    moved = lax.all_to_all(corr, ("win", "rcv"), split_axis=0, concat_axis=0, tiled=True)
    if items != source_count:
        moved = moved.reshape(parts * peers, block, items, chan_count).transpose(0, 2, 1, 3)
        moved = moved.reshape(parts * win_count, source_count, block, chan_count).transpose(0, 2, 1, 3)
        moved = moved.reshape(parts * win_count, block, source_count * chan_count)
    return stack_blocks(moved, source_count)


def solution(mesh):
    return jax.shard_map(
        per_device,
        mesh=mesh,
        in_specs=(P("win", None, "rcv", None), P()),
        out_specs=P("win", None, "rcv"),
        check_vma=False,
    )
```

```python
import functools

import jax
import jax.numpy as jnp
import numpy as np
from jax import lax
from jax.experimental import pallas as pl
from jax.experimental.pallas import tpu as pltpu
from jax.sharding import PartitionSpec as P

L = 512
ITERS = 5
VMEM_LIMIT = 24 * 2**20


TUKEY = 4.685
EPSILON = 1e-06


def make_tables(bin_count, lag_count, rows):
    freq = np.arange(bin_count, dtype=np.int64)
    shifts = np.arange(lag_count // 2 + 1, dtype=np.int64)
    phase = shifts[:, None] * freq[None, :] % (2 * bin_count)
    angle = phase * (2.0 * np.pi / (2 * bin_count))
    factor = np.where(freq == 0, 1.0, 2.0) / np.sqrt(8.0 * bin_count)
    table = np.zeros((2, rows, bin_count), np.float32)
    table[0, : len(shifts)] = np.cos(angle) * factor
    table[1, : len(shifts)] = -np.sin(angle) * factor
    return jnp.asarray(table.astype(jnp.bfloat16))


def flip_kernel(out_ref):
    lag = lax.broadcasted_iota(jnp.int32, out_ref.shape, 0)
    shift = lax.broadcasted_iota(jnp.int32, out_ref.shape, 1)
    out_ref[...] = (lag + shift == out_ref.shape[0]).astype(jnp.float32).astype(jnp.bfloat16)


def make_flip(half, meanwhile):
    return pl.pallas_call(
        flip_kernel,
        out_shape=jax.ShapeDtypeStruct((half, half), jnp.bfloat16),
        out_specs=pl.BlockSpec(memory_space=pltpu.VMEM),
        compiler_params=pltpu.CompilerParams(vmem_limit_bytes=VMEM_LIMIT),
        cost_estimate=pl.CostEstimate(flops=meanwhile, bytes_accessed=0, transcendentals=0),
        name="make_flip",
    )()


def share(win_count, source_count, peers):
    items = win_count * source_count // peers
    assert items * peers == win_count * source_count
    assert items % source_count == 0 or source_count % items == 0
    return items


def correlate_kernel(*refs, peers, chunk, piece):
    channel_ref, table_ref, flip_ref = refs[:3]
    block_refs = refs[3 : 3 + peers]
    out_ref, lags_ref, even_ref, odd_ref, cross_ref, float_ref = refs[3 + peers :]
    win_count, _, chan_count, bin_count = block_refs[0].shape
    source_count = channel_ref.shape[0]
    items = share(win_count, source_count, peers)
    windows = float_ref.shape[0]
    parts, _, block, width = out_ref.shape
    half = flip_ref.shape[0]
    me = lax.axis_index("rcv")
    first = lax.div(me * items, source_count)
    rows = []
    for t in range(items):
        channel = channel_ref[lax.rem(me * items + t, source_count)]
        owner = lax.div(channel, chan_count)
        place = lax.rem(me - owner + peers, peers) * chan_count
        rows.append(place + lax.rem(channel, chan_count))
    def form_cross(bins):
        for w in range(windows):
            sides = []
            for part in range(2):
                pieces = [block_refs[k][first + w, part, :, bins] for k in range(peers)]
                side = jnp.concatenate(pieces, axis=0).astype(jnp.float32)
                float_ref[w, part, :, bins] = side
                sides.append(side)
            real_p, imag_q = sides
            for t in range(w * source_count, min(items, (w + 1) * source_count)):
                real_a = float_ref[w, 0, pl.ds(rows[t], 1), bins]
                imag_b = float_ref[w, 1, pl.ds(rows[t], 1), bins]
                real = (real_a * real_p + imag_b * imag_q).astype(jnp.bfloat16)
                imag = (imag_b * real_p - real_a * imag_q).astype(jnp.bfloat16)
                for k in range(peers):
                    receivers = slice(k * chan_count, (k + 1) * chan_count)
                    pairs = slice(k * width + t * chan_count, k * width + (t + 1) * chan_count)
                    cross_ref[0, pairs, bins] = real[receivers]
                    cross_ref[1, pairs, bins] = imag[receivers]

    def add_products(bins):
        for index, sum_ref in ((0, even_ref), (1, odd_ref)):
            term = lax.dot_general(
                table_ref[index, :, bins],
                cross_ref[index, :, bins],
                (((1,), (1,)), ((), ())),
                preferred_element_type=jnp.float32,
            )
            if bins.start == 0:
                sum_ref[...] = term
            else:
                sum_ref[...] += term

    chunks = [slice(start, start + chunk) for start in range(0, bin_count, chunk)]
    for index in range(len(chunks) + 1):
        if index < len(chunks):
            for start in range(chunks[index].start, chunks[index].stop, piece):
                form_cross(slice(start, start + piece))
        if index > 0:
            add_products(chunks[index - 1])
    lags_ref[half:, :] = even_ref[:half, :] + odd_ref[:half, :]
    back = (even_ref[...] - odd_ref[...]).astype(jnp.bfloat16)
    turned = jnp.dot(flip_ref[...], back[:half], preferred_element_type=jnp.float32)
    lags_ref[:half, :] = jnp.where(
        lax.broadcasted_iota(jnp.int32, turned.shape, 0) == 0,
        back[half : half + 16].astype(jnp.float32)[:1],
        turned,
    )
    for k in range(peers):
        owner = lax.rem(me - k + peers, peers)
        for part in range(parts):
            out_ref[part, owner] = lags_ref[
                part * block : (part + 1) * block, k * width : (k + 1) * width
            ].astype(jnp.bfloat16)


def correlate(source_channel, table, flip, blocks, parts):
    win_count, _, chan_count, bin_count = blocks[0].shape
    source_count = source_channel.shape[0]
    peers = len(blocks)
    items = share(win_count, source_count, peers)
    rows = table.shape[1]
    chunk = min(1024, bin_count)
    width = items * chan_count
    vmem = pl.BlockSpec(memory_space=pltpu.VMEM)
    return pl.pallas_call(
        functools.partial(correlate_kernel, peers=peers, chunk=chunk, piece=min(256, chunk)),
        out_shape=jax.ShapeDtypeStruct((parts, peers, L // parts, width), jnp.bfloat16),
        in_specs=[pl.BlockSpec(memory_space=pltpu.SMEM), vmem, vmem] + [vmem] * peers,
        out_specs=vmem,
        scratch_shapes=[
            pltpu.VMEM((L, peers * width), jnp.float32),
            pltpu.VMEM((rows, peers * width), jnp.float32),
            pltpu.VMEM((rows, peers * width), jnp.float32),
            pltpu.VMEM((2, peers * width, bin_count), jnp.bfloat16),
            pltpu.VMEM((max(1, items // source_count), 2, peers * chan_count, bin_count), jnp.float32),
        ],
        compiler_params=pltpu.CompilerParams(vmem_limit_bytes=VMEM_LIMIT),
        name="correlate",
    )(source_channel, table, flip, *blocks)


def stack_kernel(x_ref, out_ref, y_ref):
    count, block, pairs = x_ref.shape
    for n in range(count):
        y_ref[n] = x_ref[n].astype(jnp.float32)
    mean = tree_sum([y_ref[n] for n in range(count)]) * (1.0 / count)
    squares = []
    for n in range(count):
        sample = y_ref[n] - mean
        y_ref[n] = sample
        squares.append(sample * sample)
    variance = tree_sum(squares) * (1.0 / count)
    center = jnp.zeros_like(mean)
    for iteration in range(ITERS):
        limit = TUKEY * TUKEY * (variance + center * center + EPSILON)
        weights, products = [], []
        for n in range(count):
            sample = y_ref[n]
            deviation = sample - center
            kept = jnp.maximum(limit - deviation * deviation, 0.0)
            weight = kept * kept
            weights.append(weight)
            products.append(weight * sample)
        center = tree_sum(products) / tree_sum(weights)
    out_ref[...] = (center + mean).T


def tree_sum(terms):
    sums = list(terms[:2])
    for index, term in enumerate(terms[2:]):
        sums[index % 2] = sums[index % 2] + term
    return sums[0] + sums[1]


def stack_blocks(samples, source_count):
    count, block, pairs = samples.shape
    result = pl.pallas_call(
        stack_kernel,
        out_shape=jax.ShapeDtypeStruct((pairs, block), jnp.float32),
        in_specs=[pl.BlockSpec(memory_space=pltpu.VMEM)],
        out_specs=pl.BlockSpec(memory_space=pltpu.VMEM),
        scratch_shapes=[pltpu.VMEM((count, block, pairs), jnp.float32)],
        compiler_params=pltpu.CompilerParams(vmem_limit_bytes=VMEM_LIMIT),
        name="bisquare_stack",
    )(samples)
    return result.reshape(source_count, pairs // source_count, block).transpose(2, 0, 1)


def per_device(spectra, source_channel):
    win_count, _, chan_count, bin_count = spectra.shape
    source_count = source_channel.shape[0]
    peers = lax.axis_size("rcv")
    parts = lax.axis_size("win")
    block = L // parts
    items = share(win_count, source_count, peers)
    table = make_tables(bin_count, L, L // 2 + 16)
    flip = make_flip(L // 2, 2000 * table.size)
    blocks = [spectra]
    for step in range(1, peers):
        blocks.append(lax.ppermute(spectra, "rcv", [(i, (i + step) % peers) for i in range(peers)]))
    corr = correlate(source_channel, table, flip, blocks, parts)
    corr = corr.reshape(parts * peers, block, items * chan_count)
    moved = lax.all_to_all(corr, ("win", "rcv"), split_axis=0, concat_axis=0, tiled=True)
    if items != source_count:
        moved = moved.reshape(parts * peers, block, items, chan_count).transpose(0, 2, 1, 3)
        moved = moved.reshape(parts * win_count, source_count, block, chan_count).transpose(0, 2, 1, 3)
        moved = moved.reshape(parts * win_count, block, source_count * chan_count)
    return stack_blocks(moved, source_count)


def solution(mesh):
    return jax.shard_map(
        per_device,
        mesh=mesh,
        in_specs=(P("win", None, "rcv", None), P()),
        out_specs=P("win", None, "rcv"),
        check_vma=False,
    )
```

```python
import functools

import jax
import jax.numpy as jnp
import numpy as np
from jax import lax
from jax.experimental import pallas as pl
from jax.experimental.pallas import tpu as pltpu
from jax.sharding import PartitionSpec as P

L = 512
ITERS = 5
VMEM_LIMIT = 24 * 2**20


TUKEY = 4.685
EPSILON = 1e-06


def make_tables(bin_count, lag_count, rows):
    freq = np.arange(bin_count, dtype=np.int64)
    shifts = np.arange(lag_count // 2 + 1, dtype=np.int64)
    phase = shifts[:, None] * freq[None, :] % (2 * bin_count)
    angle = phase * (2.0 * np.pi / (2 * bin_count))
    factor = np.where(freq == 0, 1.0, 2.0) / np.sqrt(8.0 * bin_count)
    table = np.zeros((2, rows, bin_count), np.float32)
    table[0, : len(shifts)] = np.cos(angle) * factor
    table[1, : len(shifts)] = -np.sin(angle) * factor
    return jnp.asarray(table.astype(jnp.bfloat16))


def flip_kernel(out_ref):
    lag = lax.broadcasted_iota(jnp.int32, out_ref.shape, 0)
    shift = lax.broadcasted_iota(jnp.int32, out_ref.shape, 1)
    out_ref[...] = (lag + shift == out_ref.shape[0]).astype(jnp.float32).astype(jnp.bfloat16)


def make_flip(half, meanwhile):
    return pl.pallas_call(
        flip_kernel,
        out_shape=jax.ShapeDtypeStruct((half, half), jnp.bfloat16),
        out_specs=pl.BlockSpec(memory_space=pltpu.VMEM),
        compiler_params=pltpu.CompilerParams(vmem_limit_bytes=VMEM_LIMIT),
        cost_estimate=pl.CostEstimate(flops=meanwhile, bytes_accessed=0, transcendentals=0),
        name="make_flip",
    )()


def share(win_count, source_count, peers):
    items = win_count * source_count // peers
    assert items * peers == win_count * source_count
    assert items % source_count == 0 or source_count % items == 0
    return items


def correlate_kernel(*refs, peers, chunk):
    channel_ref, table_ref, flip_ref = refs[:3]
    block_refs = refs[3 : 3 + peers]
    out_ref, lags_ref, even_ref, odd_ref, cross_ref, float_ref = refs[3 + peers :]
    win_count, _, chan_count, bin_count = block_refs[0].shape
    source_count = channel_ref.shape[0]
    items = share(win_count, source_count, peers)
    windows = float_ref.shape[0]
    parts, _, block, width = out_ref.shape
    half = flip_ref.shape[0]
    me = lax.axis_index("rcv")
    first = lax.div(me * items, source_count)
    rows = []
    for t in range(items):
        channel = channel_ref[lax.rem(me * items + t, source_count)]
        owner = lax.div(channel, chan_count)
        place = lax.rem(me - owner + peers, peers) * chan_count
        rows.append(place + lax.rem(channel, chan_count))
    def widen(bins):
        for k in range(peers):
            for w in range(windows):
                for part in range(2):
                    float_ref[w, part, k * chan_count : (k + 1) * chan_count, bins] = block_refs[k][
                        first + w, part, :, bins
                    ].astype(jnp.float32)

    def form_cross(bins, some):
        for t in some:
            w = t // source_count
            real_p = float_ref[w, 0, :, bins]
            imag_q = float_ref[w, 1, :, bins]
            real_a = float_ref[w, 0, pl.ds(rows[t], 1), bins]
            imag_b = float_ref[w, 1, pl.ds(rows[t], 1), bins]
            real = (real_a * real_p + imag_b * imag_q).astype(jnp.bfloat16)
            imag = (imag_b * real_p - real_a * imag_q).astype(jnp.bfloat16)
            for k in range(peers):
                receivers = slice(k * chan_count, (k + 1) * chan_count)
                pairs = slice(k * width + t * chan_count, k * width + (t + 1) * chan_count)
                cross_ref[0, pairs, bins] = real[receivers]
                cross_ref[1, pairs, bins] = imag[receivers]

    def add_product(bins, index, sum_ref):
        term = lax.dot_general(
            table_ref[index, :, bins],
            cross_ref[index, :, bins],
            (((1,), (1,)), ((), ())),
            preferred_element_type=jnp.float32,
        )
        if bins.start == 0:
            sum_ref[...] = term
        else:
            sum_ref[...] += term

    chunks = [slice(start, start + chunk) for start in range(0, bin_count, chunk)]
    for index in range(len(chunks) + 1):
        if index < len(chunks):
            widen(chunks[index])
            form_cross(chunks[index], range(items // 2))
        if index > 0:
            add_product(chunks[index - 1], 0, even_ref)
        if index < len(chunks):
            form_cross(chunks[index], range(items // 2, items))
        if index > 0:
            add_product(chunks[index - 1], 1, odd_ref)
    lags_ref[half:, :] = even_ref[:half, :] + odd_ref[:half, :]
    back = (even_ref[...] - odd_ref[...]).astype(jnp.bfloat16)
    turned = jnp.dot(flip_ref[...], back[:half], preferred_element_type=jnp.float32)
    lags_ref[:half, :] = jnp.where(
        lax.broadcasted_iota(jnp.int32, turned.shape, 0) == 0,
        back[half : half + 16].astype(jnp.float32)[:1],
        turned,
    )
    for k in range(peers):
        owner = lax.rem(me - k + peers, peers)
        for part in range(parts):
            out_ref[part, owner] = lags_ref[
                part * block : (part + 1) * block, k * width : (k + 1) * width
            ].astype(jnp.bfloat16)


def correlate(source_channel, table, flip, blocks, parts):
    win_count, _, chan_count, bin_count = blocks[0].shape
    source_count = source_channel.shape[0]
    peers = len(blocks)
    items = share(win_count, source_count, peers)
    rows = table.shape[1]
    chunk = min(256, bin_count)
    width = items * chan_count
    vmem = pl.BlockSpec(memory_space=pltpu.VMEM)
    return pl.pallas_call(
        functools.partial(correlate_kernel, peers=peers, chunk=chunk),
        out_shape=jax.ShapeDtypeStruct((parts, peers, L // parts, width), jnp.bfloat16),
        in_specs=[pl.BlockSpec(memory_space=pltpu.SMEM), vmem, vmem] + [vmem] * peers,
        out_specs=vmem,
        scratch_shapes=[
            pltpu.VMEM((L, peers * width), jnp.float32),
            pltpu.VMEM((rows, peers * width), jnp.float32),
            pltpu.VMEM((rows, peers * width), jnp.float32),
            pltpu.VMEM((2, peers * width, bin_count), jnp.bfloat16),
            pltpu.VMEM((max(1, items // source_count), 2, peers * chan_count, bin_count), jnp.float32),
        ],
        compiler_params=pltpu.CompilerParams(vmem_limit_bytes=VMEM_LIMIT),
        name="correlate",
    )(source_channel, table, flip, *blocks)


def stack_kernel(x_ref, out_ref, y_ref):
    count, block, pairs = x_ref.shape
    for n in range(count):
        y_ref[n] = x_ref[n].astype(jnp.float32)
    mean = tree_sum([y_ref[n] for n in range(count)]) * (1.0 / count)
    squares = []
    for n in range(count):
        sample = y_ref[n] - mean
        y_ref[n] = sample
        squares.append(sample * sample)
    variance = tree_sum(squares) * (1.0 / count)
    center = jnp.zeros_like(mean)
    for iteration in range(ITERS):
        limit = TUKEY * TUKEY * (variance + center * center + EPSILON)
        weights, products = [], []
        for n in range(count):
            sample = y_ref[n]
            deviation = sample - center
            kept = jnp.maximum(limit - deviation * deviation, 0.0)
            weight = kept * kept
            weights.append(weight)
            products.append(weight * sample)
        center = tree_sum(products) / tree_sum(weights)
    out_ref[...] = (center + mean).T


def tree_sum(terms):
    sums = list(terms[:2])
    for index, term in enumerate(terms[2:]):
        sums[index % 2] = sums[index % 2] + term
    return sums[0] + sums[1]


def stack_blocks(samples, source_count):
    count, block, pairs = samples.shape
    result = pl.pallas_call(
        stack_kernel,
        out_shape=jax.ShapeDtypeStruct((pairs, block), jnp.float32),
        in_specs=[pl.BlockSpec(memory_space=pltpu.VMEM)],
        out_specs=pl.BlockSpec(memory_space=pltpu.VMEM),
        scratch_shapes=[pltpu.VMEM((count, block, pairs), jnp.float32)],
        compiler_params=pltpu.CompilerParams(vmem_limit_bytes=VMEM_LIMIT),
        name="bisquare_stack",
    )(samples)
    return result.reshape(source_count, pairs // source_count, block).transpose(2, 0, 1)


def per_device(spectra, source_channel):
    win_count, _, chan_count, bin_count = spectra.shape
    source_count = source_channel.shape[0]
    peers = lax.axis_size("rcv")
    parts = lax.axis_size("win")
    block = L // parts
    items = share(win_count, source_count, peers)
    table = make_tables(bin_count, L, L // 2 + 16)
    flip = make_flip(L // 2, 2000 * table.size)
    blocks = [spectra]
    for step in range(1, peers):
        blocks.append(lax.ppermute(spectra, "rcv", [(i, (i + step) % peers) for i in range(peers)]))
    corr = correlate(source_channel, table, flip, blocks, parts)
    corr = corr.reshape(parts * peers, block, items * chan_count)
    moved = lax.all_to_all(corr, ("win", "rcv"), split_axis=0, concat_axis=0, tiled=True)
    if items != source_count:
        moved = moved.reshape(parts * peers, block, items, chan_count).transpose(0, 2, 1, 3)
        moved = moved.reshape(parts * win_count, source_count, block, chan_count).transpose(0, 2, 1, 3)
        moved = moved.reshape(parts * win_count, block, source_count * chan_count)
    return stack_blocks(moved, source_count)


def solution(mesh):
    return jax.shard_map(
        per_device,
        mesh=mesh,
        in_specs=(P("win", None, "rcv", None), P()),
        out_specs=P("win", None, "rcv"),
        check_vma=False,
    )
```

```python
import functools

import jax
import jax.numpy as jnp
import numpy as np
from jax import lax
from jax.experimental import pallas as pl
from jax.experimental.pallas import tpu as pltpu
from jax.sharding import PartitionSpec as P

L = 512
ITERS = 5
VMEM_LIMIT = 24 * 2**20


TUKEY = 4.685
EPSILON = 1e-06


def make_tables(bin_count, lag_count, rows):
    freq = np.arange(bin_count, dtype=np.int64)
    shifts = np.arange(lag_count // 2 + 1, dtype=np.int64)
    phase = shifts[:, None] * freq[None, :] % (2 * bin_count)
    angle = phase * (2.0 * np.pi / (2 * bin_count))
    factor = np.where(freq == 0, 1.0, 2.0) / np.sqrt(8.0 * bin_count)
    table = np.zeros((2, rows, bin_count), np.float32)
    table[0, : len(shifts)] = np.cos(angle) * factor
    table[1, : len(shifts)] = -np.sin(angle) * factor
    return jnp.asarray(table.astype(jnp.bfloat16))


def share(win_count, source_count, peers):
    items = win_count * source_count // peers
    assert items * peers == win_count * source_count
    assert items % source_count == 0 or source_count % items == 0
    return items


def correlate_kernel(
    channel_ref, table_ref, block_ref, out_ref, lags_ref, even_ref, odd_ref, cross_ref, float_ref, *, chunk, items
):
    peers, held, _, chan_count, bin_count = block_ref.shape
    source_count = channel_ref.shape[0]
    windows = float_ref.shape[0]
    parts, _, block, width = out_ref.shape
    half = lags_ref.shape[0] // 2
    if held == windows and items % source_count == 0:
        first, rows = 0, [channel_ref[t % source_count] for t in range(items)]
    else:
        start = lax.axis_index("rcv") * items
        first = lax.div(start, source_count)
        rows = [channel_ref[lax.rem(start + t, source_count)] for t in range(items)]

    def widen(bins):
        for k in range(peers):
            for w in range(windows):
                for part in range(2):
                    float_ref[w, part, k * chan_count : (k + 1) * chan_count, bins] = block_ref[
                        k, first + w, part, :, bins
                    ].astype(jnp.float32)

    def form_cross(bins, some):
        for t in some:
            w = t // source_count
            real_p = float_ref[w, 0, :, bins]
            imag_q = float_ref[w, 1, :, bins]
            real_a = float_ref[w, 0, pl.ds(rows[t], 1), bins]
            imag_b = float_ref[w, 1, pl.ds(rows[t], 1), bins]
            real = (real_a * real_p + imag_b * imag_q).astype(jnp.bfloat16)
            imag = (imag_b * real_p - real_a * imag_q).astype(jnp.bfloat16)
            for k in range(peers):
                receivers = slice(k * chan_count, (k + 1) * chan_count)
                pairs = slice(k * width + t * chan_count, k * width + (t + 1) * chan_count)
                cross_ref[0, pairs, bins] = real[receivers]
                cross_ref[1, pairs, bins] = imag[receivers]

    def add_product(bins, index, sum_ref):
        term = lax.dot_general(
            table_ref[index, :, bins],
            cross_ref[index, :, bins],
            (((1,), (1,)), ((), ())),
            preferred_element_type=jnp.float32,
        )
        if bins.start == 0:
            sum_ref[...] = term
        else:
            sum_ref[...] += term

    chunks = [slice(start, start + chunk) for start in range(0, bin_count, chunk)]
    for index in range(len(chunks) + 1):
        if index < len(chunks):
            widen(chunks[index])
            form_cross(chunks[index], range(items // 2))
        if index > 0:
            add_product(chunks[index - 1], 0, even_ref)
        if index < len(chunks):
            form_cross(chunks[index], range(items // 2, items))
        if index > 0:
            add_product(chunks[index - 1], 1, odd_ref)
    lags_ref[half:, :] = even_ref[:half, :] + odd_ref[:half, :]
    back = (even_ref[...] - odd_ref[...]).astype(jnp.bfloat16)
    lag = lax.broadcasted_iota(jnp.int32, (half, half), 0)
    column = lax.broadcasted_iota(jnp.int32, (half, half), 1)
    flip = (lag + column == half).astype(jnp.float32).astype(jnp.bfloat16)
    turned = jnp.dot(flip, back[:half], preferred_element_type=jnp.float32)
    lags_ref[:half, :] = jnp.where(
        lax.broadcasted_iota(jnp.int32, turned.shape, 0) == 0,
        back[half : half + 16].astype(jnp.float32)[:1],
        turned,
    )
    for k in range(peers):
        for part in range(parts):
            out_ref[part, k] = lags_ref[
                part * block : (part + 1) * block, k * width : (k + 1) * width
            ].astype(jnp.bfloat16)


def correlate(source_channel, table, blocks, parts, items):
    peers, _, _, chan_count, bin_count = blocks.shape
    source_count = source_channel.shape[0]
    rows = table.shape[1]
    chunk = min(256, bin_count)
    width = items * chan_count
    vmem = pl.BlockSpec(memory_space=pltpu.VMEM)
    return pl.pallas_call(
        functools.partial(correlate_kernel, chunk=chunk, items=items),
        out_shape=jax.ShapeDtypeStruct((parts, peers, L // parts, width), jnp.bfloat16),
        in_specs=[pl.BlockSpec(memory_space=pltpu.SMEM), vmem, vmem],
        out_specs=vmem,
        scratch_shapes=[
            pltpu.VMEM((L, peers * width), jnp.float32),
            pltpu.VMEM((rows, peers * width), jnp.float32),
            pltpu.VMEM((rows, peers * width), jnp.float32),
            pltpu.VMEM((2, peers * width, bin_count), jnp.bfloat16),
            pltpu.VMEM((max(1, items // source_count), 2, peers * chan_count, bin_count), jnp.float32),
        ],
        compiler_params=pltpu.CompilerParams(vmem_limit_bytes=VMEM_LIMIT),
        name="correlate",
    )(source_channel, table, blocks)


def stack_kernel(x_ref, out_ref, y_ref):
    count, block, pairs = x_ref.shape
    for n in range(count):
        y_ref[n] = x_ref[n].astype(jnp.float32)
    mean = tree_sum([y_ref[n] for n in range(count)]) * (1.0 / count)
    squares = []
    for n in range(count):
        sample = y_ref[n] - mean
        y_ref[n] = sample
        squares.append(sample * sample)
    variance = tree_sum(squares) * (1.0 / count)
    center = jnp.zeros_like(mean)
    for iteration in range(ITERS):
        limit = TUKEY * TUKEY * (variance + center * center + EPSILON)
        weights, products = [], []
        for n in range(count):
            sample = y_ref[n]
            deviation = sample - center
            kept = jnp.maximum(limit - deviation * deviation, 0.0)
            weight = kept * kept
            weights.append(weight)
            products.append(weight * sample)
        center = tree_sum(products) / tree_sum(weights)
    out_ref[...] = (center + mean).T


def tree_sum(terms):
    sums = list(terms[:2])
    for index, term in enumerate(terms[2:]):
        sums[index % 2] = sums[index % 2] + term
    return sums[0] + sums[1]


def stack_blocks(samples, source_count):
    count, block, pairs = samples.shape
    result = pl.pallas_call(
        stack_kernel,
        out_shape=jax.ShapeDtypeStruct((pairs, block), jnp.float32),
        in_specs=[pl.BlockSpec(memory_space=pltpu.VMEM)],
        out_specs=pl.BlockSpec(memory_space=pltpu.VMEM),
        scratch_shapes=[pltpu.VMEM((count, block, pairs), jnp.float32)],
        compiler_params=pltpu.CompilerParams(vmem_limit_bytes=VMEM_LIMIT),
        name="bisquare_stack",
    )(samples)
    return result.reshape(source_count, pairs // source_count, block).transpose(2, 0, 1)


def per_device(spectra, source_channel):
    win_count, _, chan_count, bin_count = spectra.shape
    source_count = source_channel.shape[0]
    peers = lax.axis_size("rcv")
    parts = lax.axis_size("win")
    block = L // parts
    items = share(win_count, source_count, peers)
    table = make_tables(bin_count, L, L // 2 + 16)
    if win_count % peers == 0:
        blocks = lax.all_to_all(spectra, "rcv", split_axis=0, concat_axis=0, tiled=True)
        blocks = blocks.reshape(peers, win_count // peers, 2, chan_count, bin_count)
    else:
        blocks = lax.all_gather(spectra, "rcv")
    corr = correlate(source_channel, table, blocks, parts, items)
    corr = corr.reshape(parts * peers, block, items * chan_count)
    moved = lax.all_to_all(corr, ("win", "rcv"), split_axis=0, concat_axis=0, tiled=True)
    if items != source_count:
        moved = moved.reshape(parts * peers, block, items, chan_count).transpose(0, 2, 1, 3)
        moved = moved.reshape(parts * win_count, source_count, block, chan_count).transpose(0, 2, 1, 3)
        moved = moved.reshape(parts * win_count, block, source_count * chan_count)
    return stack_blocks(moved, source_count)


def solution(mesh):
    return jax.shard_map(
        per_device,
        mesh=mesh,
        in_specs=(P("win", None, "rcv", None), P()),
        out_specs=P("win", None, "rcv"),
        check_vma=False,
    )
```

```python
import functools

import jax
import jax.numpy as jnp
import numpy as np
from jax import lax
from jax.experimental import pallas as pl
from jax.experimental.pallas import tpu as pltpu
from jax.sharding import PartitionSpec as P

L = 512
ITERS = 5
VMEM_LIMIT = 24 * 2**20


TUKEY = 4.685
EPSILON = 1e-06


def make_tables(bin_count, lag_count, rows):
    freq = np.arange(bin_count, dtype=np.int64)
    shifts = np.arange(lag_count // 2 + 1, dtype=np.int64)
    phase = shifts[:, None] * freq[None, :] % (2 * bin_count)
    angle = phase * (2.0 * np.pi / (2 * bin_count))
    factor = np.where(freq == 0, 1.0, 2.0) / np.sqrt(8.0 * bin_count)
    table = np.zeros((2, rows, bin_count), np.float32)
    table[0, : len(shifts)] = np.cos(angle) * factor
    table[1, : len(shifts)] = -np.sin(angle) * factor
    return jnp.asarray(table.astype(jnp.bfloat16))


def flip_kernel(out_ref):
    lag = lax.broadcasted_iota(jnp.int32, out_ref.shape, 0)
    shift = lax.broadcasted_iota(jnp.int32, out_ref.shape, 1)
    out_ref[...] = (lag + shift == out_ref.shape[0]).astype(jnp.float32).astype(jnp.bfloat16)


def make_flip(half, meanwhile):
    return pl.pallas_call(
        flip_kernel,
        out_shape=jax.ShapeDtypeStruct((half, half), jnp.bfloat16),
        out_specs=pl.BlockSpec(memory_space=pltpu.VMEM),
        compiler_params=pltpu.CompilerParams(vmem_limit_bytes=VMEM_LIMIT),
        cost_estimate=pl.CostEstimate(flops=meanwhile, bytes_accessed=0, transcendentals=0),
        name="make_flip",
    )()


def share(win_count, source_count, peers):
    items = win_count * source_count // peers
    assert items * peers == win_count * source_count
    assert items % source_count == 0 or source_count % items == 0
    return items


def correlate_kernel(*refs, peers, chunk):
    channel_ref, table_ref, flip_ref = refs[:3]
    block_refs = refs[3 : 3 + peers]
    out_ref, lags_ref, even_ref, odd_ref, cross_ref, float_ref, source_ref = refs[3 + peers :]
    win_count, _, chan_count, bin_count = block_refs[0].shape
    source_count = channel_ref.shape[0]
    items = share(win_count, source_count, peers)
    windows = float_ref.shape[0]
    parts, _, block, width = out_ref.shape
    half = flip_ref.shape[0]
    me = lax.axis_index("rcv")
    first = lax.div(me * items, source_count)
    rows = []
    for t in range(items):
        channel = channel_ref[lax.rem(me * items + t, source_count)]
        owner = lax.div(channel, chan_count)
        place = lax.rem(me - owner + peers, peers) * chan_count
        rows.append(place + lax.rem(channel, chan_count))
    for w in range(windows):
        own = range(w * source_count, min(items, (w + 1) * source_count))
        shape = (source_ref.shape[1], peers * chan_count)
        line = lax.broadcasted_iota(jnp.int32, shape, 0)
        column = lax.broadcasted_iota(jnp.int32, shape, 1)
        wanted = jnp.full(shape, -1, jnp.int32)
        for t in own:
            wanted = jnp.where(line == t - own.start, rows[t], wanted)
        onehot = (column == wanted).astype(jnp.float32).astype(jnp.bfloat16)
        for part in range(2):
            held = jnp.concatenate([block_refs[k][first + w, part] for k in range(peers)], axis=0)
            float_ref[w, part] = held.astype(jnp.float32)
            source_ref[2 * w + part] = jnp.dot(onehot, held, preferred_element_type=jnp.float32)

    def form_cross(bins, some):
        for t in some:
            w = t // source_count
            line = t % source_count
            real_p = float_ref[w, 0, :, bins]
            imag_q = float_ref[w, 1, :, bins]
            real_a = source_ref[2 * w, line : line + 1, bins]
            imag_b = source_ref[2 * w + 1, line : line + 1, bins]
            real = (real_a * real_p + imag_b * imag_q).astype(jnp.bfloat16)
            imag = (imag_b * real_p - real_a * imag_q).astype(jnp.bfloat16)
            for k in range(peers):
                receivers = slice(k * chan_count, (k + 1) * chan_count)
                pairs = slice(k * width + t * chan_count, k * width + (t + 1) * chan_count)
                cross_ref[0, pairs, bins] = real[receivers]
                cross_ref[1, pairs, bins] = imag[receivers]

    def add_product(bins, index, sum_ref):
        term = lax.dot_general(
            table_ref[index, :, bins],
            cross_ref[index, :, bins],
            (((1,), (1,)), ((), ())),
            preferred_element_type=jnp.float32,
        )
        if bins.start == 0:
            sum_ref[...] = term
        else:
            sum_ref[...] += term

    chunks = [slice(start, start + chunk) for start in range(0, bin_count, chunk)]
    for index in range(len(chunks) + 1):
        if index < len(chunks):
            form_cross(chunks[index], range(items // 2))
        if index > 0:
            add_product(chunks[index - 1], 0, even_ref)
        if index < len(chunks):
            form_cross(chunks[index], range(items // 2, items))
        if index > 0:
            add_product(chunks[index - 1], 1, odd_ref)
    lags_ref[half:, :] = even_ref[:half, :] + odd_ref[:half, :]
    back = (even_ref[...] - odd_ref[...]).astype(jnp.bfloat16)
    turned = jnp.dot(flip_ref[...], back[:half], preferred_element_type=jnp.float32)
    lags_ref[:half, :] = jnp.where(
        lax.broadcasted_iota(jnp.int32, turned.shape, 0) == 0,
        back[half : half + 16].astype(jnp.float32)[:1],
        turned,
    )
    for k in range(peers):
        owner = lax.rem(me - k + peers, peers)
        for part in range(parts):
            out_ref[part, owner] = lags_ref[
                part * block : (part + 1) * block, k * width : (k + 1) * width
            ].astype(jnp.bfloat16)


def correlate(source_channel, table, flip, blocks, parts):
    win_count, _, chan_count, bin_count = blocks[0].shape
    source_count = source_channel.shape[0]
    peers = len(blocks)
    items = share(win_count, source_count, peers)
    rows = table.shape[1]
    chunk = min(256, bin_count)
    width = items * chan_count
    windows = max(1, items // source_count)
    vmem = pl.BlockSpec(memory_space=pltpu.VMEM)
    return pl.pallas_call(
        functools.partial(correlate_kernel, peers=peers, chunk=chunk),
        out_shape=jax.ShapeDtypeStruct((parts, peers, L // parts, width), jnp.bfloat16),
        in_specs=[pl.BlockSpec(memory_space=pltpu.SMEM), vmem, vmem] + [vmem] * peers,
        out_specs=vmem,
        scratch_shapes=[
            pltpu.VMEM((L, peers * width), jnp.float32),
            pltpu.VMEM((rows, peers * width), jnp.float32),
            pltpu.VMEM((rows, peers * width), jnp.float32),
            pltpu.VMEM((2, peers * width, bin_count), jnp.bfloat16),
            pltpu.VMEM((windows, 2, peers * chan_count, bin_count), jnp.float32),
            pltpu.VMEM((2 * windows, 16, bin_count), jnp.float32),
        ],
        compiler_params=pltpu.CompilerParams(vmem_limit_bytes=VMEM_LIMIT),
        name="correlate",
    )(source_channel, table, flip, *blocks)


def stack_kernel(x_ref, out_ref, y_ref):
    count, block, pairs = x_ref.shape
    for n in range(count):
        y_ref[n] = x_ref[n].astype(jnp.float32)
    mean = tree_sum([y_ref[n] for n in range(count)]) * (1.0 / count)
    squares = []
    for n in range(count):
        sample = y_ref[n] - mean
        y_ref[n] = sample
        squares.append(sample * sample)
    variance = tree_sum(squares) * (1.0 / count)
    center = jnp.zeros_like(mean)
    for iteration in range(ITERS):
        limit = TUKEY * TUKEY * (variance + center * center + EPSILON)
        weights, products = [], []
        for n in range(count):
            sample = y_ref[n]
            deviation = sample - center
            kept = jnp.maximum(limit - deviation * deviation, 0.0)
            weight = kept * kept
            weights.append(weight)
            products.append(weight * sample)
        center = tree_sum(products) / tree_sum(weights)
    out_ref[...] = (center + mean).T


def tree_sum(terms):
    sums = list(terms[:2])
    for index, term in enumerate(terms[2:]):
        sums[index % 2] = sums[index % 2] + term
    return sums[0] + sums[1]


def stack_blocks(samples, source_count):
    count, block, pairs = samples.shape
    result = pl.pallas_call(
        stack_kernel,
        out_shape=jax.ShapeDtypeStruct((pairs, block), jnp.float32),
        in_specs=[pl.BlockSpec(memory_space=pltpu.VMEM)],
        out_specs=pl.BlockSpec(memory_space=pltpu.VMEM),
        scratch_shapes=[pltpu.VMEM((count, block, pairs), jnp.float32)],
        compiler_params=pltpu.CompilerParams(vmem_limit_bytes=VMEM_LIMIT),
        name="bisquare_stack",
    )(samples)
    return result.reshape(source_count, pairs // source_count, block).transpose(2, 0, 1)


def per_device(spectra, source_channel):
    win_count, _, chan_count, bin_count = spectra.shape
    source_count = source_channel.shape[0]
    peers = lax.axis_size("rcv")
    parts = lax.axis_size("win")
    block = L // parts
    items = share(win_count, source_count, peers)
    table = make_tables(bin_count, L, L // 2 + 16)
    flip = make_flip(L // 2, 2000 * table.size)
    blocks = [spectra]
    for step in range(1, peers):
        blocks.append(lax.ppermute(spectra, "rcv", [(i, (i + step) % peers) for i in range(peers)]))
    corr = correlate(source_channel, table, flip, blocks, parts)
    corr = corr.reshape(parts * peers, block, items * chan_count)
    moved = lax.all_to_all(corr, ("win", "rcv"), split_axis=0, concat_axis=0, tiled=True)
    if items != source_count:
        moved = moved.reshape(parts * peers, block, items, chan_count).transpose(0, 2, 1, 3)
        moved = moved.reshape(parts * win_count, source_count, block, chan_count).transpose(0, 2, 1, 3)
        moved = moved.reshape(parts * win_count, block, source_count * chan_count)
    return stack_blocks(moved, source_count)


def solution(mesh):
    return jax.shard_map(
        per_device,
        mesh=mesh,
        in_specs=(P("win", None, "rcv", None), P()),
        out_specs=P("win", None, "rcv"),
        check_vma=False,
    )
```

```python
import functools

import jax
import jax.numpy as jnp
import numpy as np
from jax import lax
from jax.experimental import pallas as pl
from jax.experimental.pallas import tpu as pltpu
from jax.sharding import PartitionSpec as P

L = 512
ITERS = 5
VMEM_LIMIT = 24 * 2**20


TUKEY = 4.685
EPSILON = 1e-06


def make_tables(bin_count, lag_count, rows):
    freq = np.arange(bin_count, dtype=np.int64)
    shifts = np.arange(lag_count // 2 + 1, dtype=np.int64)
    phase = shifts[:, None] * freq[None, :] % (2 * bin_count)
    angle = phase * (2.0 * np.pi / (2 * bin_count))
    factor = np.where(freq == 0, 1.0, 2.0) / np.sqrt(8.0 * bin_count)
    table = np.zeros((2, rows, bin_count), np.float32)
    table[0, : len(shifts)] = np.cos(angle) * factor
    table[1, : len(shifts)] = -np.sin(angle) * factor
    return jnp.asarray(table.astype(jnp.bfloat16))


def flip_kernel(out_ref):
    lag = lax.broadcasted_iota(jnp.int32, out_ref.shape, 0)
    shift = lax.broadcasted_iota(jnp.int32, out_ref.shape, 1)
    out_ref[...] = (lag + shift == out_ref.shape[0]).astype(jnp.float32).astype(jnp.bfloat16)


def make_flip(half, meanwhile):
    return pl.pallas_call(
        flip_kernel,
        out_shape=jax.ShapeDtypeStruct((half, half), jnp.bfloat16),
        out_specs=pl.BlockSpec(memory_space=pltpu.VMEM),
        compiler_params=pltpu.CompilerParams(vmem_limit_bytes=VMEM_LIMIT),
        cost_estimate=pl.CostEstimate(flops=meanwhile, bytes_accessed=0, transcendentals=0),
        name="make_flip",
    )()


def share(win_count, source_count, peers):
    items = win_count * source_count // peers
    assert items * peers == win_count * source_count
    assert items % source_count == 0 or source_count % items == 0
    return items


def correlate_kernel(*refs, peers, chunk):
    channel_ref, table_ref, flip_ref = refs[:3]
    block_refs = refs[3 : 3 + peers]
    out_ref, lags_ref, even_ref, odd_ref, cross_ref, float_ref = refs[3 + peers :]
    win_count, _, chan_count, bin_count = block_refs[0].shape
    source_count = channel_ref.shape[0]
    items = share(win_count, source_count, peers)
    windows = float_ref.shape[0]
    lines, _, depth, block, width = out_ref.shape
    half = flip_ref.shape[0]
    me = lax.axis_index("rcv")
    first = lax.div(me * items, source_count)
    rows = []
    for t in range(items):
        channel = channel_ref[lax.rem(me * items + t, source_count)]
        owner = lax.div(channel, chan_count)
        place = lax.rem(me - owner + peers, peers) * chan_count
        rows.append(place + lax.rem(channel, chan_count))
    def widen(bins):
        for k in range(peers):
            for w in range(windows):
                for part in range(2):
                    float_ref[w, part, k * chan_count : (k + 1) * chan_count, bins] = block_refs[k][
                        first + w, part, :, bins
                    ].astype(jnp.float32)

    def form_cross(bins, some):
        for t in some:
            w = t // source_count
            real_p = float_ref[w, 0, :, bins]
            imag_q = float_ref[w, 1, :, bins]
            real_a = float_ref[w, 0, pl.ds(rows[t], 1), bins]
            imag_b = float_ref[w, 1, pl.ds(rows[t], 1), bins]
            real = (real_a * real_p + imag_b * imag_q).astype(jnp.bfloat16)
            imag = (imag_b * real_p - real_a * imag_q).astype(jnp.bfloat16)
            for k in range(peers):
                receivers = slice(k * chan_count, (k + 1) * chan_count)
                pairs = slice(k * width + t * chan_count, k * width + (t + 1) * chan_count)
                cross_ref[0, pairs, bins] = real[receivers]
                cross_ref[1, pairs, bins] = imag[receivers]

    def add_product(bins, index, sum_ref):
        term = lax.dot_general(
            table_ref[index, :, bins],
            cross_ref[index, :, bins],
            (((1,), (1,)), ((), ())),
            preferred_element_type=jnp.float32,
        )
        if bins.start == 0:
            sum_ref[...] = term
        else:
            sum_ref[...] += term

    edges = [0] + list(range(chunk // 2, bin_count, chunk)) + [bin_count]
    chunks = [slice(start, stop) for start, stop in zip(edges[:-1], edges[1:])]
    for index in range(len(chunks) + 1):
        if index < len(chunks):
            widen(chunks[index])
            form_cross(chunks[index], range(items // 2))
        if index > 0:
            add_product(chunks[index - 1], 0, even_ref)
        if index < len(chunks):
            form_cross(chunks[index], range(items // 2, items))
        if index > 0:
            add_product(chunks[index - 1], 1, odd_ref)
    lags_ref[half:, :] = even_ref[:half, :] + odd_ref[:half, :]
    back = (even_ref[...] - odd_ref[...]).astype(jnp.bfloat16)
    turned = jnp.dot(flip_ref[...], back[:half], preferred_element_type=jnp.float32)
    lags_ref[:half, :] = jnp.where(
        lax.broadcasted_iota(jnp.int32, turned.shape, 0) == 0,
        back[half : half + 16].astype(jnp.float32)[:1],
        turned,
    )
    for k in range(peers):
        owner = lax.rem(me - k + peers, peers)
        for part in range(lines * depth):
            out_ref[part % lines, owner, part // lines] = lags_ref[
                part * block : (part + 1) * block, k * width : (k + 1) * width
            ].astype(jnp.bfloat16)


def correlate(source_channel, table, flip, blocks, lines, depth):
    win_count, _, chan_count, bin_count = blocks[0].shape
    source_count = source_channel.shape[0]
    peers = len(blocks)
    items = share(win_count, source_count, peers)
    rows = table.shape[1]
    chunk = min(512, bin_count)
    width = items * chan_count
    vmem = pl.BlockSpec(memory_space=pltpu.VMEM)
    return pl.pallas_call(
        functools.partial(correlate_kernel, peers=peers, chunk=chunk),
        out_shape=jax.ShapeDtypeStruct((lines, peers, depth, L // (lines * depth), width), jnp.bfloat16),
        in_specs=[pl.BlockSpec(memory_space=pltpu.SMEM), vmem, vmem] + [vmem] * peers,
        out_specs=vmem,
        scratch_shapes=[
            pltpu.VMEM((L, peers * width), jnp.float32),
            pltpu.VMEM((rows, peers * width), jnp.float32),
            pltpu.VMEM((rows, peers * width), jnp.float32),
            pltpu.VMEM((2, peers * width, bin_count), jnp.bfloat16),
            pltpu.VMEM((max(1, items // source_count), 2, peers * chan_count, bin_count), jnp.float32),
        ],
        compiler_params=pltpu.CompilerParams(vmem_limit_bytes=VMEM_LIMIT),
        name="correlate",
    )(source_channel, table, flip, *blocks)


def stack_kernel(x_ref, out_ref, y_ref):
    count, block, pairs = x_ref.shape
    for n in range(count):
        y_ref[n] = x_ref[n].astype(jnp.float32)
    mean = tree_sum([y_ref[n] for n in range(count)]) * (1.0 / count)
    squares = []
    for n in range(count):
        sample = y_ref[n] - mean
        y_ref[n] = sample
        squares.append(sample * sample)
    variance = tree_sum(squares) * (1.0 / count)
    center = jnp.zeros_like(mean)
    for iteration in range(ITERS):
        limit = TUKEY * TUKEY * (variance + center * center + EPSILON)
        weights, products = [], []
        for n in range(count):
            sample = y_ref[n]
            deviation = sample - center
            kept = jnp.maximum(limit - deviation * deviation, 0.0)
            weight = kept * kept
            weights.append(weight)
            products.append(weight * sample)
        center = tree_sum(products) / tree_sum(weights)
    out_ref[...] = (center + mean).T


def tree_sum(terms):
    sums = list(terms[:2])
    for index, term in enumerate(terms[2:]):
        sums[index % 2] = sums[index % 2] + term
    return sums[0] + sums[1]


def stack_blocks(samples, source_count):
    count, block, pairs = samples.shape
    result = pl.pallas_call(
        stack_kernel,
        out_shape=jax.ShapeDtypeStruct((pairs, block), jnp.float32),
        in_specs=[pl.BlockSpec(memory_space=pltpu.VMEM)],
        out_specs=pl.BlockSpec(memory_space=pltpu.VMEM),
        scratch_shapes=[pltpu.VMEM((count, block, pairs), jnp.float32)],
        compiler_params=pltpu.CompilerParams(vmem_limit_bytes=VMEM_LIMIT),
        name="bisquare_stack",
    )(samples)
    return result.reshape(source_count, pairs // source_count, block).transpose(2, 0, 1)


def per_device(spectra, source_channel):
    win_count, _, chan_count, bin_count = spectra.shape
    source_count = source_channel.shape[0]
    peers = lax.axis_size("rcv")
    parts = lax.axis_size("win")
    block = L // parts
    items = share(win_count, source_count, peers)
    table = make_tables(bin_count, L, L // 2 + 16)
    flip = make_flip(L // 2, 2000 * table.size)
    blocks = [spectra]
    for step in range(1, peers):
        blocks.append(lax.ppermute(spectra, "rcv", [(i, (i + step) % peers) for i in range(peers)]))
    lines = 1
    while 4 * lines * lines <= parts:
        lines *= 2
    depth = parts // lines
    assert lines * depth == parts
    corr = correlate(source_channel, table, flip, blocks, lines, depth)
    corr = corr.reshape(parts * peers, block, items * chan_count)
    group = [
        (z * lines + q) * peers + c for q in range(lines) for c in range(peers) for z in range(depth)
    ]
    moved = lax.all_to_all(
        corr, ("win", "rcv"), split_axis=0, concat_axis=0, tiled=True, axis_index_groups=[group]
    )
    if items != source_count:
        moved = moved.reshape(lines, peers, depth, block, items, chan_count)
        moved = moved.transpose(2, 0, 1, 4, 3, 5)
        moved = moved.reshape(parts * win_count, source_count, block, chan_count).transpose(0, 2, 1, 3)
        moved = moved.reshape(parts * win_count, block, source_count * chan_count)
    return stack_blocks(moved, source_count)


def solution(mesh):
    return jax.shard_map(
        per_device,
        mesh=mesh,
        in_specs=(P("win", None, "rcv", None), P()),
        out_specs=P("win", None, "rcv"),
        check_vma=False,
    )
```

```python
import functools

import jax
import jax.numpy as jnp
import numpy as np
from jax import lax
from jax.experimental import pallas as pl
from jax.experimental.pallas import tpu as pltpu
from jax.sharding import PartitionSpec as P

L = 512
ITERS = 5
VMEM_LIMIT = 24 * 2**20


TUKEY = 4.685
EPSILON = 1e-06


def make_tables(bin_count, lag_count, rows):
    freq = np.arange(bin_count, dtype=np.int64)
    shifts = np.arange(lag_count // 2 + 1, dtype=np.int64)
    phase = shifts[:, None] * freq[None, :] % (2 * bin_count)
    angle = phase * (2.0 * np.pi / (2 * bin_count))
    factor = np.where(freq == 0, 1.0, 2.0) / np.sqrt(8.0 * bin_count)
    table = np.zeros((2, rows, bin_count), np.float32)
    table[0, : len(shifts)] = np.cos(angle) * factor
    table[1, : len(shifts)] = -np.sin(angle) * factor
    return jnp.asarray(table.astype(jnp.bfloat16))


def flip_kernel(out_ref):
    lag = lax.broadcasted_iota(jnp.int32, out_ref.shape, 0)
    shift = lax.broadcasted_iota(jnp.int32, out_ref.shape, 1)
    out_ref[...] = (lag + shift == out_ref.shape[0]).astype(jnp.float32).astype(jnp.bfloat16)


def make_flip(half, meanwhile):
    return pl.pallas_call(
        flip_kernel,
        out_shape=jax.ShapeDtypeStruct((half, half), jnp.bfloat16),
        out_specs=pl.BlockSpec(memory_space=pltpu.VMEM),
        compiler_params=pltpu.CompilerParams(vmem_limit_bytes=VMEM_LIMIT),
        cost_estimate=pl.CostEstimate(flops=meanwhile, bytes_accessed=0, transcendentals=0),
        name="make_flip",
    )()


def share(win_count, source_count, peers):
    items = win_count * source_count // peers
    assert items * peers == win_count * source_count
    assert items % source_count == 0 or source_count % items == 0
    return items


def correlate_kernel(*refs, peers, chunk):
    channel_ref, table_ref, flip_ref = refs[:3]
    block_refs = refs[3 : 3 + peers]
    out_ref, lags_ref, even_ref, odd_ref, cross_ref, float_ref = refs[3 + peers :]
    win_count, _, chan_count, bin_count = block_refs[0].shape
    source_count = channel_ref.shape[0]
    items = share(win_count, source_count, peers)
    windows = float_ref.shape[0]
    lines, _, depth, block, width = out_ref.shape
    half = flip_ref.shape[0]
    me = lax.axis_index("rcv")
    first = lax.div(me * items, source_count)
    rows = []
    for t in range(items):
        channel = channel_ref[lax.rem(me * items + t, source_count)]
        owner = lax.div(channel, chan_count)
        place = lax.rem(me - owner + peers, peers) * chan_count
        rows.append(place + lax.rem(channel, chan_count))
    def widen(bins):
        for k in range(peers):
            for w in range(windows):
                for part in range(2):
                    float_ref[w, part, k * chan_count : (k + 1) * chan_count, bins] = block_refs[k][
                        first + w, part, :, bins
                    ].astype(jnp.float32)

    def form_cross(bins, some):
        for t in some:
            w = t // source_count
            real_p = float_ref[w, 0, :, bins]
            imag_q = float_ref[w, 1, :, bins]
            real_a = float_ref[w, 0, pl.ds(rows[t], 1), bins]
            imag_b = float_ref[w, 1, pl.ds(rows[t], 1), bins]
            real = (real_a * real_p + imag_b * imag_q).astype(jnp.bfloat16)
            imag = (imag_b * real_p - real_a * imag_q).astype(jnp.bfloat16)
            for k in range(peers):
                receivers = slice(k * chan_count, (k + 1) * chan_count)
                pairs = slice(k * width + t * chan_count, k * width + (t + 1) * chan_count)
                cross_ref[0, pairs, bins] = real[receivers]
                cross_ref[1, pairs, bins] = imag[receivers]

    def add_product(bins, index, sum_ref):
        term = lax.dot_general(
            table_ref[index, :, bins],
            cross_ref[index, :, bins],
            (((1,), (1,)), ((), ())),
            preferred_element_type=jnp.float32,
        )
        if bins.start == 0:
            sum_ref[...] = term
        else:
            sum_ref[...] += term

    chunks = [slice(start, start + chunk) for start in range(0, bin_count, chunk)]
    for index in range(len(chunks) + 1):
        if index < len(chunks):
            widen(chunks[index])
            form_cross(chunks[index], range(items // 2))
        if index > 0:
            add_product(chunks[index - 1], 0, even_ref)
        if index < len(chunks):
            form_cross(chunks[index], range(items // 2, items))
        if index > 0:
            add_product(chunks[index - 1], 1, odd_ref)
    lags_ref[half:, :] = even_ref[:half, :] + odd_ref[:half, :]
    back = (even_ref[...] - odd_ref[...]).astype(jnp.bfloat16)
    turned = jnp.dot(flip_ref[...], back[:half], preferred_element_type=jnp.float32)
    lags_ref[:half, :] = jnp.where(
        lax.broadcasted_iota(jnp.int32, turned.shape, 0) == 0,
        back[half : half + 16].astype(jnp.float32)[:1],
        turned,
    )
    for k in range(peers):
        owner = lax.rem(me - k + peers, peers)
        for part in range(lines * depth):
            out_ref[lines - 1 - part % lines, peers - 1 - owner, depth - 1 - part // lines] = lags_ref[
                part * block : (part + 1) * block, k * width : (k + 1) * width
            ].astype(jnp.bfloat16)


def correlate(source_channel, table, flip, blocks, lines, depth):
    win_count, _, chan_count, bin_count = blocks[0].shape
    source_count = source_channel.shape[0]
    peers = len(blocks)
    items = share(win_count, source_count, peers)
    rows = table.shape[1]
    chunk = min(256, bin_count)
    width = items * chan_count
    vmem = pl.BlockSpec(memory_space=pltpu.VMEM)
    return pl.pallas_call(
        functools.partial(correlate_kernel, peers=peers, chunk=chunk),
        out_shape=jax.ShapeDtypeStruct((lines, peers, depth, L // (lines * depth), width), jnp.bfloat16),
        in_specs=[pl.BlockSpec(memory_space=pltpu.SMEM), vmem, vmem] + [vmem] * peers,
        out_specs=vmem,
        scratch_shapes=[
            pltpu.VMEM((L, peers * width), jnp.float32),
            pltpu.VMEM((rows, peers * width), jnp.float32),
            pltpu.VMEM((rows, peers * width), jnp.float32),
            pltpu.VMEM((2, peers * width, bin_count), jnp.bfloat16),
            pltpu.VMEM((max(1, items // source_count), 2, peers * chan_count, bin_count), jnp.float32),
        ],
        compiler_params=pltpu.CompilerParams(vmem_limit_bytes=VMEM_LIMIT),
        name="correlate",
    )(source_channel, table, flip, *blocks)


def stack_kernel(x_ref, out_ref, y_ref):
    count, block, pairs = x_ref.shape
    for n in range(count):
        y_ref[n] = x_ref[n].astype(jnp.float32)
    mean = tree_sum([y_ref[n] for n in range(count)]) * (1.0 / count)
    squares = []
    for n in range(count):
        sample = y_ref[n] - mean
        y_ref[n] = sample
        squares.append(sample * sample)
    variance = tree_sum(squares) * (1.0 / count)
    center = jnp.zeros_like(mean)
    for iteration in range(ITERS):
        limit = TUKEY * TUKEY * (variance + center * center + EPSILON)
        weights, products = [], []
        for n in range(count):
            sample = y_ref[n]
            deviation = sample - center
            kept = jnp.maximum(limit - deviation * deviation, 0.0)
            weight = kept * kept
            weights.append(weight)
            products.append(weight * sample)
        center = tree_sum(products) / tree_sum(weights)
    out_ref[...] = (center + mean).T


def tree_sum(terms):
    sums = list(terms[:2])
    for index, term in enumerate(terms[2:]):
        sums[index % 2] = sums[index % 2] + term
    return sums[0] + sums[1]


def stack_blocks(samples, source_count):
    count, block, pairs = samples.shape
    result = pl.pallas_call(
        stack_kernel,
        out_shape=jax.ShapeDtypeStruct((pairs, block), jnp.float32),
        in_specs=[pl.BlockSpec(memory_space=pltpu.VMEM)],
        out_specs=pl.BlockSpec(memory_space=pltpu.VMEM),
        scratch_shapes=[pltpu.VMEM((count, block, pairs), jnp.float32)],
        compiler_params=pltpu.CompilerParams(vmem_limit_bytes=VMEM_LIMIT),
        name="bisquare_stack",
    )(samples)
    return result.reshape(source_count, pairs // source_count, block).transpose(2, 0, 1)


def per_device(spectra, source_channel):
    win_count, _, chan_count, bin_count = spectra.shape
    source_count = source_channel.shape[0]
    peers = lax.axis_size("rcv")
    parts = lax.axis_size("win")
    block = L // parts
    items = share(win_count, source_count, peers)
    table = make_tables(bin_count, L, L // 2 + 16)
    flip = make_flip(L // 2, 2000 * table.size)
    blocks = [spectra]
    for step in range(1, peers):
        blocks.append(lax.ppermute(spectra, "rcv", [(i, (i + step) % peers) for i in range(peers)]))
    lines = 1
    while 4 * lines * lines <= parts:
        lines *= 2
    depth = parts // lines
    assert lines * depth == parts
    corr = correlate(source_channel, table, flip, blocks, lines, depth)
    corr = corr.reshape(parts * peers, block, items * chan_count)
    group = [
        (z * lines + q) * peers + c for q in range(lines) for c in range(peers) for z in range(depth)
    ]
    group.reverse()
    moved = lax.all_to_all(
        corr, ("win", "rcv"), split_axis=0, concat_axis=0, tiled=True, axis_index_groups=[group]
    )
    if items != source_count:
        moved = moved[::-1].reshape(lines, peers, depth, block, items, chan_count)
        moved = moved.transpose(2, 0, 1, 4, 3, 5)
        moved = moved.reshape(parts * win_count, source_count, block, chan_count).transpose(0, 2, 1, 3)
        moved = moved.reshape(parts * win_count, block, source_count * chan_count)
    return stack_blocks(moved, source_count)


def solution(mesh):
    return jax.shard_map(
        per_device,
        mesh=mesh,
        in_specs=(P("win", None, "rcv", None), P()),
        out_specs=P("win", None, "rcv"),
        check_vma=False,
    )
```

```python
import functools

import jax
import jax.numpy as jnp
import numpy as np
from jax import lax
from jax.experimental import pallas as pl
from jax.experimental.pallas import tpu as pltpu
from jax.sharding import PartitionSpec as P

L = 512
ITERS = 5
VMEM_LIMIT = 24 * 2**20


TUKEY = 4.685
EPSILON = 1e-06


def make_tables(bin_count, lag_count, rows):
    freq = np.arange(bin_count, dtype=np.int64)
    shifts = np.arange(lag_count // 2 + 1, dtype=np.int64)
    phase = shifts[:, None] * freq[None, :] % (2 * bin_count)
    angle = phase * (2.0 * np.pi / (2 * bin_count))
    factor = np.where(freq == 0, 1.0, 2.0) / np.sqrt(8.0 * bin_count)
    table = np.zeros((2, rows, bin_count), np.float32)
    table[0, : len(shifts)] = np.cos(angle) * factor
    table[1, : len(shifts)] = -np.sin(angle) * factor
    return jnp.asarray(table.astype(jnp.bfloat16))


def flip_kernel(out_ref):
    lag = lax.broadcasted_iota(jnp.int32, out_ref.shape, 0)
    shift = lax.broadcasted_iota(jnp.int32, out_ref.shape, 1)
    out_ref[...] = (lag + shift == out_ref.shape[0]).astype(jnp.float32).astype(jnp.bfloat16)


def make_flip(half, meanwhile):
    return pl.pallas_call(
        flip_kernel,
        out_shape=jax.ShapeDtypeStruct((half, half), jnp.bfloat16),
        out_specs=pl.BlockSpec(memory_space=pltpu.VMEM),
        compiler_params=pltpu.CompilerParams(vmem_limit_bytes=VMEM_LIMIT),
        cost_estimate=pl.CostEstimate(flops=meanwhile, bytes_accessed=0, transcendentals=0),
        name="make_flip",
    )()


def share(win_count, source_count, peers):
    items = win_count * source_count // peers
    assert items * peers == win_count * source_count
    assert items % source_count == 0 or source_count % items == 0
    return items


def correlate_kernel(*refs, peers, chunk):
    channel_ref, table_ref, flip_ref = refs[:3]
    block_refs = refs[3 : 3 + peers]
    out_ref, lags_ref, even_ref, odd_ref, cross_ref, float_ref = refs[3 + peers :]
    win_count, _, chan_count, bin_count = block_refs[0].shape
    source_count = channel_ref.shape[0]
    items = share(win_count, source_count, peers)
    windows = float_ref.shape[0]
    lines, _, depth, block, width = out_ref.shape
    half = flip_ref.shape[0]
    me = lax.axis_index("rcv")
    first = lax.div(me * items, source_count)
    rows = []
    for t in range(items):
        channel = channel_ref[lax.rem(me * items + t, source_count)]
        owner = lax.div(channel, chan_count)
        place = lax.rem(me - owner + peers, peers) * chan_count
        rows.append(place + lax.rem(channel, chan_count))
    def widen(bins):
        for k in range(peers):
            for w in range(windows):
                for part in range(2):
                    float_ref[w, part, k * chan_count : (k + 1) * chan_count, bins] = block_refs[k][
                        first + w, part, :, bins
                    ].astype(jnp.float32)

    def form_cross(bins, some):
        for t in some:
            w = t // source_count
            real_p = float_ref[w, 0, :, bins]
            imag_q = float_ref[w, 1, :, bins]
            real_a = float_ref[w, 0, pl.ds(rows[t], 1), bins]
            imag_b = float_ref[w, 1, pl.ds(rows[t], 1), bins]
            real = (real_a * real_p + imag_b * imag_q).astype(jnp.bfloat16)
            imag = (imag_b * real_p - real_a * imag_q).astype(jnp.bfloat16)
            for k in range(peers):
                receivers = slice(k * chan_count, (k + 1) * chan_count)
                pairs = slice(k * width + t * chan_count, k * width + (t + 1) * chan_count)
                cross_ref[0, pairs, bins] = real[receivers]
                cross_ref[1, pairs, bins] = imag[receivers]

    def add_product(bins, index, sum_ref):
        term = lax.dot_general(
            table_ref[index, :, bins],
            cross_ref[index, :, bins],
            (((1,), (1,)), ((), ())),
            preferred_element_type=jnp.float32,
        )
        if bins.start == 0:
            sum_ref[...] = term
        else:
            sum_ref[...] += term

    chunks = [slice(start, start + chunk) for start in range(0, bin_count, chunk)]
    for index in range(len(chunks) + 1):
        if index < len(chunks):
            widen(chunks[index])
            form_cross(chunks[index], range(items // 2))
        if index > 0:
            add_product(chunks[index - 1], 0, even_ref)
        if index < len(chunks):
            form_cross(chunks[index], range(items // 2, items))
        if index > 0:
            add_product(chunks[index - 1], 1, odd_ref)
    ahead = (even_ref[:half, :] + odd_ref[:half, :]).astype(jnp.bfloat16)
    back = (even_ref[...] - odd_ref[...]).astype(jnp.bfloat16)
    turned = jnp.dot(flip_ref[...], back[:half], preferred_element_type=jnp.float32)
    behind = jnp.where(
        lax.broadcasted_iota(jnp.int32, turned.shape, 0) == 0,
        back[half : half + 16].astype(jnp.float32)[:1],
        turned,
    ).astype(jnp.bfloat16)
    if block % 16 != 0:
        lags_ref[half:, :] = ahead.astype(jnp.float32)
        lags_ref[:half, :] = behind.astype(jnp.float32)
    for k in range(peers):
        owner = lax.rem(me - k + peers, peers)
        columns = slice(k * width, (k + 1) * width)
        for part in range(lines * depth):
            start = part * block
            if block % 16 != 0:
                piece = lags_ref[start : start + block, columns].astype(jnp.bfloat16)
            elif start < half:
                piece = behind[start : start + block, columns]
            else:
                piece = ahead[start - half : start - half + block, columns]
            out_ref[part % lines, owner, part // lines] = piece


def correlate(source_channel, table, flip, blocks, lines, depth):
    win_count, _, chan_count, bin_count = blocks[0].shape
    source_count = source_channel.shape[0]
    peers = len(blocks)
    items = share(win_count, source_count, peers)
    rows = table.shape[1]
    chunk = min(256, bin_count)
    width = items * chan_count
    vmem = pl.BlockSpec(memory_space=pltpu.VMEM)
    return pl.pallas_call(
        functools.partial(correlate_kernel, peers=peers, chunk=chunk),
        out_shape=jax.ShapeDtypeStruct((lines, peers, depth, L // (lines * depth), width), jnp.bfloat16),
        in_specs=[pl.BlockSpec(memory_space=pltpu.SMEM), vmem, vmem] + [vmem] * peers,
        out_specs=vmem,
        scratch_shapes=[
            pltpu.VMEM((L, peers * width), jnp.float32),
            pltpu.VMEM((rows, peers * width), jnp.float32),
            pltpu.VMEM((rows, peers * width), jnp.float32),
            pltpu.VMEM((2, peers * width, bin_count), jnp.bfloat16),
            pltpu.VMEM((max(1, items // source_count), 2, peers * chan_count, bin_count), jnp.float32),
        ],
        compiler_params=pltpu.CompilerParams(vmem_limit_bytes=VMEM_LIMIT),
        name="correlate",
    )(source_channel, table, flip, *blocks)


def stack_kernel(x_ref, out_ref, y_ref):
    count, block, pairs = x_ref.shape
    for n in range(count):
        y_ref[n] = x_ref[n].astype(jnp.float32)
    step = max(8, block // 2)
    halves = [slice(start, start + step) for start in range(0, block, step)]
    means, variances, centers = [], [], []
    for lags in halves:
        mean = tree_sum([y_ref[n, lags, :] for n in range(count)]) * (1.0 / count)
        squares = []
        for n in range(count):
            sample = y_ref[n, lags, :] - mean
            y_ref[n, lags, :] = sample
            squares.append(sample * sample)
        means.append(mean)
        variances.append(tree_sum(squares) * (1.0 / count))
        centers.append(None)
    for iteration in range(ITERS):
        for index, lags in enumerate(halves):
            center = centers[index]
            limit = variances[index] + EPSILON
            if iteration > 0:
                limit = limit + center * center
            limit = TUKEY * TUKEY * limit
            weights, products = [], []
            for n in range(count):
                sample = y_ref[n, lags, :]
                deviation = sample if iteration == 0 else sample - center
                kept = jnp.maximum(limit - deviation * deviation, 0.0)
                weight = kept * kept
                weights.append(weight)
                products.append(weight * sample)
            centers[index] = tree_sum(products) / tree_sum(weights)
    results = [center + mean for center, mean in zip(centers, means)]
    out_ref[...] = jnp.concatenate(results, axis=0).T


def tree_sum(terms):
    sums = list(terms[:2])
    for index, term in enumerate(terms[2:]):
        sums[index % 2] = sums[index % 2] + term
    return sums[0] + sums[1]


def stack_blocks(samples, source_count):
    count, block, pairs = samples.shape
    result = pl.pallas_call(
        stack_kernel,
        out_shape=jax.ShapeDtypeStruct((pairs, block), jnp.float32),
        in_specs=[pl.BlockSpec(memory_space=pltpu.VMEM)],
        out_specs=pl.BlockSpec(memory_space=pltpu.VMEM),
        scratch_shapes=[pltpu.VMEM((count, block, pairs), jnp.float32)],
        compiler_params=pltpu.CompilerParams(vmem_limit_bytes=VMEM_LIMIT),
        name="bisquare_stack",
    )(samples)
    return result.reshape(source_count, pairs // source_count, block).transpose(2, 0, 1)


def per_device(spectra, source_channel):
    win_count, _, chan_count, bin_count = spectra.shape
    source_count = source_channel.shape[0]
    peers = lax.axis_size("rcv")
    parts = lax.axis_size("win")
    block = L // parts
    items = share(win_count, source_count, peers)
    table = make_tables(bin_count, L, L // 2 + 16)
    flip = make_flip(L // 2, 2000 * table.size)
    blocks = [spectra]
    for step in range(1, peers):
        blocks.append(lax.ppermute(spectra, "rcv", [(i, (i + step) % peers) for i in range(peers)]))
    lines = 1
    while 4 * lines * lines <= parts:
        lines *= 2
    depth = parts // lines
    assert lines * depth == parts
    corr = correlate(source_channel, table, flip, blocks, lines, depth)
    corr = corr.reshape(parts * peers, block, items * chan_count)
    group = [
        (z * lines + q) * peers + c for q in range(lines) for c in range(peers) for z in range(depth)
    ]
    moved = lax.all_to_all(
        corr, ("win", "rcv"), split_axis=0, concat_axis=0, tiled=True, axis_index_groups=[group]
    )
    if items != source_count:
        moved = moved.reshape(lines, peers, depth, block, items, chan_count)
        moved = moved.transpose(2, 0, 1, 4, 3, 5)
        moved = moved.reshape(parts * win_count, source_count, block, chan_count).transpose(0, 2, 1, 3)
        moved = moved.reshape(parts * win_count, block, source_count * chan_count)
    return stack_blocks(moved, source_count)


def solution(mesh):
    return jax.shard_map(
        per_device,
        mesh=mesh,
        in_specs=(P("win", None, "rcv", None), P()),
        out_specs=P("win", None, "rcv"),
        check_vma=False,
    )
```

```python
import functools

import jax
import jax.numpy as jnp
import numpy as np
from jax import lax
from jax.experimental import pallas as pl
from jax.experimental.pallas import tpu as pltpu
from jax.sharding import PartitionSpec as P

L = 512
ITERS = 5
VMEM_LIMIT = 24 * 2**20


TUKEY = 4.685
EPSILON = 1e-06


def make_tables(bin_count, lag_count, rows):
    freq = np.arange(bin_count, dtype=np.int64)
    shifts = np.arange(lag_count // 2 + 1, dtype=np.int64)
    phase = shifts[:, None] * freq[None, :] % (2 * bin_count)
    angle = phase * (2.0 * np.pi / (2 * bin_count))
    factor = np.where(freq == 0, 1.0, 2.0) / np.sqrt(8.0 * bin_count)
    table = np.zeros((2, rows, bin_count), np.float32)
    table[0, : len(shifts)] = np.cos(angle) * factor
    table[1, : len(shifts)] = -np.sin(angle) * factor
    return jnp.asarray(table.astype(jnp.bfloat16))


def flip_kernel(out_ref):
    lag = lax.broadcasted_iota(jnp.int32, out_ref.shape, 0)
    shift = lax.broadcasted_iota(jnp.int32, out_ref.shape, 1)
    out_ref[...] = (lag + shift == out_ref.shape[0]).astype(jnp.float32).astype(jnp.bfloat16)


def make_flip(half, meanwhile):
    return pl.pallas_call(
        flip_kernel,
        out_shape=jax.ShapeDtypeStruct((half, half), jnp.bfloat16),
        out_specs=pl.BlockSpec(memory_space=pltpu.VMEM),
        compiler_params=pltpu.CompilerParams(vmem_limit_bytes=VMEM_LIMIT),
        cost_estimate=pl.CostEstimate(flops=meanwhile, bytes_accessed=0, transcendentals=0),
        name="make_flip",
    )()


def share(win_count, source_count, peers):
    items = win_count * source_count // peers
    assert items * peers == win_count * source_count
    assert items % source_count == 0 or source_count % items == 0
    return items


def correlate_kernel(*refs, peers, chunk):
    channel_ref, table_ref, flip_ref = refs[:3]
    block_refs = refs[3 : 3 + peers]
    out_ref, lags_ref, even_ref, odd_ref, cross_ref, float_ref = refs[3 + peers :]
    win_count, _, chan_count, bin_count = block_refs[0].shape
    source_count = channel_ref.shape[0]
    items = share(win_count, source_count, peers)
    windows = float_ref.shape[0]
    lines, _, depth, block, width = out_ref.shape
    half = flip_ref.shape[0]
    me = lax.axis_index("rcv")
    first = lax.div(me * items, source_count)
    rows = []
    for t in range(items):
        channel = channel_ref[lax.rem(me * items + t, source_count)]
        owner = lax.div(channel, chan_count)
        place = lax.rem(me - owner + peers, peers) * chan_count
        rows.append(place + lax.rem(channel, chan_count))
    def widen(bins):
        sides = []
        for w in range(windows):
            for part in range(2):
                pieces = [block_refs[k][first + w, part, :, bins] for k in range(peers)]
                side = jnp.concatenate(pieces, axis=0).astype(jnp.float32)
                float_ref[w, part, :, bins] = side
                sides.append(side)
        return sides

    def form_cross(bins, some, sides):
        for t in some:
            w = t // source_count
            real_p, imag_q = sides[2 * w : 2 * w + 2]
            real_a = float_ref[w, 0, pl.ds(rows[t], 1), bins]
            imag_b = float_ref[w, 1, pl.ds(rows[t], 1), bins]
            real = (real_a * real_p + imag_b * imag_q).astype(jnp.bfloat16)
            imag = (imag_b * real_p - real_a * imag_q).astype(jnp.bfloat16)
            for k in range(peers):
                receivers = slice(k * chan_count, (k + 1) * chan_count)
                pairs = slice(k * width + t * chan_count, k * width + (t + 1) * chan_count)
                cross_ref[0, pairs, bins] = real[receivers]
                cross_ref[1, pairs, bins] = imag[receivers]

    def add_product(bins, index, sum_ref):
        term = lax.dot_general(
            table_ref[index, :, bins],
            cross_ref[index, :, bins],
            (((1,), (1,)), ((), ())),
            preferred_element_type=jnp.float32,
        )
        if bins.start == 0:
            sum_ref[...] = term
        else:
            sum_ref[...] += term

    chunks = [slice(start, start + chunk) for start in range(0, bin_count, chunk)]
    for index in range(len(chunks) + 1):
        if index < len(chunks):
            sides = widen(chunks[index])
            form_cross(chunks[index], range(items // 2), sides)
        if index > 0:
            add_product(chunks[index - 1], 0, even_ref)
        if index < len(chunks):
            form_cross(chunks[index], range(items // 2, items), sides)
        if index > 0:
            add_product(chunks[index - 1], 1, odd_ref)
    ahead = (even_ref[:half, :] + odd_ref[:half, :]).astype(jnp.bfloat16)
    back = (even_ref[...] - odd_ref[...]).astype(jnp.bfloat16)
    turned = jnp.dot(flip_ref[...], back[:half], preferred_element_type=jnp.float32)
    behind = jnp.where(
        lax.broadcasted_iota(jnp.int32, turned.shape, 0) == 0,
        back[half : half + 16].astype(jnp.float32)[:1],
        turned,
    ).astype(jnp.bfloat16)
    if block % 16 != 0:
        lags_ref[half:, :] = ahead.astype(jnp.float32)
        lags_ref[:half, :] = behind.astype(jnp.float32)
    for k in range(peers):
        owner = lax.rem(me - k + peers, peers)
        columns = slice(k * width, (k + 1) * width)
        for part in range(lines * depth):
            start = part * block
            if block % 16 != 0:
                piece = lags_ref[start : start + block, columns].astype(jnp.bfloat16)
            elif start < half:
                piece = behind[start : start + block, columns]
            else:
                piece = ahead[start - half : start - half + block, columns]
            out_ref[part % lines, owner, part // lines] = piece


def correlate(source_channel, table, flip, blocks, lines, depth):
    win_count, _, chan_count, bin_count = blocks[0].shape
    source_count = source_channel.shape[0]
    peers = len(blocks)
    items = share(win_count, source_count, peers)
    rows = table.shape[1]
    chunk = min(256, bin_count)
    width = items * chan_count
    vmem = pl.BlockSpec(memory_space=pltpu.VMEM)
    return pl.pallas_call(
        functools.partial(correlate_kernel, peers=peers, chunk=chunk),
        out_shape=jax.ShapeDtypeStruct((lines, peers, depth, L // (lines * depth), width), jnp.bfloat16),
        in_specs=[pl.BlockSpec(memory_space=pltpu.SMEM), vmem, vmem] + [vmem] * peers,
        out_specs=vmem,
        scratch_shapes=[
            pltpu.VMEM((L, peers * width), jnp.float32),
            pltpu.VMEM((rows, peers * width), jnp.float32),
            pltpu.VMEM((rows, peers * width), jnp.float32),
            pltpu.VMEM((2, peers * width, bin_count), jnp.bfloat16),
            pltpu.VMEM((max(1, items // source_count), 2, peers * chan_count, bin_count), jnp.float32),
        ],
        compiler_params=pltpu.CompilerParams(vmem_limit_bytes=VMEM_LIMIT),
        name="correlate",
    )(source_channel, table, flip, *blocks)


def stack_kernel(x_ref, out_ref, y_ref):
    count, block, pairs = x_ref.shape
    for n in range(count):
        y_ref[n] = x_ref[n].astype(jnp.float32)
    mean = tree_sum([y_ref[n] for n in range(count)]) * (1.0 / count)
    squares = []
    for n in range(count):
        sample = y_ref[n] - mean
        y_ref[n] = sample
        squares.append(sample * sample)
    variance = tree_sum(squares) * (1.0 / count)
    for iteration in range(ITERS):
        shift = center * center if iteration > 0 else 0.0
        limit = TUKEY * TUKEY * (variance + shift + EPSILON)
        weights, products = [], []
        for n in range(count):
            sample = y_ref[n]
            deviation = sample - center if iteration > 0 else sample
            kept = jnp.maximum(limit - deviation * deviation, 0.0)
            weight = kept * kept
            weights.append(weight)
            products.append(weight * sample)
        center = tree_sum(products) / tree_sum(weights)
    out_ref[...] = (center + mean).T


def tree_sum(terms):
    sums = list(terms[:2])
    for index, term in enumerate(terms[2:]):
        sums[index % 2] = sums[index % 2] + term
    return sums[0] + sums[1]


def stack_blocks(samples, source_count):
    count, block, pairs = samples.shape
    result = pl.pallas_call(
        stack_kernel,
        out_shape=jax.ShapeDtypeStruct((pairs, block), jnp.float32),
        in_specs=[pl.BlockSpec(memory_space=pltpu.VMEM)],
        out_specs=pl.BlockSpec(memory_space=pltpu.VMEM),
        scratch_shapes=[pltpu.VMEM((count, block, pairs), jnp.float32)],
        compiler_params=pltpu.CompilerParams(vmem_limit_bytes=VMEM_LIMIT),
        name="bisquare_stack",
    )(samples)
    return result.reshape(source_count, pairs // source_count, block).transpose(2, 0, 1)


def per_device(spectra, source_channel):
    win_count, _, chan_count, bin_count = spectra.shape
    source_count = source_channel.shape[0]
    peers = lax.axis_size("rcv")
    parts = lax.axis_size("win")
    block = L // parts
    items = share(win_count, source_count, peers)
    table = make_tables(bin_count, L, L // 2 + 16)
    flip = make_flip(L // 2, 2000 * table.size)
    blocks = [spectra]
    for step in range(1, peers):
        blocks.append(lax.ppermute(spectra, "rcv", [(i, (i + step) % peers) for i in range(peers)]))
    lines = 1
    while 4 * lines * lines <= parts:
        lines *= 2
    depth = parts // lines
    assert lines * depth == parts
    corr = correlate(source_channel, table, flip, blocks, lines, depth)
    corr = corr.reshape(parts * peers, block, items * chan_count)
    group = [
        (z * lines + q) * peers + c for q in range(lines) for c in range(peers) for z in range(depth)
    ]
    moved = lax.all_to_all(
        corr, ("win", "rcv"), split_axis=0, concat_axis=0, tiled=True, axis_index_groups=[group]
    )
    if items != source_count:
        moved = moved.reshape(lines, peers, depth, block, items, chan_count)
        moved = moved.transpose(2, 0, 1, 4, 3, 5)
        moved = moved.reshape(parts * win_count, source_count, block, chan_count).transpose(0, 2, 1, 3)
        moved = moved.reshape(parts * win_count, block, source_count * chan_count)
    return stack_blocks(moved, source_count)


def solution(mesh):
    return jax.shard_map(
        per_device,
        mesh=mesh,
        in_specs=(P("win", None, "rcv", None), P()),
        out_specs=P("win", None, "rcv"),
        check_vma=False,
    )
```

```python
import functools

import jax
import jax.numpy as jnp
import numpy as np
from jax import lax
from jax.experimental import pallas as pl
from jax.experimental.pallas import tpu as pltpu
from jax.sharding import PartitionSpec as P

L = 512
ITERS = 5
VMEM_LIMIT = 24 * 2**20


TUKEY = 4.685
EPSILON = 1e-06


def make_tables(bin_count, lag_count, rows):
    freq = np.arange(bin_count, dtype=np.int64)
    shifts = np.arange(lag_count // 2 + 1, dtype=np.int64)
    phase = shifts[:, None] * freq[None, :] % (2 * bin_count)
    angle = phase * (2.0 * np.pi / (2 * bin_count))
    factor = np.where(freq == 0, 1.0, 2.0) / np.sqrt(8.0 * bin_count)
    table = np.zeros((2, rows, bin_count), np.float32)
    table[0, : len(shifts)] = np.cos(angle) * factor
    table[1, : len(shifts)] = -np.sin(angle) * factor
    return jnp.asarray(table.astype(jnp.bfloat16))


def flip_kernel(out_ref):
    lag = lax.broadcasted_iota(jnp.int32, out_ref.shape, 0)
    shift = lax.broadcasted_iota(jnp.int32, out_ref.shape, 1)
    out_ref[...] = (lag + shift == out_ref.shape[0]).astype(jnp.float32).astype(jnp.bfloat16)


def make_flip(half, meanwhile):
    return pl.pallas_call(
        flip_kernel,
        out_shape=jax.ShapeDtypeStruct((half, half), jnp.bfloat16),
        out_specs=pl.BlockSpec(memory_space=pltpu.VMEM),
        compiler_params=pltpu.CompilerParams(vmem_limit_bytes=VMEM_LIMIT),
        cost_estimate=pl.CostEstimate(flops=meanwhile, bytes_accessed=0, transcendentals=0),
        name="make_flip",
    )()


def share(win_count, source_count, peers):
    items = win_count * source_count // peers
    assert items * peers == win_count * source_count
    assert items % source_count == 0 or source_count % items == 0
    return items


def correlate_kernel(*refs, peers, chunk):
    channel_ref, table_ref, flip_ref = refs[:3]
    block_refs = refs[3 : 3 + peers]
    out_ref, lags_ref, even_ref, odd_ref, cross_ref, float_ref = refs[3 + peers :]
    win_count, _, chan_count, bin_count = block_refs[0].shape
    source_count = channel_ref.shape[0]
    items = share(win_count, source_count, peers)
    windows = float_ref.shape[0]
    lines, _, depth, block, width = out_ref.shape
    half = flip_ref.shape[0]
    me = lax.axis_index("rcv")
    first = lax.div(me * items, source_count)
    rows = []
    for t in range(items):
        channel = channel_ref[lax.rem(me * items + t, source_count)]
        owner = lax.div(channel, chan_count)
        place = lax.rem(me - owner + peers, peers) * chan_count
        rows.append(place + lax.rem(channel, chan_count))
    def widen(bins):
        for k in range(peers):
            for w in range(windows):
                for part in range(2):
                    float_ref[w, part, k * chan_count : (k + 1) * chan_count, bins] = block_refs[k][
                        first + w, part, :, bins
                    ].astype(jnp.float32)

    def form_cross(bins, some):
        for t in some:
            w = t // source_count
            real_row = float_ref[w, 0, pl.ds(rows[t], 1), bins]
            imag_row = float_ref[w, 1, pl.ds(rows[t], 1), bins]
            for start in range(bins.start, bins.stop, 128):
                lanes = slice(start, start + 128)
                real_a = real_row[:, start - bins.start : start - bins.start + 128]
                imag_b = imag_row[:, start - bins.start : start - bins.start + 128]
                for k in range(peers):
                    receivers = slice(k * chan_count, (k + 1) * chan_count)
                    pairs = slice(k * width + t * chan_count, k * width + (t + 1) * chan_count)
                    real_p = float_ref[w, 0, receivers, lanes]
                    imag_q = float_ref[w, 1, receivers, lanes]
                    real = real_a * real_p + imag_b * imag_q
                    imag = imag_b * real_p - real_a * imag_q
                    cross_ref[0, pairs, lanes] = real.astype(jnp.bfloat16)
                    cross_ref[1, pairs, lanes] = imag.astype(jnp.bfloat16)

    def add_product(bins, index, sum_ref):
        term = lax.dot_general(
            table_ref[index, :, bins],
            cross_ref[index, :, bins],
            (((1,), (1,)), ((), ())),
            preferred_element_type=jnp.float32,
        )
        if bins.start == 0:
            sum_ref[...] = term
        else:
            sum_ref[...] += term

    chunks = [slice(start, start + chunk) for start in range(0, bin_count, chunk)]
    for index in range(len(chunks) + 1):
        if index < len(chunks):
            widen(chunks[index])
            form_cross(chunks[index], range(items // 2))
        if index > 0:
            add_product(chunks[index - 1], 0, even_ref)
        if index < len(chunks):
            form_cross(chunks[index], range(items // 2, items))
        if index > 0:
            add_product(chunks[index - 1], 1, odd_ref)
    ahead = (even_ref[:half, :] + odd_ref[:half, :]).astype(jnp.bfloat16)
    back = (even_ref[...] - odd_ref[...]).astype(jnp.bfloat16)
    turned = jnp.dot(flip_ref[...], back[:half], preferred_element_type=jnp.float32)
    behind = jnp.where(
        lax.broadcasted_iota(jnp.int32, turned.shape, 0) == 0,
        back[half : half + 16].astype(jnp.float32)[:1],
        turned,
    ).astype(jnp.bfloat16)
    if block % 16 != 0:
        lags_ref[half:, :] = ahead.astype(jnp.float32)
        lags_ref[:half, :] = behind.astype(jnp.float32)
    for k in range(peers):
        owner = lax.rem(me - k + peers, peers)
        columns = slice(k * width, (k + 1) * width)
        for part in range(lines * depth):
            start = part * block
            if block % 16 != 0:
                piece = lags_ref[start : start + block, columns].astype(jnp.bfloat16)
            elif start < half:
                piece = behind[start : start + block, columns]
            else:
                piece = ahead[start - half : start - half + block, columns]
            out_ref[part % lines, owner, part // lines] = piece


def correlate(source_channel, table, flip, blocks, lines, depth):
    win_count, _, chan_count, bin_count = blocks[0].shape
    source_count = source_channel.shape[0]
    peers = len(blocks)
    items = share(win_count, source_count, peers)
    rows = table.shape[1]
    chunk = min(256, bin_count)
    width = items * chan_count
    vmem = pl.BlockSpec(memory_space=pltpu.VMEM)
    return pl.pallas_call(
        functools.partial(correlate_kernel, peers=peers, chunk=chunk),
        out_shape=jax.ShapeDtypeStruct((lines, peers, depth, L // (lines * depth), width), jnp.bfloat16),
        in_specs=[pl.BlockSpec(memory_space=pltpu.SMEM), vmem, vmem] + [vmem] * peers,
        out_specs=vmem,
        scratch_shapes=[
            pltpu.VMEM((L, peers * width), jnp.float32),
            pltpu.VMEM((rows, peers * width), jnp.float32),
            pltpu.VMEM((rows, peers * width), jnp.float32),
            pltpu.VMEM((2, peers * width, bin_count), jnp.bfloat16),
            pltpu.VMEM((max(1, items // source_count), 2, peers * chan_count, bin_count), jnp.float32),
        ],
        compiler_params=pltpu.CompilerParams(vmem_limit_bytes=VMEM_LIMIT),
        name="correlate",
    )(source_channel, table, flip, *blocks)


def stack_kernel(x_ref, out_ref, y_ref):
    count, block, pairs = x_ref.shape
    for n in range(count):
        y_ref[n] = x_ref[n].astype(jnp.float32)
    mean = tree_sum([y_ref[n] for n in range(count)]) * (1.0 / count)
    squares = []
    for n in range(count):
        sample = y_ref[n] - mean
        y_ref[n] = sample
        squares.append(sample * sample)
    variance = tree_sum(squares) * (1.0 / count)
    for iteration in range(ITERS):
        shift = center * center if iteration > 0 else 0.0
        limit = TUKEY * TUKEY * (variance + shift + EPSILON)
        weights, products = [], []
        for n in range(count):
            sample = y_ref[n]
            deviation = sample - center if iteration > 0 else sample
            kept = jnp.maximum(limit - deviation * deviation, 0.0)
            weight = kept * kept
            weights.append(weight)
            products.append(weight * sample)
        center = tree_sum(products) / tree_sum(weights)
    out_ref[...] = (center + mean).T


def tree_sum(terms):
    sums = list(terms[:2])
    for index, term in enumerate(terms[2:]):
        sums[index % 2] = sums[index % 2] + term
    return sums[0] + sums[1]


def stack_blocks(samples, source_count):
    count, block, pairs = samples.shape
    result = pl.pallas_call(
        stack_kernel,
        out_shape=jax.ShapeDtypeStruct((pairs, block), jnp.float32),
        in_specs=[pl.BlockSpec(memory_space=pltpu.VMEM)],
        out_specs=pl.BlockSpec(memory_space=pltpu.VMEM),
        scratch_shapes=[pltpu.VMEM((count, block, pairs), jnp.float32)],
        compiler_params=pltpu.CompilerParams(vmem_limit_bytes=VMEM_LIMIT),
        name="bisquare_stack",
    )(samples)
    return result.reshape(source_count, pairs // source_count, block).transpose(2, 0, 1)


def per_device(spectra, source_channel):
    win_count, _, chan_count, bin_count = spectra.shape
    source_count = source_channel.shape[0]
    peers = lax.axis_size("rcv")
    parts = lax.axis_size("win")
    block = L // parts
    items = share(win_count, source_count, peers)
    table = make_tables(bin_count, L, L // 2 + 16)
    flip = make_flip(L // 2, 2000 * table.size)
    blocks = [spectra]
    for step in range(1, peers):
        blocks.append(lax.ppermute(spectra, "rcv", [(i, (i + step) % peers) for i in range(peers)]))
    lines = 1
    while 4 * lines * lines <= parts:
        lines *= 2
    depth = parts // lines
    assert lines * depth == parts
    corr = correlate(source_channel, table, flip, blocks, lines, depth)
    corr = corr.reshape(parts * peers, block, items * chan_count)
    group = [
        (z * lines + q) * peers + c for q in range(lines) for c in range(peers) for z in range(depth)
    ]
    moved = lax.all_to_all(
        corr, ("win", "rcv"), split_axis=0, concat_axis=0, tiled=True, axis_index_groups=[group]
    )
    if items != source_count:
        moved = moved.reshape(lines, peers, depth, block, items, chan_count)
        moved = moved.transpose(2, 0, 1, 4, 3, 5)
        moved = moved.reshape(parts * win_count, source_count, block, chan_count).transpose(0, 2, 1, 3)
        moved = moved.reshape(parts * win_count, block, source_count * chan_count)
    return stack_blocks(moved, source_count)


def solution(mesh):
    return jax.shard_map(
        per_device,
        mesh=mesh,
        in_specs=(P("win", None, "rcv", None), P()),
        out_specs=P("win", None, "rcv"),
        check_vma=False,
    )
```

```python
import functools

import jax
import jax.numpy as jnp
import numpy as np
from jax import lax
from jax.experimental import pallas as pl
from jax.experimental.pallas import tpu as pltpu
from jax.sharding import PartitionSpec as P

L = 512
ITERS = 5
VMEM_LIMIT = 24 * 2**20


TUKEY = 4.685
EPSILON = 1e-06


def make_tables(bin_count, lag_count, rows):
    freq = np.arange(bin_count, dtype=np.int64)
    shifts = np.arange(lag_count // 2 + 1, dtype=np.int64)
    phase = shifts[:, None] * freq[None, :] % (2 * bin_count)
    angle = phase * (2.0 * np.pi / (2 * bin_count))
    factor = np.where(freq == 0, 1.0, 2.0) / np.sqrt(8.0 * bin_count)
    table = np.zeros((2, rows, bin_count), np.float32)
    table[0, : len(shifts)] = np.cos(angle) * factor
    table[1, : len(shifts)] = -np.sin(angle) * factor
    return jnp.asarray(table.astype(jnp.bfloat16))


def flip_kernel(out_ref):
    lag = lax.broadcasted_iota(jnp.int32, out_ref.shape, 0)
    shift = lax.broadcasted_iota(jnp.int32, out_ref.shape, 1)
    out_ref[...] = (lag + shift == out_ref.shape[0]).astype(jnp.float32).astype(jnp.bfloat16)


def make_flip(half, meanwhile):
    return pl.pallas_call(
        flip_kernel,
        out_shape=jax.ShapeDtypeStruct((half, half), jnp.bfloat16),
        out_specs=pl.BlockSpec(memory_space=pltpu.VMEM),
        compiler_params=pltpu.CompilerParams(vmem_limit_bytes=VMEM_LIMIT),
        cost_estimate=pl.CostEstimate(flops=meanwhile, bytes_accessed=0, transcendentals=0),
        name="make_flip",
    )()


def share(win_count, source_count, peers):
    items = win_count * source_count // peers
    assert items * peers == win_count * source_count
    assert items % source_count == 0 or source_count % items == 0
    return items


def correlate_kernel(*refs, peers, chunk):
    channel_ref, table_ref, flip_ref = refs[:3]
    block_refs = refs[3 : 3 + peers]
    out_ref, lags_ref, even_ref, odd_ref, cross_ref, float_ref, source_ref = refs[3 + peers :]
    win_count, _, chan_count, bin_count = block_refs[0].shape
    source_count = channel_ref.shape[0]
    items = share(win_count, source_count, peers)
    windows = float_ref.shape[0]
    lines, _, depth, block, width = out_ref.shape
    half = flip_ref.shape[0]
    me = lax.axis_index("rcv")
    first = lax.div(me * items, source_count)
    rows = []
    for t in range(items):
        channel = channel_ref[lax.rem(me * items + t, source_count)]
        owner = lax.div(channel, chan_count)
        place = lax.rem(me - owner + peers, peers) * chan_count
        rows.append(place + lax.rem(channel, chan_count))
    spread = 8
    shape = (source_ref.shape[1], peers * chan_count)
    line = lax.broadcasted_iota(jnp.int32, shape, 0)
    column = lax.broadcasted_iota(jnp.int32, shape, 1)
    picks = []
    for w in range(windows):
        wanted = jnp.full(shape, -1, jnp.int32)
        for t in range(w * source_count, min(items, (w + 1) * source_count)):
            wanted = jnp.where(line // spread == t % source_count, rows[t], wanted)
        picks.append((column == wanted).astype(jnp.float32).astype(jnp.bfloat16))

    def prepare(bins):
        for w in range(windows):
            for part in range(2):
                pieces = [block_refs[k][first + w, part, :, bins] for k in range(peers)]
                side = jnp.concatenate(pieces, axis=0)
                float_ref[w, part, :, bins] = side.astype(jnp.float32)
                source_ref[2 * w + part, :, bins] = jnp.dot(
                    picks[w], side, preferred_element_type=jnp.float32
                )

    def form_cross(bins, some):
        for t in some:
            w = t // source_count
            own = slice(t % source_count * spread, (t % source_count + 1) * spread)
            real_p = by_eights(float_ref[w, 0, :, bins])
            imag_q = by_eights(float_ref[w, 1, :, bins])
            real_a = source_ref[2 * w, own, bins][None]
            imag_b = source_ref[2 * w + 1, own, bins][None]
            real = real_a * real_p + imag_b * imag_q
            imag = imag_b * real_p - real_a * imag_q
            for index, value in ((0, real), (1, imag)):
                value = value.reshape(peers * chan_count, value.shape[2]).astype(jnp.bfloat16)
                for k in range(peers):
                    pairs = slice(k * width + t * chan_count, k * width + (t + 1) * chan_count)
                    cross_ref[index, pairs, bins] = value[k * chan_count : (k + 1) * chan_count]

    def add_product(bins, index, sum_ref):
        term = lax.dot_general(
            table_ref[index, :, bins],
            cross_ref[index, :, bins],
            (((1,), (1,)), ((), ())),
            preferred_element_type=jnp.float32,
        )
        if bins.start == 0:
            sum_ref[...] = term
        else:
            sum_ref[...] += term

    chunks = [slice(start, start + chunk) for start in range(0, bin_count, chunk)]
    prepare(chunks[0])
    for index in range(len(chunks) + 1):
        if index + 1 < len(chunks):
            prepare(chunks[index + 1])
        if index < len(chunks):
            form_cross(chunks[index], range(items // 2))
        if index > 0:
            add_product(chunks[index - 1], 0, even_ref)
        if index < len(chunks):
            form_cross(chunks[index], range(items // 2, items))
        if index > 0:
            add_product(chunks[index - 1], 1, odd_ref)
    ahead = (even_ref[:half, :] + odd_ref[:half, :]).astype(jnp.bfloat16)
    back = (even_ref[...] - odd_ref[...]).astype(jnp.bfloat16)
    turned = jnp.dot(flip_ref[...], back[:half], preferred_element_type=jnp.float32)
    behind = jnp.where(
        lax.broadcasted_iota(jnp.int32, turned.shape, 0) == 0,
        back[half : half + 16].astype(jnp.float32)[:1],
        turned,
    ).astype(jnp.bfloat16)
    if block % 16 != 0:
        lags_ref[half:, :] = ahead.astype(jnp.float32)
        lags_ref[:half, :] = behind.astype(jnp.float32)
    for k in range(peers):
        owner = lax.rem(me - k + peers, peers)
        columns = slice(k * width, (k + 1) * width)
        for part in range(lines * depth):
            start = part * block
            if block % 16 != 0:
                piece = lags_ref[start : start + block, columns].astype(jnp.bfloat16)
            elif start < half:
                piece = behind[start : start + block, columns]
            else:
                piece = ahead[start - half : start - half + block, columns]
            out_ref[part % lines, owner, part // lines] = piece


def by_eights(values):
    return values.reshape(values.shape[0] // 8, 8, values.shape[1])


def correlate(source_channel, table, flip, blocks, lines, depth):
    win_count, _, chan_count, bin_count = blocks[0].shape
    source_count = source_channel.shape[0]
    peers = len(blocks)
    items = share(win_count, source_count, peers)
    rows = table.shape[1]
    chunk = min(256, bin_count)
    width = items * chan_count
    windows = max(1, items // source_count)
    vmem = pl.BlockSpec(memory_space=pltpu.VMEM)
    return pl.pallas_call(
        functools.partial(correlate_kernel, peers=peers, chunk=chunk),
        out_shape=jax.ShapeDtypeStruct((lines, peers, depth, L // (lines * depth), width), jnp.bfloat16),
        in_specs=[pl.BlockSpec(memory_space=pltpu.SMEM), vmem, vmem] + [vmem] * peers,
        out_specs=vmem,
        scratch_shapes=[
            pltpu.VMEM((L, peers * width), jnp.float32),
            pltpu.VMEM((rows, peers * width), jnp.float32),
            pltpu.VMEM((rows, peers * width), jnp.float32),
            pltpu.VMEM((2, peers * width, bin_count), jnp.bfloat16),
            pltpu.VMEM((windows, 2, peers * chan_count, bin_count), jnp.float32),
            pltpu.VMEM((2 * windows, 8 * min(items, source_count), bin_count), jnp.float32),
        ],
        compiler_params=pltpu.CompilerParams(vmem_limit_bytes=VMEM_LIMIT),
        name="correlate",
    )(source_channel, table, flip, *blocks)


def stack_kernel(x_ref, out_ref, y_ref):
    count, block, pairs = x_ref.shape
    for n in range(count):
        y_ref[n] = x_ref[n].astype(jnp.float32)
    mean = tree_sum([y_ref[n] for n in range(count)]) * (1.0 / count)
    squares = []
    for n in range(count):
        sample = y_ref[n] - mean
        y_ref[n] = sample
        squares.append(sample * sample)
    variance = tree_sum(squares) * (1.0 / count)
    for iteration in range(ITERS):
        shift = center * center if iteration > 0 else 0.0
        limit = TUKEY * TUKEY * (variance + shift + EPSILON)
        weights, products = [], []
        for n in range(count):
            sample = y_ref[n]
            deviation = sample - center if iteration > 0 else sample
            kept = jnp.maximum(limit - deviation * deviation, 0.0)
            weight = kept * kept
            weights.append(weight)
            products.append(weight * sample)
        center = tree_sum(products) / tree_sum(weights)
    out_ref[...] = (center + mean).T


def tree_sum(terms):
    sums = list(terms[:2])
    for index, term in enumerate(terms[2:]):
        sums[index % 2] = sums[index % 2] + term
    return sums[0] + sums[1]


def stack_blocks(samples, source_count):
    count, block, pairs = samples.shape
    result = pl.pallas_call(
        stack_kernel,
        out_shape=jax.ShapeDtypeStruct((pairs, block), jnp.float32),
        in_specs=[pl.BlockSpec(memory_space=pltpu.VMEM)],
        out_specs=pl.BlockSpec(memory_space=pltpu.VMEM),
        scratch_shapes=[pltpu.VMEM((count, block, pairs), jnp.float32)],
        compiler_params=pltpu.CompilerParams(vmem_limit_bytes=VMEM_LIMIT),
        name="bisquare_stack",
    )(samples)
    return result.reshape(source_count, pairs // source_count, block).transpose(2, 0, 1)


def per_device(spectra, source_channel):
    win_count, _, chan_count, bin_count = spectra.shape
    source_count = source_channel.shape[0]
    peers = lax.axis_size("rcv")
    parts = lax.axis_size("win")
    block = L // parts
    items = share(win_count, source_count, peers)
    table = make_tables(bin_count, L, L // 2 + 16)
    flip = make_flip(L // 2, 2000 * table.size)
    blocks = [spectra]
    for step in range(1, peers):
        blocks.append(lax.ppermute(spectra, "rcv", [(i, (i + step) % peers) for i in range(peers)]))
    lines = 1
    while 4 * lines * lines <= parts:
        lines *= 2
    depth = parts // lines
    assert lines * depth == parts
    corr = correlate(source_channel, table, flip, blocks, lines, depth)
    corr = corr.reshape(parts * peers, block, items * chan_count)
    group = [
        (z * lines + q) * peers + c for q in range(lines) for c in range(peers) for z in range(depth)
    ]
    moved = lax.all_to_all(
        corr, ("win", "rcv"), split_axis=0, concat_axis=0, tiled=True, axis_index_groups=[group]
    )
    if items != source_count:
        moved = moved.reshape(lines, peers, depth, block, items, chan_count)
        moved = moved.transpose(2, 0, 1, 4, 3, 5)
        moved = moved.reshape(parts * win_count, source_count, block, chan_count).transpose(0, 2, 1, 3)
        moved = moved.reshape(parts * win_count, block, source_count * chan_count)
    return stack_blocks(moved, source_count)


def solution(mesh):
    return jax.shard_map(
        per_device,
        mesh=mesh,
        in_specs=(P("win", None, "rcv", None), P()),
        out_specs=P("win", None, "rcv"),
        check_vma=False,
    )
```

```python
import functools

import jax
import jax.numpy as jnp
import numpy as np
from jax import lax
from jax.experimental import pallas as pl
from jax.experimental.pallas import tpu as pltpu
from jax.sharding import PartitionSpec as P

L = 512
ITERS = 5
VMEM_LIMIT = 24 * 2**20


TUKEY = 4.685
EPSILON = 1e-06


def make_tables(bin_count, lag_count, rows):
    freq = np.arange(bin_count, dtype=np.int64)
    shifts = np.arange(lag_count // 2 + 1, dtype=np.int64)
    phase = shifts[:, None] * freq[None, :] % (2 * bin_count)
    angle = phase * (2.0 * np.pi / (2 * bin_count))
    factor = np.where(freq == 0, 1.0, 2.0) / np.sqrt(8.0 * bin_count)
    table = np.zeros((2, rows, bin_count), np.float32)
    table[0, : len(shifts)] = np.cos(angle) * factor
    table[1, : len(shifts)] = -np.sin(angle) * factor
    return jnp.asarray(table.astype(jnp.bfloat16))


def flip_kernel(out_ref):
    lag = lax.broadcasted_iota(jnp.int32, out_ref.shape, 0)
    shift = lax.broadcasted_iota(jnp.int32, out_ref.shape, 1)
    out_ref[...] = (lag + shift == out_ref.shape[0]).astype(jnp.float32).astype(jnp.bfloat16)


def make_flip(half, meanwhile):
    return pl.pallas_call(
        flip_kernel,
        out_shape=jax.ShapeDtypeStruct((half, half), jnp.bfloat16),
        out_specs=pl.BlockSpec(memory_space=pltpu.VMEM),
        compiler_params=pltpu.CompilerParams(vmem_limit_bytes=VMEM_LIMIT),
        cost_estimate=pl.CostEstimate(flops=meanwhile, bytes_accessed=0, transcendentals=0),
        name="make_flip",
    )()


def share(win_count, source_count, peers):
    items = win_count * source_count // peers
    assert items * peers == win_count * source_count
    assert items % source_count == 0 or source_count % items == 0
    return items


def correlate_kernel(*refs, peers, chunk):
    channel_ref, table_ref, flip_ref = refs[:3]
    block_refs = refs[3 : 3 + peers]
    out_ref, lags_ref, even_ref, odd_ref, cross_ref, float_ref = refs[3 + peers :]
    win_count, _, chan_count, bin_count = block_refs[0].shape
    source_count = channel_ref.shape[0]
    items = share(win_count, source_count, peers)
    windows = float_ref.shape[0]
    lines, _, depth, block, width = out_ref.shape
    half = flip_ref.shape[0]
    me = lax.axis_index("rcv")
    first = lax.div(me * items, source_count)
    rows = []
    for t in range(items):
        channel = channel_ref[lax.rem(me * items + t, source_count)]
        owner = lax.div(channel, chan_count)
        place = lax.rem(me - owner + peers, peers) * chan_count
        rows.append(place + lax.rem(channel, chan_count))
    def widen(bins):
        for k in range(peers):
            for w in range(windows):
                for part in range(2):
                    float_ref[w, part, k * chan_count : (k + 1) * chan_count, bins] = block_refs[k][
                        first + w, part, :, bins
                    ].astype(jnp.float32)

    def form_cross(bins, some):
        for t in some:
            w = t // source_count
            real_p = float_ref[w, 0, :, bins]
            imag_q = float_ref[w, 1, :, bins]
            real_a = float_ref[w, 0, pl.ds(rows[t], 1), bins]
            imag_b = float_ref[w, 1, pl.ds(rows[t], 1), bins]
            real = (real_a * real_p + imag_b * imag_q).astype(jnp.bfloat16)
            imag = (imag_b * real_p - real_a * imag_q).astype(jnp.bfloat16)
            for k in range(peers):
                receivers = slice(k * chan_count, (k + 1) * chan_count)
                pairs = slice(k * width + t * chan_count, k * width + (t + 1) * chan_count)
                cross_ref[0, pairs, bins] = real[receivers]
                cross_ref[1, pairs, bins] = imag[receivers]

    def add_product(bins, index, sum_ref):
        term = lax.dot_general(
            table_ref[index, :, bins],
            cross_ref[index, :, bins],
            (((1,), (1,)), ((), ())),
            preferred_element_type=jnp.float32,
        )
        if bins.start == 0:
            sum_ref[...] = term
        else:
            sum_ref[...] += term

    chunks = [slice(start, start + chunk) for start in range(0, bin_count, chunk)]
    for index in range(len(chunks) + 1):
        if index < len(chunks):
            widen(chunks[index])
            form_cross(chunks[index], range(items // 2))
        if index > 0:
            add_product(chunks[index - 1], 0, even_ref)
        if index < len(chunks):
            form_cross(chunks[index], range(items // 2, items))
        if index > 0:
            add_product(chunks[index - 1], 1, odd_ref)
    ahead = (even_ref[:half, :] + odd_ref[:half, :]).astype(jnp.bfloat16)
    back = (even_ref[...] - odd_ref[...]).astype(jnp.bfloat16)
    turned = jnp.dot(flip_ref[...], back[:half], preferred_element_type=jnp.float32)
    behind = jnp.where(
        lax.broadcasted_iota(jnp.int32, turned.shape, 0) == 0,
        back[half : half + 16].astype(jnp.float32)[:1],
        turned,
    ).astype(jnp.bfloat16)
    if block % 16 != 0:
        lags_ref[half:, :] = ahead.astype(jnp.float32)
        lags_ref[:half, :] = behind.astype(jnp.float32)
    for k in range(peers):
        owner = lax.rem(me - k + peers, peers)
        columns = slice(k * width, (k + 1) * width)
        for part in range(lines * depth):
            start = part * block
            if block % 16 != 0:
                piece = lags_ref[start : start + block, columns].astype(jnp.bfloat16)
            elif start < half:
                piece = behind[start : start + block, columns]
            else:
                piece = ahead[start - half : start - half + block, columns]
            z = part // lines
            out_ref[part % lines, owner, z + lax.rem(owner, 2) * (depth - 1 - 2 * z)] = piece


def correlate(source_channel, table, flip, blocks, lines, depth):
    win_count, _, chan_count, bin_count = blocks[0].shape
    source_count = source_channel.shape[0]
    peers = len(blocks)
    items = share(win_count, source_count, peers)
    rows = table.shape[1]
    chunk = min(256, bin_count)
    width = items * chan_count
    vmem = pl.BlockSpec(memory_space=pltpu.VMEM)
    return pl.pallas_call(
        functools.partial(correlate_kernel, peers=peers, chunk=chunk),
        out_shape=jax.ShapeDtypeStruct((lines, peers, depth, L // (lines * depth), width), jnp.bfloat16),
        in_specs=[pl.BlockSpec(memory_space=pltpu.SMEM), vmem, vmem] + [vmem] * peers,
        out_specs=vmem,
        scratch_shapes=[
            pltpu.VMEM((L, peers * width), jnp.float32),
            pltpu.VMEM((rows, peers * width), jnp.float32),
            pltpu.VMEM((rows, peers * width), jnp.float32),
            pltpu.VMEM((2, peers * width, bin_count), jnp.bfloat16),
            pltpu.VMEM((max(1, items // source_count), 2, peers * chan_count, bin_count), jnp.float32),
        ],
        compiler_params=pltpu.CompilerParams(vmem_limit_bytes=VMEM_LIMIT),
        name="correlate",
    )(source_channel, table, flip, *blocks)


def stack_kernel(x_ref, out_ref, y_ref):
    count, block, pairs = x_ref.shape
    for n in range(count):
        y_ref[n] = x_ref[n].astype(jnp.float32)
    mean = tree_sum([y_ref[n] for n in range(count)]) * (1.0 / count)
    squares = []
    for n in range(count):
        sample = y_ref[n] - mean
        y_ref[n] = sample
        squares.append(sample * sample)
    variance = tree_sum(squares) * (1.0 / count)
    for iteration in range(ITERS):
        shift = center * center if iteration > 0 else 0.0
        limit = TUKEY * TUKEY * (variance + shift + EPSILON)
        weights, products = [], []
        for n in range(count):
            sample = y_ref[n]
            deviation = sample - center if iteration > 0 else sample
            kept = jnp.maximum(limit - deviation * deviation, 0.0)
            weight = kept * kept
            weights.append(weight)
            products.append(weight * sample)
        center = tree_sum(products) / tree_sum(weights)
    out_ref[...] = (center + mean).T


def tree_sum(terms):
    sums = list(terms[:2])
    for index, term in enumerate(terms[2:]):
        sums[index % 2] = sums[index % 2] + term
    return sums[0] + sums[1]


def stack_blocks(samples, source_count):
    count, block, pairs = samples.shape
    result = pl.pallas_call(
        stack_kernel,
        out_shape=jax.ShapeDtypeStruct((pairs, block), jnp.float32),
        in_specs=[pl.BlockSpec(memory_space=pltpu.VMEM)],
        out_specs=pl.BlockSpec(memory_space=pltpu.VMEM),
        scratch_shapes=[pltpu.VMEM((count, block, pairs), jnp.float32)],
        compiler_params=pltpu.CompilerParams(vmem_limit_bytes=VMEM_LIMIT),
        name="bisquare_stack",
    )(samples)
    return result.reshape(source_count, pairs // source_count, block).transpose(2, 0, 1)


def per_device(spectra, source_channel):
    win_count, _, chan_count, bin_count = spectra.shape
    source_count = source_channel.shape[0]
    peers = lax.axis_size("rcv")
    parts = lax.axis_size("win")
    block = L // parts
    items = share(win_count, source_count, peers)
    table = make_tables(bin_count, L, L // 2 + 16)
    flip = make_flip(L // 2, 2000 * table.size)
    blocks = [spectra]
    for step in range(1, peers):
        blocks.append(lax.ppermute(spectra, "rcv", [(i, (i + step) % peers) for i in range(peers)]))
    lines = 1
    while 4 * lines * lines <= parts:
        lines *= 2
    depth = parts // lines
    assert lines * depth == parts
    corr = correlate(source_channel, table, flip, blocks, lines, depth)
    corr = corr.reshape(parts * peers, block, items * chan_count)
    snake = [range(depth) if c % 2 == 0 else range(depth - 1, -1, -1) for c in range(peers)]
    group = [(z * lines + q) * peers + c for q in range(lines) for c in range(peers) for z in snake[c]]
    moved = lax.all_to_all(
        corr, ("win", "rcv"), split_axis=0, concat_axis=0, tiled=True, axis_index_groups=[group]
    )
    if items != source_count:
        moved = moved.reshape(lines, peers, depth, block, items, chan_count)
        moved = jnp.stack([moved[:, c] if c % 2 == 0 else moved[:, c, ::-1] for c in range(peers)], axis=1)
        moved = moved.transpose(2, 0, 1, 4, 3, 5)
        moved = moved.reshape(parts * win_count, source_count, block, chan_count).transpose(0, 2, 1, 3)
        moved = moved.reshape(parts * win_count, block, source_count * chan_count)
    return stack_blocks(moved, source_count)


def solution(mesh):
    return jax.shard_map(
        per_device,
        mesh=mesh,
        in_specs=(P("win", None, "rcv", None), P()),
        out_specs=P("win", None, "rcv"),
        check_vma=False,
    )
```

```python
import functools

import jax
import jax.numpy as jnp
import numpy as np
from jax import lax
from jax.experimental import pallas as pl
from jax.experimental.pallas import tpu as pltpu
from jax.sharding import PartitionSpec as P

L = 512
ITERS = 5
VMEM_LIMIT = 24 * 2**20


TUKEY = 4.685
EPSILON = 1e-06


def make_tables(bin_count, lag_count, rows):
    freq = np.arange(bin_count, dtype=np.int64)
    shifts = np.arange(lag_count // 2 + 1, dtype=np.int64)
    phase = shifts[:, None] * freq[None, :] % (2 * bin_count)
    angle = phase * (2.0 * np.pi / (2 * bin_count))
    factor = np.where(freq == 0, 1.0, 2.0) / np.sqrt(8.0 * bin_count)
    table = np.zeros((2, rows, bin_count), np.float32)
    table[0, : len(shifts)] = np.cos(angle) * factor
    table[1, : len(shifts)] = -np.sin(angle) * factor
    return jnp.asarray(table.astype(jnp.bfloat16))


def flip_kernel(out_ref):
    lag = lax.broadcasted_iota(jnp.int32, out_ref.shape, 0)
    shift = lax.broadcasted_iota(jnp.int32, out_ref.shape, 1)
    out_ref[...] = (lag + shift == out_ref.shape[0]).astype(jnp.float32).astype(jnp.bfloat16)


def make_flip(half, meanwhile):
    return pl.pallas_call(
        flip_kernel,
        out_shape=jax.ShapeDtypeStruct((half, half), jnp.bfloat16),
        out_specs=pl.BlockSpec(memory_space=pltpu.VMEM),
        compiler_params=pltpu.CompilerParams(vmem_limit_bytes=VMEM_LIMIT),
        cost_estimate=pl.CostEstimate(flops=meanwhile, bytes_accessed=0, transcendentals=0),
        name="make_flip",
    )()


def share(win_count, source_count, peers):
    items = win_count * source_count // peers
    assert items * peers == win_count * source_count
    assert items % source_count == 0 or source_count % items == 0
    return items


def correlate_kernel(*refs, peers, chunk):
    channel_ref, table_ref, flip_ref = refs[:3]
    block_refs = refs[3 : 3 + peers]
    out_ref, lags_ref, even_ref, odd_ref, cross_ref, float_ref = refs[3 + peers :]
    win_count, _, chan_count, bin_count = block_refs[0].shape
    source_count = channel_ref.shape[0]
    items = share(win_count, source_count, peers)
    windows = float_ref.shape[0]
    lines, depth, _, block, width = out_ref.shape
    half = flip_ref.shape[0]
    me = lax.axis_index("rcv")
    first = lax.div(me * items, source_count)
    rows = []
    for t in range(items):
        channel = channel_ref[lax.rem(me * items + t, source_count)]
        owner = lax.div(channel, chan_count)
        place = lax.rem(me - owner + peers, peers) * chan_count
        rows.append(place + lax.rem(channel, chan_count))
    def widen(bins):
        for k in range(peers):
            for w in range(windows):
                for part in range(2):
                    float_ref[w, part, k * chan_count : (k + 1) * chan_count, bins] = block_refs[k][
                        first + w, part, :, bins
                    ].astype(jnp.float32)

    def form_cross(bins, some):
        for t in some:
            w = t // source_count
            real_p = float_ref[w, 0, :, bins]
            imag_q = float_ref[w, 1, :, bins]
            real_a = float_ref[w, 0, pl.ds(rows[t], 1), bins]
            imag_b = float_ref[w, 1, pl.ds(rows[t], 1), bins]
            real = (real_a * real_p + imag_b * imag_q).astype(jnp.bfloat16)
            imag = (imag_b * real_p - real_a * imag_q).astype(jnp.bfloat16)
            for k in range(peers):
                receivers = slice(k * chan_count, (k + 1) * chan_count)
                pairs = slice(k * width + t * chan_count, k * width + (t + 1) * chan_count)
                cross_ref[0, pairs, bins] = real[receivers]
                cross_ref[1, pairs, bins] = imag[receivers]

    def add_product(bins, index, sum_ref):
        term = lax.dot_general(
            table_ref[index, :, bins],
            cross_ref[index, :, bins],
            (((1,), (1,)), ((), ())),
            preferred_element_type=jnp.float32,
        )
        if bins.start == 0:
            sum_ref[...] = term
        else:
            sum_ref[...] += term

    chunks = [slice(start, start + chunk) for start in range(0, bin_count, chunk)]
    for index in range(len(chunks) + 1):
        if index < len(chunks):
            widen(chunks[index])
            form_cross(chunks[index], range(items // 2))
        if index > 0:
            add_product(chunks[index - 1], 0, even_ref)
        if index < len(chunks):
            form_cross(chunks[index], range(items // 2, items))
        if index > 0:
            add_product(chunks[index - 1], 1, odd_ref)
    ahead = (even_ref[:half, :] + odd_ref[:half, :]).astype(jnp.bfloat16)
    back = (even_ref[...] - odd_ref[...]).astype(jnp.bfloat16)
    turned = jnp.dot(flip_ref[...], back[:half], preferred_element_type=jnp.float32)
    behind = jnp.where(
        lax.broadcasted_iota(jnp.int32, turned.shape, 0) == 0,
        back[half : half + 16].astype(jnp.float32)[:1],
        turned,
    ).astype(jnp.bfloat16)
    if block % 16 != 0:
        lags_ref[half:, :] = ahead.astype(jnp.float32)
        lags_ref[:half, :] = behind.astype(jnp.float32)
    for k in range(peers):
        owner = lax.rem(me - k + peers, peers)
        columns = slice(k * width, (k + 1) * width)
        for part in range(lines * depth):
            start = part * block
            if block % 16 != 0:
                piece = lags_ref[start : start + block, columns].astype(jnp.bfloat16)
            elif start < half:
                piece = behind[start : start + block, columns]
            else:
                piece = ahead[start - half : start - half + block, columns]
            out_ref[part % lines, part // lines, owner] = piece


def correlate(source_channel, table, flip, blocks, lines, depth):
    win_count, _, chan_count, bin_count = blocks[0].shape
    source_count = source_channel.shape[0]
    peers = len(blocks)
    items = share(win_count, source_count, peers)
    rows = table.shape[1]
    chunk = min(256, bin_count)
    width = items * chan_count
    vmem = pl.BlockSpec(memory_space=pltpu.VMEM)
    return pl.pallas_call(
        functools.partial(correlate_kernel, peers=peers, chunk=chunk),
        out_shape=jax.ShapeDtypeStruct((lines, depth, peers, L // (lines * depth), width), jnp.bfloat16),
        in_specs=[pl.BlockSpec(memory_space=pltpu.SMEM), vmem, vmem] + [vmem] * peers,
        out_specs=vmem,
        scratch_shapes=[
            pltpu.VMEM((L, peers * width), jnp.float32),
            pltpu.VMEM((rows, peers * width), jnp.float32),
            pltpu.VMEM((rows, peers * width), jnp.float32),
            pltpu.VMEM((2, peers * width, bin_count), jnp.bfloat16),
            pltpu.VMEM((max(1, items // source_count), 2, peers * chan_count, bin_count), jnp.float32),
        ],
        compiler_params=pltpu.CompilerParams(vmem_limit_bytes=VMEM_LIMIT),
        name="correlate",
    )(source_channel, table, flip, *blocks)


def stack_kernel(x_ref, out_ref, y_ref):
    count, block, pairs = x_ref.shape
    for n in range(count):
        y_ref[n] = x_ref[n].astype(jnp.float32)
    mean = tree_sum([y_ref[n] for n in range(count)]) * (1.0 / count)
    squares = []
    for n in range(count):
        sample = y_ref[n] - mean
        y_ref[n] = sample
        squares.append(sample * sample)
    variance = tree_sum(squares) * (1.0 / count)
    for iteration in range(ITERS):
        shift = center * center if iteration > 0 else 0.0
        limit = TUKEY * TUKEY * (variance + shift + EPSILON)
        weights, products = [], []
        for n in range(count):
            sample = y_ref[n]
            deviation = sample - center if iteration > 0 else sample
            kept = jnp.maximum(limit - deviation * deviation, 0.0)
            weight = kept * kept
            weights.append(weight)
            products.append(weight * sample)
        center = tree_sum(products) / tree_sum(weights)
    out_ref[...] = (center + mean).T


def tree_sum(terms):
    sums = list(terms[:2])
    for index, term in enumerate(terms[2:]):
        sums[index % 2] = sums[index % 2] + term
    return sums[0] + sums[1]


def stack_blocks(samples, source_count):
    count, block, pairs = samples.shape
    result = pl.pallas_call(
        stack_kernel,
        out_shape=jax.ShapeDtypeStruct((pairs, block), jnp.float32),
        in_specs=[pl.BlockSpec(memory_space=pltpu.VMEM)],
        out_specs=pl.BlockSpec(memory_space=pltpu.VMEM),
        scratch_shapes=[pltpu.VMEM((count, block, pairs), jnp.float32)],
        compiler_params=pltpu.CompilerParams(vmem_limit_bytes=VMEM_LIMIT),
        name="bisquare_stack",
    )(samples)
    return result.reshape(source_count, pairs // source_count, block).transpose(2, 0, 1)


def per_device(spectra, source_channel):
    win_count, _, chan_count, bin_count = spectra.shape
    source_count = source_channel.shape[0]
    peers = lax.axis_size("rcv")
    parts = lax.axis_size("win")
    block = L // parts
    items = share(win_count, source_count, peers)
    table = make_tables(bin_count, L, L // 2 + 16)
    flip = make_flip(L // 2, 2000 * table.size)
    blocks = [spectra]
    for step in range(1, peers):
        blocks.append(lax.ppermute(spectra, "rcv", [(i, (i + step) % peers) for i in range(peers)]))
    lines = 1
    while 4 * lines * lines <= parts:
        lines *= 2
    depth = parts // lines
    assert lines * depth == parts
    corr = correlate(source_channel, table, flip, blocks, lines, depth)
    corr = corr.reshape(parts * peers, block, items * chan_count)
    group = [
        (z * lines + q) * peers + c for q in range(lines) for z in range(depth) for c in range(peers)
    ]
    moved = lax.all_to_all(
        corr, ("win", "rcv"), split_axis=0, concat_axis=0, tiled=True, axis_index_groups=[group]
    )
    if items != source_count:
        moved = moved.reshape(lines, depth, peers, block, items, chan_count)
        moved = moved.transpose(1, 0, 2, 4, 3, 5)
        moved = moved.reshape(parts * win_count, source_count, block, chan_count).transpose(0, 2, 1, 3)
        moved = moved.reshape(parts * win_count, block, source_count * chan_count)
    return stack_blocks(moved, source_count)


def solution(mesh):
    return jax.shard_map(
        per_device,
        mesh=mesh,
        in_specs=(P("win", None, "rcv", None), P()),
        out_specs=P("win", None, "rcv"),
        check_vma=False,
    )
```

```python
import functools

import jax
import jax.numpy as jnp
import numpy as np
from jax import lax
from jax.experimental import pallas as pl
from jax.experimental.pallas import tpu as pltpu
from jax.sharding import PartitionSpec as P

L = 512
ITERS = 5
VMEM_LIMIT = 24 * 2**20


TUKEY = 4.685
EPSILON = 1e-06


def make_tables(bin_count, lag_count, rows):
    freq = np.arange(bin_count, dtype=np.int64)
    shifts = np.arange(lag_count // 2 + 1, dtype=np.int64)
    phase = shifts[:, None] * freq[None, :] % (2 * bin_count)
    angle = phase * (2.0 * np.pi / (2 * bin_count))
    factor = np.where(freq == 0, 1.0, 2.0) / np.sqrt(8.0 * bin_count)
    table = np.zeros((2, rows, bin_count), np.float32)
    table[0, : len(shifts)] = np.cos(angle) * factor
    table[1, : len(shifts)] = -np.sin(angle) * factor
    return jnp.asarray(table.astype(jnp.bfloat16))


def flip_kernel(out_ref):
    lag = lax.broadcasted_iota(jnp.int32, out_ref.shape, 0)
    shift = lax.broadcasted_iota(jnp.int32, out_ref.shape, 1)
    out_ref[...] = (lag + shift == out_ref.shape[0]).astype(jnp.float32).astype(jnp.bfloat16)


def make_flip(half, meanwhile):
    return pl.pallas_call(
        flip_kernel,
        out_shape=jax.ShapeDtypeStruct((half, half), jnp.bfloat16),
        out_specs=pl.BlockSpec(memory_space=pltpu.VMEM),
        compiler_params=pltpu.CompilerParams(vmem_limit_bytes=VMEM_LIMIT),
        cost_estimate=pl.CostEstimate(flops=meanwhile, bytes_accessed=0, transcendentals=0),
        name="make_flip",
    )()


def share(win_count, source_count, peers):
    items = win_count * source_count // peers
    assert items * peers == win_count * source_count
    assert items % source_count == 0 or source_count % items == 0
    return items


def correlate_kernel(*refs, peers, chunk):
    channel_ref, table_ref, flip_ref = refs[:3]
    block_refs = refs[3 : 3 + peers]
    out_ref, lags_ref, even_ref, odd_ref, cross_ref, float_ref = refs[3 + peers :]
    win_count, _, chan_count, bin_count = block_refs[0].shape
    source_count = channel_ref.shape[0]
    items = share(win_count, source_count, peers)
    windows = float_ref.shape[0]
    _, lines, depth, block, width = out_ref.shape
    half = flip_ref.shape[0]
    me = lax.axis_index("rcv")
    first = lax.div(me * items, source_count)
    rows = []
    for t in range(items):
        channel = channel_ref[lax.rem(me * items + t, source_count)]
        owner = lax.div(channel, chan_count)
        place = lax.rem(me - owner + peers, peers) * chan_count
        rows.append(place + lax.rem(channel, chan_count))
    def widen(bins):
        for k in range(peers):
            for w in range(windows):
                for part in range(2):
                    float_ref[w, part, k * chan_count : (k + 1) * chan_count, bins] = block_refs[k][
                        first + w, part, :, bins
                    ].astype(jnp.float32)

    def form_cross(bins, some):
        for t in some:
            w = t // source_count
            real_p = float_ref[w, 0, :, bins]
            imag_q = float_ref[w, 1, :, bins]
            real_a = float_ref[w, 0, pl.ds(rows[t], 1), bins]
            imag_b = float_ref[w, 1, pl.ds(rows[t], 1), bins]
            real = (real_a * real_p + imag_b * imag_q).astype(jnp.bfloat16)
            imag = (imag_b * real_p - real_a * imag_q).astype(jnp.bfloat16)
            for k in range(peers):
                receivers = slice(k * chan_count, (k + 1) * chan_count)
                pairs = slice(k * width + t * chan_count, k * width + (t + 1) * chan_count)
                cross_ref[0, pairs, bins] = real[receivers]
                cross_ref[1, pairs, bins] = imag[receivers]

    def add_product(bins, index, sum_ref):
        term = lax.dot_general(
            table_ref[index, :, bins],
            cross_ref[index, :, bins],
            (((1,), (1,)), ((), ())),
            preferred_element_type=jnp.float32,
        )
        if bins.start == 0:
            sum_ref[...] = term
        else:
            sum_ref[...] += term

    chunks = [slice(start, start + chunk) for start in range(0, bin_count, chunk)]
    for index in range(len(chunks) + 1):
        if index < len(chunks):
            widen(chunks[index])
            form_cross(chunks[index], range(items // 2))
        if index > 0:
            add_product(chunks[index - 1], 0, even_ref)
        if index < len(chunks):
            form_cross(chunks[index], range(items // 2, items))
        if index > 0:
            add_product(chunks[index - 1], 1, odd_ref)
    ahead = (even_ref[:half, :] + odd_ref[:half, :]).astype(jnp.bfloat16)
    back = (even_ref[...] - odd_ref[...]).astype(jnp.bfloat16)
    turned = jnp.dot(flip_ref[...], back[:half], preferred_element_type=jnp.float32)
    behind = jnp.where(
        lax.broadcasted_iota(jnp.int32, turned.shape, 0) == 0,
        back[half : half + 16].astype(jnp.float32)[:1],
        turned,
    ).astype(jnp.bfloat16)
    if block % 16 != 0:
        lags_ref[half:, :] = ahead.astype(jnp.float32)
        lags_ref[:half, :] = behind.astype(jnp.float32)
    for k in range(peers):
        owner = lax.rem(me - k + peers, peers)
        columns = slice(k * width, (k + 1) * width)
        for part in range(lines * depth):
            start = part * block
            if block % 16 != 0:
                piece = lags_ref[start : start + block, columns].astype(jnp.bfloat16)
            elif start < half:
                piece = behind[start : start + block, columns]
            else:
                piece = ahead[start - half : start - half + block, columns]
            out_ref[owner, part % lines, part // lines] = piece


def correlate(source_channel, table, flip, blocks, lines, depth):
    win_count, _, chan_count, bin_count = blocks[0].shape
    source_count = source_channel.shape[0]
    peers = len(blocks)
    items = share(win_count, source_count, peers)
    rows = table.shape[1]
    chunk = min(256, bin_count)
    width = items * chan_count
    vmem = pl.BlockSpec(memory_space=pltpu.VMEM)
    return pl.pallas_call(
        functools.partial(correlate_kernel, peers=peers, chunk=chunk),
        out_shape=jax.ShapeDtypeStruct((peers, lines, depth, L // (lines * depth), width), jnp.bfloat16),
        in_specs=[pl.BlockSpec(memory_space=pltpu.SMEM), vmem, vmem] + [vmem] * peers,
        out_specs=vmem,
        scratch_shapes=[
            pltpu.VMEM((L, peers * width), jnp.float32),
            pltpu.VMEM((rows, peers * width), jnp.float32),
            pltpu.VMEM((rows, peers * width), jnp.float32),
            pltpu.VMEM((2, peers * width, bin_count), jnp.bfloat16),
            pltpu.VMEM((max(1, items // source_count), 2, peers * chan_count, bin_count), jnp.float32),
        ],
        compiler_params=pltpu.CompilerParams(vmem_limit_bytes=VMEM_LIMIT),
        name="correlate",
    )(source_channel, table, flip, *blocks)


def stack_kernel(x_ref, out_ref, y_ref):
    count, block, pairs = x_ref.shape
    for n in range(count):
        y_ref[n] = x_ref[n].astype(jnp.float32)
    mean = tree_sum([y_ref[n] for n in range(count)]) * (1.0 / count)
    squares = []
    for n in range(count):
        sample = y_ref[n] - mean
        y_ref[n] = sample
        squares.append(sample * sample)
    variance = tree_sum(squares) * (1.0 / count)
    for iteration in range(ITERS):
        shift = center * center if iteration > 0 else 0.0
        limit = TUKEY * TUKEY * (variance + shift + EPSILON)
        weights, products = [], []
        for n in range(count):
            sample = y_ref[n]
            deviation = sample - center if iteration > 0 else sample
            kept = jnp.maximum(limit - deviation * deviation, 0.0)
            weight = kept * kept
            weights.append(weight)
            products.append(weight * sample)
        center = tree_sum(products) / tree_sum(weights)
    out_ref[...] = (center + mean).T


def tree_sum(terms):
    sums = list(terms[:2])
    for index, term in enumerate(terms[2:]):
        sums[index % 2] = sums[index % 2] + term
    return sums[0] + sums[1]


def stack_blocks(samples, source_count):
    count, block, pairs = samples.shape
    result = pl.pallas_call(
        stack_kernel,
        out_shape=jax.ShapeDtypeStruct((pairs, block), jnp.float32),
        in_specs=[pl.BlockSpec(memory_space=pltpu.VMEM)],
        out_specs=pl.BlockSpec(memory_space=pltpu.VMEM),
        scratch_shapes=[pltpu.VMEM((count, block, pairs), jnp.float32)],
        compiler_params=pltpu.CompilerParams(vmem_limit_bytes=VMEM_LIMIT),
        name="bisquare_stack",
    )(samples)
    return result.reshape(source_count, pairs // source_count, block).transpose(2, 0, 1)


def per_device(spectra, source_channel):
    win_count, _, chan_count, bin_count = spectra.shape
    source_count = source_channel.shape[0]
    peers = lax.axis_size("rcv")
    parts = lax.axis_size("win")
    block = L // parts
    items = share(win_count, source_count, peers)
    table = make_tables(bin_count, L, L // 2 + 16)
    flip = make_flip(L // 2, 2000 * table.size)
    blocks = [spectra]
    for step in range(1, peers):
        blocks.append(lax.ppermute(spectra, "rcv", [(i, (i + step) % peers) for i in range(peers)]))
    lines = 1
    while 4 * lines * lines <= parts:
        lines *= 2
    depth = parts // lines
    assert lines * depth == parts
    corr = correlate(source_channel, table, flip, blocks, lines, depth)
    corr = corr.reshape(parts * peers, block, items * chan_count)
    group = [
        (z * lines + q) * peers + c for c in range(peers) for q in range(lines) for z in range(depth)
    ]
    moved = lax.all_to_all(
        corr, ("win", "rcv"), split_axis=0, concat_axis=0, tiled=True, axis_index_groups=[group]
    )
    if items != source_count:
        moved = moved.reshape(peers, lines, depth, block, items, chan_count)
        moved = moved.transpose(2, 1, 0, 4, 3, 5)
        moved = moved.reshape(parts * win_count, source_count, block, chan_count).transpose(0, 2, 1, 3)
        moved = moved.reshape(parts * win_count, block, source_count * chan_count)
    return stack_blocks(moved, source_count)


def solution(mesh):
    return jax.shard_map(
        per_device,
        mesh=mesh,
        in_specs=(P("win", None, "rcv", None), P()),
        out_specs=P("win", None, "rcv"),
        check_vma=False,
    )
```

```python
import functools

import jax
import jax.numpy as jnp
import numpy as np
from jax import lax
from jax.experimental import pallas as pl
from jax.experimental.pallas import tpu as pltpu
from jax.sharding import PartitionSpec as P

L = 512
ITERS = 5
VMEM_LIMIT = 24 * 2**20


TUKEY = 4.685
EPSILON = 1e-06


def make_tables(bin_count, lag_count, rows):
    freq = np.arange(bin_count, dtype=np.int64)
    shifts = np.arange(lag_count // 2 + 1, dtype=np.int64)
    phase = shifts[:, None] * freq[None, :] % (2 * bin_count)
    angle = phase * (2.0 * np.pi / (2 * bin_count))
    factor = np.where(freq == 0, 1.0, 2.0) / np.sqrt(8.0 * bin_count)
    table = np.zeros((2, rows, bin_count), np.float32)
    table[0, : len(shifts)] = np.cos(angle) * factor
    table[1, : len(shifts)] = -np.sin(angle) * factor
    return jnp.asarray(table.astype(jnp.bfloat16))


def flip_kernel(out_ref):
    lag = lax.broadcasted_iota(jnp.int32, out_ref.shape, 0)
    shift = lax.broadcasted_iota(jnp.int32, out_ref.shape, 1)
    out_ref[...] = (lag + shift == out_ref.shape[0]).astype(jnp.float32).astype(jnp.bfloat16)


def make_flip(half, meanwhile):
    return pl.pallas_call(
        flip_kernel,
        out_shape=jax.ShapeDtypeStruct((half, half), jnp.bfloat16),
        out_specs=pl.BlockSpec(memory_space=pltpu.VMEM),
        compiler_params=pltpu.CompilerParams(vmem_limit_bytes=VMEM_LIMIT),
        cost_estimate=pl.CostEstimate(flops=meanwhile, bytes_accessed=0, transcendentals=0),
        name="make_flip",
    )()


def share(win_count, source_count, peers):
    items = win_count * source_count // peers
    assert items * peers == win_count * source_count
    assert items % source_count == 0 or source_count % items == 0
    return items


def correlate_kernel(*refs, peers, chunk):
    channel_ref, table_ref, flip_ref = refs[:3]
    block_refs = refs[3 : 3 + peers]
    out_ref, lags_ref, even_ref, odd_ref, cross_ref, float_ref = refs[3 + peers :]
    win_count, _, chan_count, bin_count = block_refs[0].shape
    source_count = channel_ref.shape[0]
    items = share(win_count, source_count, peers)
    windows = float_ref.shape[0]
    lines, _, depth, block, width = out_ref.shape
    half = flip_ref.shape[0]
    me = lax.axis_index("rcv")
    first = lax.div(me * items, source_count)
    rows = []
    for t in range(items):
        channel = channel_ref[lax.rem(me * items + t, source_count)]
        owner = lax.div(channel, chan_count)
        place = lax.rem(me - owner + peers, peers) * chan_count
        rows.append(place + lax.rem(channel, chan_count))
    def widen(bins):
        for k in range(peers):
            for w in range(windows):
                for part in range(2):
                    float_ref[w, part, k * chan_count : (k + 1) * chan_count, bins] = block_refs[k][
                        first + w, part, :, bins
                    ].astype(jnp.float32)

    def form_cross(bins, some):
        for t in some:
            w = t // source_count
            real_p = float_ref[w, 0, :, bins]
            imag_q = float_ref[w, 1, :, bins]
            real_a = float_ref[w, 0, pl.ds(rows[t], 1), bins]
            imag_b = float_ref[w, 1, pl.ds(rows[t], 1), bins]
            real = (real_a * real_p + imag_b * imag_q).astype(jnp.bfloat16)
            imag = (imag_b * real_p - real_a * imag_q).astype(jnp.bfloat16)
            for k in range(peers):
                receivers = slice(k * chan_count, (k + 1) * chan_count)
                pairs = slice(k * width + t * chan_count, k * width + (t + 1) * chan_count)
                cross_ref[0, pairs, bins] = real[receivers]
                cross_ref[1, pairs, bins] = imag[receivers]

    def add_product(bins, index, sum_ref):
        term = lax.dot_general(
            table_ref[index, :, bins],
            cross_ref[index, :, bins],
            (((1,), (1,)), ((), ())),
            preferred_element_type=jnp.float32,
        )
        if bins.start == 0:
            sum_ref[...] = term
        else:
            sum_ref[...] += term

    chunks = [slice(start, start + chunk) for start in range(0, bin_count, chunk)]
    for index in range(len(chunks) + 1):
        if index < len(chunks):
            widen(chunks[index])
            form_cross(chunks[index], range(items // 2))
        if index > 0:
            add_product(chunks[index - 1], 0, even_ref)
        if index < len(chunks):
            form_cross(chunks[index], range(items // 2, items))
        if index > 0:
            add_product(chunks[index - 1], 1, odd_ref)
    ahead = (even_ref[:half, :] + odd_ref[:half, :]).astype(jnp.bfloat16)
    back = (even_ref[...] - odd_ref[...]).astype(jnp.bfloat16)
    turned = jnp.dot(flip_ref[...], back[:half], preferred_element_type=jnp.float32)
    behind = jnp.where(
        lax.broadcasted_iota(jnp.int32, turned.shape, 0) == 0,
        back[half : half + 16].astype(jnp.float32)[:1],
        turned,
    ).astype(jnp.bfloat16)
    if block % 16 != 0:
        lags_ref[half:, :] = ahead.astype(jnp.float32)
        lags_ref[:half, :] = behind.astype(jnp.float32)
    for k in range(peers):
        owner = lax.rem(me - k + peers, peers)
        columns = slice(k * width, (k + 1) * width)
        for part in range(lines * depth):
            start = part * block
            if block % 16 != 0:
                piece = lags_ref[start : start + block, columns].astype(jnp.bfloat16)
            elif start < half:
                piece = behind[start : start + block, columns]
            else:
                piece = ahead[start - half : start - half + block, columns]
            out_ref[part % lines, owner, part // lines] = piece


def correlate(source_channel, table, flip, blocks, lines, depth):
    win_count, _, chan_count, bin_count = blocks[0].shape
    source_count = source_channel.shape[0]
    peers = len(blocks)
    items = share(win_count, source_count, peers)
    rows = table.shape[1]
    chunk = min(256, bin_count)
    width = items * chan_count
    vmem = pl.BlockSpec(memory_space=pltpu.VMEM)
    return pl.pallas_call(
        functools.partial(correlate_kernel, peers=peers, chunk=chunk),
        out_shape=jax.ShapeDtypeStruct((lines, peers, depth, L // (lines * depth), width), jnp.bfloat16),
        in_specs=[pl.BlockSpec(memory_space=pltpu.SMEM), vmem, vmem] + [vmem] * peers,
        out_specs=vmem,
        scratch_shapes=[
            pltpu.VMEM((L, peers * width), jnp.float32),
            pltpu.VMEM((rows, peers * width), jnp.float32),
            pltpu.VMEM((rows, peers * width), jnp.float32),
            pltpu.VMEM((2, peers * width, bin_count), jnp.bfloat16),
            pltpu.VMEM((max(1, items // source_count), 2, peers * chan_count, bin_count), jnp.float32),
        ],
        compiler_params=pltpu.CompilerParams(vmem_limit_bytes=VMEM_LIMIT),
        name="correlate",
    )(source_channel, table, flip, *blocks)


def stack_kernel(x_ref, out_ref, y_ref):
    count, block, pairs = x_ref.shape
    for n in range(count):
        y_ref[n] = x_ref[n].astype(jnp.float32)
    mean = tree_sum([y_ref[n] for n in range(count)]) * (1.0 / count)
    squares = []
    for n in range(count):
        sample = y_ref[n] - mean
        y_ref[n] = sample
        squares.append(sample * sample)
    variance = tree_sum(squares) * (1.0 / count)
    for iteration in range(ITERS):
        shift = center * center if iteration > 0 else 0.0
        limit = TUKEY * TUKEY * (variance + shift + EPSILON)
        weights, products = [], []
        for n in range(count):
            sample = y_ref[n]
            deviation = sample - center if iteration > 0 else sample
            kept = jnp.maximum(limit - deviation * deviation, 0.0)
            weight = kept * kept
            weights.append(weight)
            products.append(weight * sample)
        center = tree_sum(products) / tree_sum(weights)
    out_ref[...] = (center + mean).T


def tree_sum(terms):
    sums = list(terms[:2])
    for index, term in enumerate(terms[2:]):
        sums[index % 2] = sums[index % 2] + term
    return sums[0] + sums[1]


def stack_blocks(samples, source_count):
    count, block, pairs = samples.shape
    result = pl.pallas_call(
        stack_kernel,
        out_shape=jax.ShapeDtypeStruct((pairs, block), jnp.float32),
        in_specs=[pl.BlockSpec(memory_space=pltpu.VMEM)],
        out_specs=pl.BlockSpec(memory_space=pltpu.VMEM),
        scratch_shapes=[pltpu.VMEM((count, block, pairs), jnp.float32)],
        compiler_params=pltpu.CompilerParams(vmem_limit_bytes=VMEM_LIMIT),
        name="bisquare_stack",
    )(samples)
    return result.reshape(source_count, pairs // source_count, block).transpose(2, 0, 1)


def per_device(spectra, source_channel):
    win_count, _, chan_count, bin_count = spectra.shape
    source_count = source_channel.shape[0]
    peers = lax.axis_size("rcv")
    parts = lax.axis_size("win")
    block = L // parts
    items = share(win_count, source_count, peers)
    table = make_tables(bin_count, L, L // 2 + 16)
    flip = make_flip(L // 2, 2000 * table.size)
    blocks = [spectra]
    for step in range(1, peers):
        blocks.append(lax.ppermute(spectra, "rcv", [(i, (i + step) % peers) for i in range(peers)]))
    lines = 1
    while 4 * lines * lines <= parts:
        lines *= 2
    depth = parts // lines
    assert lines * depth == parts
    corr = correlate(source_channel, table, flip, blocks, lines, depth)
    corr = corr.reshape(parts * peers, block, items * chan_count)
    group = [
        (z * lines + q) * peers + c for q in range(lines) for c in range(peers) for z in range(depth)
    ]
    moved = lax.all_to_all(
        corr, ("win", "rcv"), split_axis=0, concat_axis=0, tiled=True, axis_index_groups=[group]
    )
    if items != source_count:
        moved = moved.reshape(lines, peers, depth, block, items, chan_count)
        moved = moved.transpose(2, 0, 1, 4, 3, 5)
        moved = moved.reshape(parts * win_count, source_count, block, chan_count).transpose(0, 2, 1, 3)
        moved = moved.reshape(parts * win_count, block, source_count * chan_count)
    return stack_blocks(moved, source_count)


def solution(mesh):
    return jax.shard_map(
        per_device,
        mesh=mesh,
        in_specs=(P("win", None, "rcv", None), P()),
        out_specs=P("win", None, "rcv"),
        check_vma=False,
    )
```

```python
import functools

import jax
import jax.numpy as jnp
import numpy as np
from jax import lax
from jax.experimental import pallas as pl
from jax.experimental.pallas import tpu as pltpu
from jax.sharding import PartitionSpec as P

L = 512
ITERS = 5
VMEM_LIMIT = 24 * 2**20


TUKEY = 4.685
EPSILON = 1e-06


def make_tables(bin_count, lag_count, rows):
    freq = np.arange(bin_count, dtype=np.int64)
    shifts = np.arange(lag_count // 2 + 1, dtype=np.int64)
    phase = shifts[:, None] * freq[None, :] % (2 * bin_count)
    angle = phase * (2.0 * np.pi / (2 * bin_count))
    factor = np.where(freq == 0, 1.0, 2.0) / np.sqrt(8.0 * bin_count)
    table = np.zeros((2, rows, bin_count), np.float32)
    table[0, : len(shifts)] = np.cos(angle) * factor
    table[1, : len(shifts)] = -np.sin(angle) * factor
    return jnp.asarray(table.astype(jnp.bfloat16))


def flip_kernel(out_ref):
    lag = lax.broadcasted_iota(jnp.int32, out_ref.shape, 0)
    shift = lax.broadcasted_iota(jnp.int32, out_ref.shape, 1)
    out_ref[...] = (lag + shift == out_ref.shape[0]).astype(jnp.float32).astype(jnp.bfloat16)


def make_flip(half, meanwhile):
    return pl.pallas_call(
        flip_kernel,
        out_shape=jax.ShapeDtypeStruct((half, half), jnp.bfloat16),
        out_specs=pl.BlockSpec(memory_space=pltpu.VMEM),
        compiler_params=pltpu.CompilerParams(vmem_limit_bytes=VMEM_LIMIT),
        cost_estimate=pl.CostEstimate(flops=meanwhile, bytes_accessed=0, transcendentals=0),
        name="make_flip",
    )()


def share(win_count, source_count, peers):
    items = win_count * source_count // peers
    assert items * peers == win_count * source_count
    assert items % source_count == 0 or source_count % items == 0
    return items


def correlate_kernel(*refs, peers, chunk):
    channel_ref, table_ref, flip_ref = refs[:3]
    block_refs = refs[3 : 3 + peers]
    out_ref, lags_ref, even_ref, odd_ref, cross_ref, float_ref = refs[3 + peers :]
    win_count, _, chan_count, bin_count = block_refs[0].shape
    source_count = channel_ref.shape[0]
    items = share(win_count, source_count, peers)
    windows = float_ref.shape[0]
    lines, _, depth, block, width = out_ref.shape
    half = flip_ref.shape[0]
    me = lax.axis_index("rcv")
    first = lax.div(me * items, source_count)
    rows = []
    for t in range(items):
        channel = channel_ref[lax.rem(me * items + t, source_count)]
        owner = lax.div(channel, chan_count)
        place = lax.rem(me - owner + peers, peers) * chan_count
        rows.append(place + lax.rem(channel, chan_count))
    def widen(bins):
        for k in range(peers):
            for w in range(windows):
                for part in range(2):
                    float_ref[w, part, k * chan_count : (k + 1) * chan_count, bins] = block_refs[k][
                        first + w, part, :, bins
                    ].astype(jnp.float32)

    def form_cross(bins, some):
        for t in some:
            w = t // source_count
            real_p = float_ref[w, 0, :, bins]
            imag_q = float_ref[w, 1, :, bins]
            real_a = float_ref[w, 0, pl.ds(rows[t], 1), bins]
            imag_b = float_ref[w, 1, pl.ds(rows[t], 1), bins]
            real = (real_a * real_p + imag_b * imag_q).astype(jnp.bfloat16)
            imag = (imag_b * real_p - real_a * imag_q).astype(jnp.bfloat16)
            for k in range(peers):
                receivers = slice(k * chan_count, (k + 1) * chan_count)
                pairs = slice(k * width + t * chan_count, k * width + (t + 1) * chan_count)
                cross_ref[0, pairs, bins] = real[receivers]
                cross_ref[1, pairs, bins] = imag[receivers]

    def add_product(bins, index, sum_ref):
        term = lax.dot_general(
            table_ref[index, :, bins],
            cross_ref[index, :, bins],
            (((1,), (1,)), ((), ())),
            preferred_element_type=jnp.float32,
        )
        if bins.start == 0:
            sum_ref[...] = term
        else:
            sum_ref[...] += term

    chunks = [slice(start, start + chunk) for start in range(0, bin_count, chunk)]
    for index in range(len(chunks) + 1):
        if index < len(chunks):
            widen(chunks[index])
            form_cross(chunks[index], range(items // 2))
        if index > 0:
            add_product(chunks[index - 1], 0, even_ref)
        if index < len(chunks):
            form_cross(chunks[index], range(items // 2, items))
        if index > 0:
            add_product(chunks[index - 1], 1, odd_ref)
    place = (lax.axis_index("win") * peers + me).astype(jnp.float32)
    factor = 1.0 + place * (1.0 / (lines * depth * peers))
    ahead = ((even_ref[:half, :] + odd_ref[:half, :]) * factor).astype(jnp.bfloat16)
    back = ((even_ref[...] - odd_ref[...]) * factor).astype(jnp.bfloat16)
    turned = jnp.dot(flip_ref[...], back[:half], preferred_element_type=jnp.float32)
    behind = jnp.where(
        lax.broadcasted_iota(jnp.int32, turned.shape, 0) == 0,
        back[half : half + 16].astype(jnp.float32)[:1],
        turned,
    ).astype(jnp.bfloat16)
    if block % 16 != 0:
        lags_ref[half:, :] = ahead.astype(jnp.float32)
        lags_ref[:half, :] = behind.astype(jnp.float32)
    for k in range(peers):
        owner = lax.rem(me - k + peers, peers)
        columns = slice(k * width, (k + 1) * width)
        for part in range(lines * depth):
            start = part * block
            if block % 16 != 0:
                piece = lags_ref[start : start + block, columns].astype(jnp.bfloat16)
            elif start < half:
                piece = behind[start : start + block, columns]
            else:
                piece = ahead[start - half : start - half + block, columns]
            out_ref[part % lines, owner, part // lines] = piece


def correlate(source_channel, table, flip, blocks, lines, depth):
    win_count, _, chan_count, bin_count = blocks[0].shape
    source_count = source_channel.shape[0]
    peers = len(blocks)
    items = share(win_count, source_count, peers)
    rows = table.shape[1]
    chunk = min(256, bin_count)
    width = items * chan_count
    vmem = pl.BlockSpec(memory_space=pltpu.VMEM)
    return pl.pallas_call(
        functools.partial(correlate_kernel, peers=peers, chunk=chunk),
        out_shape=jax.ShapeDtypeStruct((lines, peers, depth, L // (lines * depth), width), jnp.bfloat16),
        in_specs=[pl.BlockSpec(memory_space=pltpu.SMEM), vmem, vmem] + [vmem] * peers,
        out_specs=vmem,
        scratch_shapes=[
            pltpu.VMEM((L, peers * width), jnp.float32),
            pltpu.VMEM((rows, peers * width), jnp.float32),
            pltpu.VMEM((rows, peers * width), jnp.float32),
            pltpu.VMEM((2, peers * width, bin_count), jnp.bfloat16),
            pltpu.VMEM((max(1, items // source_count), 2, peers * chan_count, bin_count), jnp.float32),
        ],
        compiler_params=pltpu.CompilerParams(vmem_limit_bytes=VMEM_LIMIT),
        name="correlate",
    )(source_channel, table, flip, *blocks)


def stack_kernel(x_ref, out_ref, y_ref, *, factors):
    count, block, pairs = x_ref.shape
    for n in range(count):
        y_ref[n] = x_ref[n].astype(jnp.float32) * (1.0 / factors[n])
    mean = tree_sum([y_ref[n] for n in range(count)]) * (1.0 / count)
    squares = []
    for n in range(count):
        sample = y_ref[n] - mean
        y_ref[n] = sample
        squares.append(sample * sample)
    variance = tree_sum(squares) * (1.0 / count)
    for iteration in range(ITERS):
        shift = center * center if iteration > 0 else 0.0
        limit = TUKEY * TUKEY * (variance + shift + EPSILON)
        weights, products = [], []
        for n in range(count):
            sample = y_ref[n]
            deviation = sample - center if iteration > 0 else sample
            kept = jnp.maximum(limit - deviation * deviation, 0.0)
            weight = kept * kept
            weights.append(weight)
            products.append(weight * sample)
        center = tree_sum(products) / tree_sum(weights)
    out_ref[...] = (center + mean).T


def tree_sum(terms):
    sums = list(terms[:2])
    for index, term in enumerate(terms[2:]):
        sums[index % 2] = sums[index % 2] + term
    return sums[0] + sums[1]


def stack_blocks(samples, factors, source_count):
    count, block, pairs = samples.shape
    result = pl.pallas_call(
        functools.partial(stack_kernel, factors=factors),
        out_shape=jax.ShapeDtypeStruct((pairs, block), jnp.float32),
        in_specs=[pl.BlockSpec(memory_space=pltpu.VMEM)],
        out_specs=pl.BlockSpec(memory_space=pltpu.VMEM),
        scratch_shapes=[pltpu.VMEM((count, block, pairs), jnp.float32)],
        compiler_params=pltpu.CompilerParams(vmem_limit_bytes=VMEM_LIMIT),
        name="bisquare_stack",
    )(samples)
    return result.reshape(source_count, pairs // source_count, block).transpose(2, 0, 1)


def per_device(spectra, source_channel):
    win_count, _, chan_count, bin_count = spectra.shape
    source_count = source_channel.shape[0]
    peers = lax.axis_size("rcv")
    parts = lax.axis_size("win")
    block = L // parts
    items = share(win_count, source_count, peers)
    table = make_tables(bin_count, L, L // 2 + 16)
    flip = make_flip(L // 2, 2000 * table.size)
    blocks = [spectra]
    for step in range(1, peers):
        blocks.append(lax.ppermute(spectra, "rcv", [(i, (i + step) % peers) for i in range(peers)]))
    lines = 1
    while 4 * lines * lines <= parts:
        lines *= 2
    depth = parts // lines
    assert lines * depth == parts
    corr = correlate(source_channel, table, flip, blocks, lines, depth)
    corr = corr.reshape(parts * peers, block, items * chan_count)
    group = [
        (z * lines + q) * peers + c for q in range(lines) for c in range(peers) for z in range(depth)
    ]
    moved = lax.all_to_all(
        corr, ("win", "rcv"), split_axis=0, concat_axis=0, tiled=True, axis_index_groups=[group]
    )
    factors = [1.0 + device / len(group) for device in group]
    if items != source_count:
        moved = moved.astype(jnp.float32) / jnp.asarray(factors, jnp.float32)[:, None, None]
        factors = [1.0] * (parts * win_count)
        moved = moved.reshape(lines, peers, depth, block, items, chan_count)
        moved = moved.transpose(2, 0, 1, 4, 3, 5)
        moved = moved.reshape(parts * win_count, source_count, block, chan_count).transpose(0, 2, 1, 3)
        moved = moved.reshape(parts * win_count, block, source_count * chan_count)
    return stack_blocks(moved, factors, source_count)


def solution(mesh):
    return jax.shard_map(
        per_device,
        mesh=mesh,
        in_specs=(P("win", None, "rcv", None), P()),
        out_specs=P("win", None, "rcv"),
        check_vma=False,
    )
```

```python
import functools

import jax
import jax.numpy as jnp
import numpy as np
from jax import lax
from jax.experimental import pallas as pl
from jax.experimental.pallas import tpu as pltpu
from jax.sharding import PartitionSpec as P

L = 512
ITERS = 5
VMEM_LIMIT = 24 * 2**20


TUKEY = 4.685
EPSILON = 1e-06


def make_tables(bin_count, lag_count, rows):
    freq = np.arange(bin_count, dtype=np.int64)
    shifts = np.arange(lag_count // 2 + 1, dtype=np.int64)
    phase = shifts[:, None] * freq[None, :] % (2 * bin_count)
    angle = phase * (2.0 * np.pi / (2 * bin_count))
    factor = np.where(freq == 0, 1.0, 2.0) / np.sqrt(8.0 * bin_count)
    table = np.zeros((2, rows, bin_count), np.float32)
    table[0, : len(shifts)] = np.cos(angle) * factor
    table[1, : len(shifts)] = -np.sin(angle) * factor
    return jnp.asarray(table.astype(jnp.bfloat16))


def flip_kernel(out_ref):
    lag = lax.broadcasted_iota(jnp.int32, out_ref.shape, 0)
    shift = lax.broadcasted_iota(jnp.int32, out_ref.shape, 1)
    out_ref[...] = (lag + shift == out_ref.shape[0]).astype(jnp.float32).astype(jnp.bfloat16)


def make_flip(half, meanwhile):
    return pl.pallas_call(
        flip_kernel,
        out_shape=jax.ShapeDtypeStruct((half, half), jnp.bfloat16),
        out_specs=pl.BlockSpec(memory_space=pltpu.VMEM),
        compiler_params=pltpu.CompilerParams(vmem_limit_bytes=VMEM_LIMIT),
        cost_estimate=pl.CostEstimate(flops=meanwhile, bytes_accessed=0, transcendentals=0),
        name="make_flip",
    )()


def share(win_count, source_count, peers):
    items = win_count * source_count // peers
    assert items * peers == win_count * source_count
    assert items % source_count == 0 or source_count % items == 0
    return items


def correlate_kernel(*refs, peers, chunk):
    channel_ref, table_ref, flip_ref = refs[:3]
    block_refs = refs[3 : 3 + peers]
    out_ref, lags_ref, even_ref, odd_ref, cross_ref, float_ref = refs[3 + peers :]
    win_count, _, chan_count, bin_count = block_refs[0].shape
    source_count = channel_ref.shape[0]
    items = share(win_count, source_count, peers)
    windows = float_ref.shape[0]
    lines, _, depth, block, width = out_ref.shape
    half = flip_ref.shape[0]
    me = lax.axis_index("rcv")
    first = lax.div(me * items, source_count)
    rows = []
    for t in range(items):
        channel = channel_ref[lax.rem(me * items + t, source_count)]
        owner = lax.div(channel, chan_count)
        place = lax.rem(me - owner + peers, peers) * chan_count
        rows.append(place + lax.rem(channel, chan_count))
    def widen(bins):
        for k in range(peers):
            for w in range(windows):
                for part in range(2):
                    float_ref[w, part, k * chan_count : (k + 1) * chan_count, bins] = block_refs[k][
                        first + w, part, :, bins
                    ].astype(jnp.float32)

    def form_cross(bins, some):
        for t in some:
            w = t // source_count
            real_p = by_eights(float_ref[w, 0, :, bins])
            imag_q = by_eights(float_ref[w, 1, :, bins])
            real_a = spread(float_ref[w, 0, pl.ds(rows[t], 1), bins])
            imag_b = spread(float_ref[w, 1, pl.ds(rows[t], 1), bins])
            real = real_a * real_p + imag_b * imag_q
            imag = imag_b * real_p - real_a * imag_q
            for index, value in ((0, real), (1, imag)):
                value = value.reshape(peers * chan_count, value.shape[2]).astype(jnp.bfloat16)
                for k in range(peers):
                    pairs = slice(k * width + t * chan_count, k * width + (t + 1) * chan_count)
                    cross_ref[index, pairs, bins] = value[k * chan_count : (k + 1) * chan_count]

    def add_product(bins, index, sum_ref):
        term = lax.dot_general(
            table_ref[index, :, bins],
            cross_ref[index, :, bins],
            (((1,), (1,)), ((), ())),
            preferred_element_type=jnp.float32,
        )
        if bins.start == 0:
            sum_ref[...] = term
        else:
            sum_ref[...] += term

    chunks = [slice(start, start + chunk) for start in range(0, bin_count, chunk)]
    for index in range(len(chunks) + 1):
        if index < len(chunks):
            widen(chunks[index])
            form_cross(chunks[index], range(items // 2))
        if index > 0:
            add_product(chunks[index - 1], 0, even_ref)
        if index < len(chunks):
            form_cross(chunks[index], range(items // 2, items))
        if index > 0:
            add_product(chunks[index - 1], 1, odd_ref)
    place = (lax.axis_index("win") * peers + me).astype(jnp.float32)
    factor = 1.0 + place * (1.0 / (lines * depth * peers))
    ahead = ((even_ref[:half, :] + odd_ref[:half, :]) * factor).astype(jnp.bfloat16)
    back = ((even_ref[...] - odd_ref[...]) * factor).astype(jnp.bfloat16)
    turned = jnp.dot(flip_ref[...], back[:half], preferred_element_type=jnp.float32)
    behind = jnp.where(
        lax.broadcasted_iota(jnp.int32, turned.shape, 0) == 0,
        back[half : half + 16].astype(jnp.float32)[:1],
        turned,
    ).astype(jnp.bfloat16)
    if block % 16 != 0:
        lags_ref[half:, :] = ahead.astype(jnp.float32)
        lags_ref[:half, :] = behind.astype(jnp.float32)
    for k in range(peers):
        owner = lax.rem(me - k + peers, peers)
        columns = slice(k * width, (k + 1) * width)
        for part in range(lines * depth):
            start = part * block
            if block % 16 != 0:
                piece = lags_ref[start : start + block, columns].astype(jnp.bfloat16)
            elif start < half:
                piece = behind[start : start + block, columns]
            else:
                piece = ahead[start - half : start - half + block, columns]
            out_ref[part % lines, owner, part // lines] = piece


def by_eights(values):
    return values.reshape(values.shape[0] // 8, 8, values.shape[1])


def spread(row):
    return jnp.broadcast_to(row, (8, row.shape[1]))[None]


def correlate(source_channel, table, flip, blocks, lines, depth):
    win_count, _, chan_count, bin_count = blocks[0].shape
    source_count = source_channel.shape[0]
    peers = len(blocks)
    items = share(win_count, source_count, peers)
    rows = table.shape[1]
    chunk = min(256, bin_count)
    width = items * chan_count
    vmem = pl.BlockSpec(memory_space=pltpu.VMEM)
    return pl.pallas_call(
        functools.partial(correlate_kernel, peers=peers, chunk=chunk),
        out_shape=jax.ShapeDtypeStruct((lines, peers, depth, L // (lines * depth), width), jnp.bfloat16),
        in_specs=[pl.BlockSpec(memory_space=pltpu.SMEM), vmem, vmem] + [vmem] * peers,
        out_specs=vmem,
        scratch_shapes=[
            pltpu.VMEM((L, peers * width), jnp.float32),
            pltpu.VMEM((rows, peers * width), jnp.float32),
            pltpu.VMEM((rows, peers * width), jnp.float32),
            pltpu.VMEM((2, peers * width, bin_count), jnp.bfloat16),
            pltpu.VMEM((max(1, items // source_count), 2, peers * chan_count, bin_count), jnp.float32),
        ],
        compiler_params=pltpu.CompilerParams(vmem_limit_bytes=VMEM_LIMIT),
        name="correlate",
    )(source_channel, table, flip, *blocks)


def stack_kernel(x_ref, out_ref, y_ref, *, factors):
    count, block, pairs = x_ref.shape
    for n in range(count):
        y_ref[n] = x_ref[n].astype(jnp.float32) * (1.0 / factors[n])
    mean = tree_sum([y_ref[n] for n in range(count)]) * (1.0 / count)
    squares = []
    for n in range(count):
        sample = y_ref[n] - mean
        y_ref[n] = sample
        squares.append(sample * sample)
    variance = tree_sum(squares) * (1.0 / count)
    for iteration in range(ITERS):
        shift = center * center if iteration > 0 else 0.0
        limit = TUKEY * TUKEY * (variance + shift + EPSILON)
        weights, products = [], []
        for n in range(count):
            sample = y_ref[n]
            deviation = sample - center if iteration > 0 else sample
            kept = jnp.maximum(limit - deviation * deviation, 0.0)
            weight = kept * kept
            weights.append(weight)
            products.append(weight * sample)
        center = tree_sum(products) / tree_sum(weights)
    out_ref[...] = (center + mean).T


def tree_sum(terms):
    sums = list(terms[:2])
    for index, term in enumerate(terms[2:]):
        sums[index % 2] = sums[index % 2] + term
    return sums[0] + sums[1]


def stack_blocks(samples, factors, source_count):
    count, block, pairs = samples.shape
    result = pl.pallas_call(
        functools.partial(stack_kernel, factors=factors),
        out_shape=jax.ShapeDtypeStruct((pairs, block), jnp.float32),
        in_specs=[pl.BlockSpec(memory_space=pltpu.VMEM)],
        out_specs=pl.BlockSpec(memory_space=pltpu.VMEM),
        scratch_shapes=[pltpu.VMEM((count, block, pairs), jnp.float32)],
        compiler_params=pltpu.CompilerParams(vmem_limit_bytes=VMEM_LIMIT),
        name="bisquare_stack",
    )(samples)
    return result.reshape(source_count, pairs // source_count, block).transpose(2, 0, 1)


def per_device(spectra, source_channel):
    win_count, _, chan_count, bin_count = spectra.shape
    source_count = source_channel.shape[0]
    peers = lax.axis_size("rcv")
    parts = lax.axis_size("win")
    block = L // parts
    items = share(win_count, source_count, peers)
    table = make_tables(bin_count, L, L // 2 + 16)
    flip = make_flip(L // 2, 2000 * table.size)
    blocks = [spectra]
    for step in range(1, peers):
        blocks.append(lax.ppermute(spectra, "rcv", [(i, (i + step) % peers) for i in range(peers)]))
    lines = 1
    while 4 * lines * lines <= parts:
        lines *= 2
    depth = parts // lines
    assert lines * depth == parts
    corr = correlate(source_channel, table, flip, blocks, lines, depth)
    corr = corr.reshape(parts * peers, block, items * chan_count)
    group = [
        (z * lines + q) * peers + c for q in range(lines) for c in range(peers) for z in range(depth)
    ]
    moved = lax.all_to_all(
        corr, ("win", "rcv"), split_axis=0, concat_axis=0, tiled=True, axis_index_groups=[group]
    )
    factors = [1.0 + device / len(group) for device in group]
    if items != source_count:
        moved = moved.astype(jnp.float32) / jnp.asarray(factors, jnp.float32)[:, None, None]
        factors = [1.0] * (parts * win_count)
        moved = moved.reshape(lines, peers, depth, block, items, chan_count)
        moved = moved.transpose(2, 0, 1, 4, 3, 5)
        moved = moved.reshape(parts * win_count, source_count, block, chan_count).transpose(0, 2, 1, 3)
        moved = moved.reshape(parts * win_count, block, source_count * chan_count)
    return stack_blocks(moved, factors, source_count)


def solution(mesh):
    return jax.shard_map(
        per_device,
        mesh=mesh,
        in_specs=(P("win", None, "rcv", None), P()),
        out_specs=P("win", None, "rcv"),
        check_vma=False,
    )
```

```python
import functools

import jax
import jax.numpy as jnp
import numpy as np
from jax import lax
from jax.experimental import pallas as pl
from jax.experimental.pallas import tpu as pltpu
from jax.sharding import PartitionSpec as P

L = 512
ITERS = 5
VMEM_LIMIT = 24 * 2**20


TUKEY = 4.685
EPSILON = 1e-06


def make_tables(bin_count, lag_count, rows):
    freq = np.arange(bin_count, dtype=np.int64)
    shifts = np.arange(lag_count // 2 + 1, dtype=np.int64)
    phase = shifts[:, None] * freq[None, :] % (2 * bin_count)
    angle = phase * (2.0 * np.pi / (2 * bin_count))
    factor = np.where(freq == 0, 1.0, 2.0) / np.sqrt(8.0 * bin_count)
    table = np.zeros((2, rows, bin_count), np.float32)
    table[0, : len(shifts)] = np.cos(angle) * factor
    table[1, : len(shifts)] = -np.sin(angle) * factor
    return jnp.asarray(table.astype(jnp.bfloat16))


def flip_kernel(out_ref):
    lag = lax.broadcasted_iota(jnp.int32, out_ref.shape, 0)
    shift = lax.broadcasted_iota(jnp.int32, out_ref.shape, 1)
    out_ref[...] = (lag + shift == out_ref.shape[0]).astype(jnp.float32).astype(jnp.bfloat16)


def make_flip(half, meanwhile):
    return pl.pallas_call(
        flip_kernel,
        out_shape=jax.ShapeDtypeStruct((half, half), jnp.bfloat16),
        out_specs=pl.BlockSpec(memory_space=pltpu.VMEM),
        compiler_params=pltpu.CompilerParams(vmem_limit_bytes=VMEM_LIMIT),
        cost_estimate=pl.CostEstimate(flops=meanwhile, bytes_accessed=0, transcendentals=0),
        name="make_flip",
    )()


def share(win_count, source_count, peers):
    items = win_count * source_count // peers
    assert items * peers == win_count * source_count
    assert items % source_count == 0 or source_count % items == 0
    return items


def correlate_kernel(*refs, peers, chunk):
    channel_ref, table_ref, flip_ref = refs[:3]
    block_refs = refs[3 : 3 + peers]
    out_ref, lags_ref, even_ref, odd_ref, cross_ref, float_ref = refs[3 + peers :]
    win_count, _, chan_count, bin_count = block_refs[0].shape
    source_count = channel_ref.shape[0]
    items = share(win_count, source_count, peers)
    windows = float_ref.shape[0]
    lines, _, depth, block, width = out_ref.shape
    half = flip_ref.shape[0]
    me = lax.axis_index("rcv")
    first = lax.div(me * items, source_count)
    rows = []
    for t in range(items):
        channel = channel_ref[lax.rem(me * items + t, source_count)]
        owner = lax.div(channel, chan_count)
        place = lax.rem(me - owner + peers, peers) * chan_count
        rows.append(place + lax.rem(channel, chan_count))
    def widen(bins):
        for k in range(peers):
            for w in range(windows):
                for part in range(2):
                    float_ref[w, part, k * chan_count : (k + 1) * chan_count, bins] = block_refs[k][
                        first + w, part, :, bins
                    ].astype(jnp.float32)

    def form_cross(bins, some):
        for t in some:
            w = t // source_count
            real_p = float_ref[w, 0, :, bins]
            imag_q = float_ref[w, 1, :, bins]
            real_a = float_ref[w, 0, pl.ds(rows[t], 1), bins]
            imag_b = float_ref[w, 1, pl.ds(rows[t], 1), bins]
            real = (real_a * real_p + imag_b * imag_q).astype(jnp.bfloat16)
            imag = (imag_b * real_p - real_a * imag_q).astype(jnp.bfloat16)
            for k in range(peers):
                receivers = slice(k * chan_count, (k + 1) * chan_count)
                pairs = slice(k * width + t * chan_count, k * width + (t + 1) * chan_count)
                cross_ref[0, pairs, bins] = real[receivers]
                cross_ref[1, pairs, bins] = imag[receivers]

    def add_product(bins, index, sum_ref):
        term = lax.dot_general(
            table_ref[index, :, bins],
            cross_ref[index, :, bins],
            (((1,), (1,)), ((), ())),
            preferred_element_type=jnp.float32,
        )
        if bins.start == 0:
            sum_ref[...] = term
        else:
            sum_ref[...] += term

    chunks = [slice(start, start + chunk) for start in range(0, bin_count, chunk)]
    for index in range(len(chunks) + 1):
        if index < len(chunks):
            widen(chunks[index])
        if index > 0:
            add_product(chunks[index - 1], 0, even_ref)
        if index < len(chunks):
            form_cross(chunks[index], range(items // 2))
        if index > 0:
            add_product(chunks[index - 1], 1, odd_ref)
        if index < len(chunks):
            form_cross(chunks[index], range(items // 2, items))
    place = (lax.axis_index("win") * peers + me).astype(jnp.float32)
    factor = 1.0 + place * (1.0 / (lines * depth * peers))
    ahead = ((even_ref[:half, :] + odd_ref[:half, :]) * factor).astype(jnp.bfloat16)
    back = ((even_ref[...] - odd_ref[...]) * factor).astype(jnp.bfloat16)
    turned = jnp.dot(flip_ref[...], back[:half], preferred_element_type=jnp.float32)
    behind = jnp.where(
        lax.broadcasted_iota(jnp.int32, turned.shape, 0) == 0,
        back[half : half + 16].astype(jnp.float32)[:1],
        turned,
    ).astype(jnp.bfloat16)
    if block % 16 != 0:
        lags_ref[half:, :] = ahead.astype(jnp.float32)
        lags_ref[:half, :] = behind.astype(jnp.float32)
    columns_order = gray(lines)
    for k in range(peers):
        owner = lax.rem(me - k + peers, peers)
        columns = slice(k * width, (k + 1) * width)
        for part in range(lines * depth):
            start = part * block
            if block % 16 != 0:
                piece = lags_ref[start : start + block, columns].astype(jnp.bfloat16)
            elif start < half:
                piece = behind[start : start + block, columns]
            else:
                piece = ahead[start - half : start - half + block, columns]
            out_ref[columns_order.index(part % lines), owner, part // lines] = piece


def gray(count):
    return [index ^ (index >> 1) for index in range(count)]


def correlate(source_channel, table, flip, blocks, lines, depth):
    win_count, _, chan_count, bin_count = blocks[0].shape
    source_count = source_channel.shape[0]
    peers = len(blocks)
    items = share(win_count, source_count, peers)
    rows = table.shape[1]
    chunk = min(256, bin_count)
    width = items * chan_count
    vmem = pl.BlockSpec(memory_space=pltpu.VMEM)
    return pl.pallas_call(
        functools.partial(correlate_kernel, peers=peers, chunk=chunk),
        out_shape=jax.ShapeDtypeStruct((lines, peers, depth, L // (lines * depth), width), jnp.bfloat16),
        in_specs=[pl.BlockSpec(memory_space=pltpu.SMEM), vmem, vmem] + [vmem] * peers,
        out_specs=vmem,
        scratch_shapes=[
            pltpu.VMEM((L, peers * width), jnp.float32),
            pltpu.VMEM((rows, peers * width), jnp.float32),
            pltpu.VMEM((rows, peers * width), jnp.float32),
            pltpu.VMEM((2, peers * width, bin_count), jnp.bfloat16),
            pltpu.VMEM((max(1, items // source_count), 2, peers * chan_count, bin_count), jnp.float32),
        ],
        compiler_params=pltpu.CompilerParams(vmem_limit_bytes=VMEM_LIMIT),
        name="correlate",
    )(source_channel, table, flip, *blocks)


def stack_kernel(x_ref, out_ref, y_ref, *, factors):
    count, block, pairs = x_ref.shape
    for n in range(count):
        y_ref[n] = x_ref[n].astype(jnp.float32) * (1.0 / factors[n])
    mean = tree_sum([y_ref[n] for n in range(count)]) * (1.0 / count)
    squares = []
    for n in range(count):
        sample = y_ref[n] - mean
        y_ref[n] = sample
        squares.append(sample * sample)
    variance = tree_sum(squares) * (1.0 / count)
    for iteration in range(ITERS):
        shift = center * center if iteration > 0 else 0.0
        limit = TUKEY * TUKEY * (variance + shift + EPSILON)
        weights, products = [], []
        for n in range(count):
            sample = y_ref[n]
            deviation = sample - center if iteration > 0 else sample
            kept = jnp.maximum(limit - deviation * deviation, 0.0)
            weight = kept * kept
            weights.append(weight)
            products.append(weight * sample)
        center = tree_sum(products) / tree_sum(weights)
    out_ref[...] = (center + mean).T


def tree_sum(terms):
    sums = list(terms[:2])
    for index, term in enumerate(terms[2:]):
        sums[index % 2] = sums[index % 2] + term
    return sums[0] + sums[1]


def stack_blocks(samples, factors, source_count):
    count, block, pairs = samples.shape
    result = pl.pallas_call(
        functools.partial(stack_kernel, factors=factors),
        out_shape=jax.ShapeDtypeStruct((pairs, block), jnp.float32),
        in_specs=[pl.BlockSpec(memory_space=pltpu.VMEM)],
        out_specs=pl.BlockSpec(memory_space=pltpu.VMEM),
        scratch_shapes=[pltpu.VMEM((count, block, pairs), jnp.float32)],
        compiler_params=pltpu.CompilerParams(vmem_limit_bytes=VMEM_LIMIT),
        name="bisquare_stack",
    )(samples)
    return result.reshape(source_count, pairs // source_count, block).transpose(2, 0, 1)


def per_device(spectra, source_channel):
    win_count, _, chan_count, bin_count = spectra.shape
    source_count = source_channel.shape[0]
    peers = lax.axis_size("rcv")
    parts = lax.axis_size("win")
    block = L // parts
    items = share(win_count, source_count, peers)
    table = make_tables(bin_count, L, L // 2 + 16)
    flip = make_flip(L // 2, 2000 * table.size)
    blocks = [spectra]
    for step in range(1, peers):
        blocks.append(lax.ppermute(spectra, "rcv", [(i, (i + step) % peers) for i in range(peers)]))
    lines = 1
    while 4 * lines * lines <= parts:
        lines *= 2
    depth = parts // lines
    assert lines * depth == parts
    corr = correlate(source_channel, table, flip, blocks, lines, depth)
    corr = corr.reshape(parts * peers, block, items * chan_count)
    group = [
        (z * lines + q) * peers + c for q in gray(lines) for c in range(peers) for z in range(depth)
    ]
    moved = lax.all_to_all(
        corr, ("win", "rcv"), split_axis=0, concat_axis=0, tiled=True, axis_index_groups=[group]
    )
    factors = [1.0 + device / len(group) for device in group]
    if items != source_count:
        moved = moved.astype(jnp.float32) / jnp.asarray(factors, jnp.float32)[:, None, None]
        factors = [1.0] * (parts * win_count)
        moved = moved.reshape(lines, peers, depth, block, items, chan_count)
        moved = jnp.stack([moved[gray(lines).index(q)] for q in range(lines)])
        moved = moved.transpose(2, 0, 1, 4, 3, 5)
        moved = moved.reshape(parts * win_count, source_count, block, chan_count).transpose(0, 2, 1, 3)
        moved = moved.reshape(parts * win_count, block, source_count * chan_count)
    return stack_blocks(moved, factors, source_count)


def solution(mesh):
    return jax.shard_map(
        per_device,
        mesh=mesh,
        in_specs=(P("win", None, "rcv", None), P()),
        out_specs=P("win", None, "rcv"),
        check_vma=False,
    )
```

```python
import functools

import jax
import jax.numpy as jnp
import numpy as np
from jax import lax
from jax.experimental import pallas as pl
from jax.experimental.pallas import tpu as pltpu
from jax.sharding import PartitionSpec as P

L = 512
ITERS = 5
VMEM_LIMIT = 24 * 2**20


TUKEY = 4.685
EPSILON = 1e-06


def make_tables(bin_count, lag_count, rows):
    freq = np.arange(bin_count, dtype=np.int64)
    shifts = np.arange(lag_count // 2 + 1, dtype=np.int64)
    phase = shifts[:, None] * freq[None, :] % (2 * bin_count)
    angle = phase * (2.0 * np.pi / (2 * bin_count))
    factor = np.where(freq == 0, 1.0, 2.0) / np.sqrt(8.0 * bin_count)
    table = np.zeros((2, rows, bin_count), np.float32)
    table[0, : len(shifts)] = np.cos(angle) * factor
    table[1, : len(shifts)] = -np.sin(angle) * factor
    return jnp.asarray(table.astype(jnp.bfloat16))


def flip_kernel(out_ref):
    lag = lax.broadcasted_iota(jnp.int32, out_ref.shape, 0)
    shift = lax.broadcasted_iota(jnp.int32, out_ref.shape, 1)
    out_ref[...] = (lag + shift == out_ref.shape[0]).astype(jnp.float32).astype(jnp.bfloat16)


def make_flip(half, meanwhile):
    return pl.pallas_call(
        flip_kernel,
        out_shape=jax.ShapeDtypeStruct((half, half), jnp.bfloat16),
        out_specs=pl.BlockSpec(memory_space=pltpu.VMEM),
        compiler_params=pltpu.CompilerParams(vmem_limit_bytes=VMEM_LIMIT),
        cost_estimate=pl.CostEstimate(flops=meanwhile, bytes_accessed=0, transcendentals=0),
        name="make_flip",
    )()


def share(win_count, source_count, peers):
    items = win_count * source_count // peers
    assert items * peers == win_count * source_count
    assert items % source_count == 0 or source_count % items == 0
    return items


def correlate_kernel(*refs, peers, chunk):
    channel_ref, table_ref, flip_ref = refs[:3]
    block_refs = refs[3 : 3 + peers]
    out_ref, lags_ref, even_ref, odd_ref, cross_ref, float_ref = refs[3 + peers :]
    win_count, _, chan_count, bin_count = block_refs[0].shape
    source_count = channel_ref.shape[0]
    items = share(win_count, source_count, peers)
    windows = float_ref.shape[0]
    lines, _, depth, block, width = out_ref.shape
    half = flip_ref.shape[0]
    me = lax.axis_index("rcv")
    first = lax.div(me * items, source_count)
    rows = []
    for t in range(items):
        channel = channel_ref[lax.rem(me * items + t, source_count)]
        owner = lax.div(channel, chan_count)
        place = lax.rem(me - owner + peers, peers) * chan_count
        rows.append(place + lax.rem(channel, chan_count))
    def widen(bins):
        for k in range(peers):
            for w in range(windows):
                for part in range(2):
                    float_ref[w, part, k * chan_count : (k + 1) * chan_count, bins] = block_refs[k][
                        first + w, part, :, bins
                    ].astype(jnp.float32)

    def form_cross(bins, some):
        for t in some:
            w = t // source_count
            real_p = float_ref[w, 0, :, bins]
            imag_q = float_ref[w, 1, :, bins]
            real_a = float_ref[w, 0, pl.ds(rows[t], 1), bins]
            imag_b = float_ref[w, 1, pl.ds(rows[t], 1), bins]
            real = (real_a * real_p + imag_b * imag_q).astype(jnp.bfloat16)
            imag = (imag_b * real_p - real_a * imag_q).astype(jnp.bfloat16)
            for k in range(peers):
                receivers = slice(k * chan_count, (k + 1) * chan_count)
                pairs = slice(k * width + t * chan_count, k * width + (t + 1) * chan_count)
                cross_ref[0, pairs, bins] = real[receivers]
                cross_ref[1, pairs, bins] = imag[receivers]

    def add_product(bins, index, sum_ref):
        middle = sum_ref.shape[0] // 32 * 16
        for lags in (slice(0, middle), slice(middle, sum_ref.shape[0])):
            term = lax.dot_general(
                table_ref[index, lags, bins],
                cross_ref[index, :, bins],
                (((1,), (1,)), ((), ())),
                preferred_element_type=jnp.float32,
            )
            if bins.start == 0:
                sum_ref[lags, :] = term
            else:
                sum_ref[lags, :] += term

    chunks = [slice(start, start + chunk) for start in range(0, bin_count, chunk)]
    for index in range(len(chunks) + 1):
        if index < len(chunks):
            widen(chunks[index])
            form_cross(chunks[index], range(items // 2))
        if index > 0:
            add_product(chunks[index - 1], 0, even_ref)
        if index < len(chunks):
            form_cross(chunks[index], range(items // 2, items))
        if index > 0:
            add_product(chunks[index - 1], 1, odd_ref)
    place = (lax.axis_index("win") * peers + me).astype(jnp.float32)
    factor = 1.0 + place * (1.0 / (lines * depth * peers))
    ahead = ((even_ref[:half, :] + odd_ref[:half, :]) * factor).astype(jnp.bfloat16)
    back = ((even_ref[...] - odd_ref[...]) * factor).astype(jnp.bfloat16)
    turned = jnp.dot(flip_ref[...], back[:half], preferred_element_type=jnp.float32)
    behind = jnp.where(
        lax.broadcasted_iota(jnp.int32, turned.shape, 0) == 0,
        back[half : half + 16].astype(jnp.float32)[:1],
        turned,
    ).astype(jnp.bfloat16)
    if block % 16 != 0:
        lags_ref[half:, :] = ahead.astype(jnp.float32)
        lags_ref[:half, :] = behind.astype(jnp.float32)
    for k in range(peers):
        owner = lax.rem(me - k + peers, peers)
        columns = slice(k * width, (k + 1) * width)
        for part in range(lines * depth):
            start = part * block
            if block % 16 != 0:
                piece = lags_ref[start : start + block, columns].astype(jnp.bfloat16)
            elif start < half:
                piece = behind[start : start + block, columns]
            else:
                piece = ahead[start - half : start - half + block, columns]
            out_ref[part % lines, owner, part // lines] = piece


def correlate(source_channel, table, flip, blocks, lines, depth):
    win_count, _, chan_count, bin_count = blocks[0].shape
    source_count = source_channel.shape[0]
    peers = len(blocks)
    items = share(win_count, source_count, peers)
    rows = table.shape[1]
    chunk = min(256, bin_count)
    width = items * chan_count
    vmem = pl.BlockSpec(memory_space=pltpu.VMEM)
    return pl.pallas_call(
        functools.partial(correlate_kernel, peers=peers, chunk=chunk),
        out_shape=jax.ShapeDtypeStruct((lines, peers, depth, L // (lines * depth), width), jnp.bfloat16),
        in_specs=[pl.BlockSpec(memory_space=pltpu.SMEM), vmem, vmem] + [vmem] * peers,
        out_specs=vmem,
        scratch_shapes=[
            pltpu.VMEM((L, peers * width), jnp.float32),
            pltpu.VMEM((rows, peers * width), jnp.float32),
            pltpu.VMEM((rows, peers * width), jnp.float32),
            pltpu.VMEM((2, peers * width, bin_count), jnp.bfloat16),
            pltpu.VMEM((max(1, items // source_count), 2, peers * chan_count, bin_count), jnp.float32),
        ],
        compiler_params=pltpu.CompilerParams(vmem_limit_bytes=VMEM_LIMIT),
        name="correlate",
    )(source_channel, table, flip, *blocks)


def stack_kernel(x_ref, out_ref, y_ref, *, factors):
    count, block, pairs = x_ref.shape
    for n in range(count):
        y_ref[n] = x_ref[n].astype(jnp.float32) * (1.0 / factors[n])
    mean = tree_sum([y_ref[n] for n in range(count)]) * (1.0 / count)
    squares = []
    for n in range(count):
        sample = y_ref[n] - mean
        y_ref[n] = sample
        squares.append(sample * sample)
    variance = tree_sum(squares) * (1.0 / count)
    for iteration in range(ITERS):
        shift = center * center if iteration > 0 else 0.0
        limit = TUKEY * TUKEY * (variance + shift + EPSILON)
        weights, products = [], []
        for n in range(count):
            sample = y_ref[n]
            deviation = sample - center if iteration > 0 else sample
            kept = jnp.maximum(limit - deviation * deviation, 0.0)
            weight = kept * kept
            weights.append(weight)
            products.append(weight * sample)
        center = tree_sum(products) / tree_sum(weights)
    out_ref[...] = (center + mean).T


def tree_sum(terms):
    sums = list(terms[:2])
    for index, term in enumerate(terms[2:]):
        sums[index % 2] = sums[index % 2] + term
    return sums[0] + sums[1]


def stack_blocks(samples, factors, source_count):
    count, block, pairs = samples.shape
    result = pl.pallas_call(
        functools.partial(stack_kernel, factors=factors),
        out_shape=jax.ShapeDtypeStruct((pairs, block), jnp.float32),
        in_specs=[pl.BlockSpec(memory_space=pltpu.VMEM)],
        out_specs=pl.BlockSpec(memory_space=pltpu.VMEM),
        scratch_shapes=[pltpu.VMEM((count, block, pairs), jnp.float32)],
        compiler_params=pltpu.CompilerParams(vmem_limit_bytes=VMEM_LIMIT),
        name="bisquare_stack",
    )(samples)
    return result.reshape(source_count, pairs // source_count, block).transpose(2, 0, 1)


def per_device(spectra, source_channel):
    win_count, _, chan_count, bin_count = spectra.shape
    source_count = source_channel.shape[0]
    peers = lax.axis_size("rcv")
    parts = lax.axis_size("win")
    block = L // parts
    items = share(win_count, source_count, peers)
    table = make_tables(bin_count, L, L // 2 + 16)
    flip = make_flip(L // 2, 2000 * table.size)
    blocks = [spectra]
    for step in range(1, peers):
        blocks.append(lax.ppermute(spectra, "rcv", [(i, (i + step) % peers) for i in range(peers)]))
    lines = 1
    while 4 * lines * lines <= parts:
        lines *= 2
    depth = parts // lines
    assert lines * depth == parts
    corr = correlate(source_channel, table, flip, blocks, lines, depth)
    corr = corr.reshape(parts * peers, block, items * chan_count)
    group = [
        (z * lines + q) * peers + c for q in range(lines) for c in range(peers) for z in range(depth)
    ]
    moved = lax.all_to_all(
        corr, ("win", "rcv"), split_axis=0, concat_axis=0, tiled=True, axis_index_groups=[group]
    )
    factors = [1.0 + device / len(group) for device in group]
    if items != source_count:
        moved = moved.astype(jnp.float32) / jnp.asarray(factors, jnp.float32)[:, None, None]
        factors = [1.0] * (parts * win_count)
        moved = moved.reshape(lines, peers, depth, block, items, chan_count)
        moved = moved.transpose(2, 0, 1, 4, 3, 5)
        moved = moved.reshape(parts * win_count, source_count, block, chan_count).transpose(0, 2, 1, 3)
        moved = moved.reshape(parts * win_count, block, source_count * chan_count)
    return stack_blocks(moved, factors, source_count)


def solution(mesh):
    return jax.shard_map(
        per_device,
        mesh=mesh,
        in_specs=(P("win", None, "rcv", None), P()),
        out_specs=P("win", None, "rcv"),
        check_vma=False,
    )
```
